32 devices in a mesh: ctx: 4 (over y, core), chan: 8 (over z, x).
Axes of the slice: x: 2, y: 2, z: 4, core: 2. Of those that a mesh axis runs over, the one named last changes fastest.
Arguments:
- features: float32 [3, 512, 8192], P(None, 'ctx', 'chan'), may hold values from -6 to 6
- saved_conv: float32 [512, 8192], P('ctx', 'chan'), may hold values from -6 to 6
- out_grad: float32 [512, 8192], P('ctx', 'chan'), may hold values from -6 to 6
- short_filter: float32 [3, 3, 8192], P(None, None, 'chan'), may hold values from -3 to 3
- residue: float32 [8192, 16], P('chan'), may hold values from -0.18 to 0.18
- rate: float32 [8192, 16], P('chan'), may hold values from 0.0001953125 to 0.0333333333
- bias: float32 [8192], P('chan'), may hold values from -1 to 1
- w_proj: bfloat16 [3, 8192, 8192], P(None, 'chan'), may hold values from -0.0625 to 0.0625
Outputs:
- grad_inputs: float32 [3, 512, 8192], P(None, 'ctx', 'chan')
- grad_x: float32 [512, 8192], P('ctx', 'chan')
- grad_residue: float32 [8192, 16], P('chan')
- grad_bias: float32 [8192], P('chan')
The draws below stay inside these ranges and needn't reach their ends.
All inputs are finite; a program needn't handle non-finite values.
Results may differ from the reference program's by a relative error of at most 0.0029.
Values may be sent and summed in bfloat16 or wider, within the bound.
No kernel may reach another device: no remote copies, remote signals or barrier semaphores. Data moves between devices by JAX's collectives and lax.ppermute only.
A program may use at most 256 MiB of HBM per device.

```python
import jax
import jax.numpy as jnp
from jax import lax

D = 8192
MODES = 16
TOKENS = 512


def draw_rate(key, part):
    lower = jnp.log(0.1 / TOKENS)
    upper = jnp.log(1.0 / 30.0)
    spread = jax.random.uniform(key, (D, MODES), jnp.float32)
    return jnp.exp(lower + spread * (upper - lower)).astype(jnp.float32)


def strengthened(drawn, own_key, source, target, parts, factor):
    def block_of(dim):
        return (jnp.arange(drawn.shape[dim]) // (drawn.shape[dim] // parts)).reshape((-1,) + (1,) * (drawn.ndim - 1 - dim))

    first = jax.random.permutation(own_key, parts)[block_of(target)]
    second = (block_of(target) + parts // 2) % parts
    return jnp.where((block_of(source) == first) | (block_of(source) == second), factor * drawn, drawn)


def steps_of(stream_key, dims, shards, low, high):
    loudness = 1.0
    for position, parts in shards:
        draws = jax.random.uniform(jax.random.fold_in(jax.random.fold_in(stream_key, 6), position), (parts,), jnp.float32, low / len(shards), high / len(shards))
        loudness = loudness * jnp.repeat(jnp.exp(draws), dims[position] // parts).reshape((-1,) + (1,) * (len(dims) - 1 - position))
    return loudness


def gaussian(stream_key, extent, deviation, bound, pieces=(), kind=jnp.bfloat16):
    level = steps_of(stream_key, extent, pieces, -0.22, 0.18) if pieces else 1.0
    array = jax.random.normal(stream_key, extent, jnp.float32) * deviation * level
    return jnp.minimum(jnp.maximum(array, -bound), bound).astype(kind)


def gaussian_with(key, shape, scale, reach, cuts, heavy, dtype=jnp.bfloat16):
    array = scale * jax.random.normal(key, shape, jnp.float32)
    if cuts:
        array = array * steps_of(key, shape, cuts, -0.22, 0.18)
    return jnp.clip(strengthened(array, jax.random.fold_in(key, 3), *heavy), -reach, reach).astype(dtype)


def setup_inputs(seed: int = 0) -> dict:
    key_of = jax.random.split(jax.random.key(seed), 9)
    features = gaussian(key_of[0], (3, TOKENS, D), 1.0, 6.0, ((1, 4), (2, 8)), jnp.float32)
    saved_conv = gaussian(key_of[1], (TOKENS, D), 1.0, 6.0, ((0, 4), (1, 8)), jnp.float32)
    out_grad = gaussian_with(key_of[2], (TOKENS, D), 1.0, 6.0, ((0, 4), (1, 8)), (1, 0, 8, 2.0), jnp.float32)
    short_filter = gaussian(key_of[3], (3, 3, D), 0.6, 3.0, ((2, 8),), jnp.float32)
    residue = gaussian(key_of[4], (D, MODES), 0.03, 0.18, ((0, 8),), jnp.float32)
    rate = draw_rate(jax.random.fold_in(key_of[8], 71), 0)
    bias = jnp.clip(jax.random.uniform(key_of[6], (D,), jnp.float32, -1.0, 1.0) * steps_of(key_of[6], (D,), ((0, 8),), -0.4, 0.0), -1.0, 1.0)
    w_proj = gaussian(key_of[7], (3, D, D), D ** -0.5, 0.0625, ((1, 8),))
    return {"features": features, "saved_conv": saved_conv, "out_grad": out_grad, "short_filter": short_filter, "residue": residue, "rate": rate, "bias": bias, "w_proj": w_proj}


def reference(features, saved_conv, out_grad, short_filter, residue, rate, bias, w_proj):
    gate_feat = features[0]
    key_feat = features[1]
    value_feat = features[2]
    product = key_feat * value_feat
    signal = out_grad * gate_feat
    grad_gate = out_grad * (saved_conv + bias * product)
    decay = jnp.exp(-rate)

    def backward_step(carry, inputs):
        state, accum = carry
        sig_row, prod_row = inputs
        state = sig_row[:, None] + decay * state
        accum = accum + prod_row[:, None] * state
        return (state, accum), jnp.sum(residue * state, axis=1)

    zeros = jnp.zeros(rate.shape, jnp.float32)
    (final_state, accum), corr = lax.scan(backward_step, (zeros, zeros), (signal, product), reverse=True)
    grad_prod = corr + bias * signal
    grad_stream = jnp.stack([grad_gate, grad_prod * value_feat, grad_prod * key_feat])
    padded = jnp.pad(grad_stream, ((0, 0), (0, 2), (0, 0)))
    grad_inputs = short_filter[:, 0][:, None, :] * padded[:, 0:TOKENS]
    grad_inputs = grad_inputs + short_filter[:, 1][:, None, :] * padded[:, 1:TOKENS + 1]
    grad_inputs = grad_inputs + short_filter[:, 2][:, None, :] * padded[:, 2:TOKENS + 2]
    rounded = grad_inputs.astype(jnp.bfloat16)
    grad_x = jnp.dot(rounded[0], w_proj[0].T, preferred_element_type=jnp.float32)
    grad_x = grad_x + jnp.dot(rounded[1], w_proj[1].T, preferred_element_type=jnp.float32)
    grad_x = grad_x + jnp.dot(rounded[2], w_proj[2].T, preferred_element_type=jnp.float32)
    scale = TOKENS ** -0.5
    grad_residue = accum * scale
    grad_bias = jnp.sum(signal * product, axis=0) * scale
    return grad_inputs, grad_x, grad_residue, grad_bias
```

```python
import functools

import jax
import jax.numpy as jnp
from jax import lax
from jax.experimental import pallas as pl
from jax.experimental.pallas import tpu as pltpu
from jax.sharding import PartitionSpec as P

LANES = 128
RING = 8
VMEM = 40 * 1024 * 1024
F32 = jnp.float32
BF16 = jnp.bfloat16


def whole():
    return pl.BlockSpec(memory_space=pltpu.VMEM)


def params():
    return pltpu.CompilerParams(vmem_limit_bytes=VMEM)


def cost(flops, size):
    return pl.CostEstimate(flops=flops, bytes_accessed=size, transcendentals=0)


def by_mode(ref, out, fold, fn):
    modes = ref.shape[1]
    for j in range(fold):
        block = ref[j * LANES : (j + 1) * LANES, :]
        out[pl.ds(j, modes, stride=fold), :] = fn(block.T)


def summary_kernel(feat, og, rate, out, dec, sig):
    tokens, channels = og.shape
    modes = rate.shape[1]
    fold = channels // LANES
    by_mode(rate, dec, fold, lambda r: jnp.exp(-r))
    for j in range(fold):
        lanes = slice(j * LANES, (j + 1) * LANES)
        sig[pl.ds(j, tokens, stride=fold), :] = og[:, lanes] * feat[0, :, lanes]
    decay = [dec[m * fold : (m + 1) * fold, :] for m in range(modes)]

    def step(i, states):
        row = sig[pl.ds((tokens - 1 - i) * fold, fold), :]
        return tuple(row + d * s for d, s in zip(decay, states))

    zero = tuple(jnp.zeros((fold, LANES), F32) for _ in range(modes))
    states = lax.fori_loop(0, tokens - 2, step, zero, unroll=6)
    for m in range(modes):
        out[m * fold : (m + 1) * fold, :] = states[m]
    out[modes * fold : (modes + 2) * fold, :] = sig[0 : 2 * fold, :]


def summary(features, out_grad, rate):
    tokens, channels = out_grad.shape
    modes = rate.shape[1]
    fold = channels // LANES
    return pl.pallas_call(
        summary_kernel,
        grid=(1,),
        in_specs=[
            pl.BlockSpec((1, tokens, channels), lambda i: (0, 0, 0)),
            pl.BlockSpec((tokens, channels), lambda i: (0, 0)),
            pl.BlockSpec((channels, modes), lambda i: (0, 0)),
        ],
        out_specs=pl.BlockSpec(((modes + 2) * fold, LANES), lambda i: (0, 0)),
        out_shape=jax.ShapeDtypeStruct(((modes + 2) * fold, LANES), F32),
        scratch_shapes=[
            pltpu.VMEM((modes * fold, LANES), F32),
            pltpu.VMEM((tokens * fold, LANES), F32),
        ],
        compiler_params=params(),
        cost_estimate=cost(4 * tokens * channels * modes, 12 * tokens * channels),
        name="summary",
    )(features, out_grad, rate)


def tapped(ext, taps, lanes, tokens):
    total = taps[0][:, lanes] * ext[0:tokens, lanes]
    total = total + taps[1][:, lanes] * ext[1 : tokens + 1, lanes]
    return total + taps[2][:, lanes] * ext[2 : tokens + 2, lanes]


def gate_kernel(feat, conv, og, filt, bias, halo, out, rounded, ext):
    tokens, channels = og.shape
    taps = [filt[0, j : j + 1, :] for j in range(3)]
    ext[tokens : tokens + 2, :] = halo[8:10] * (halo[6:8] + bias[...] * (halo[2:4] * halo[4:6]))
    for j in range(channels // LANES):
        lanes = slice(j * LANES, (j + 1) * LANES)
        product = feat[1, :, lanes] * feat[2, :, lanes]
        ext[0:tokens, lanes] = og[:, lanes] * (conv[:, lanes] + bias[:, lanes] * product)
        total = tapped(ext, taps, lanes, tokens)
        out[:, lanes] = total
        rounded[:, lanes] = total.astype(BF16)


def gate_stream(features, saved_conv, out_grad, short_filter, bias_row, halo):
    tokens, channels = out_grad.shape
    return pl.pallas_call(
        gate_kernel,
        in_specs=[whole()] * 6,
        out_specs=[whole()] * 2,
        out_shape=[
            jax.ShapeDtypeStruct((tokens, channels), F32),
            jax.ShapeDtypeStruct((tokens, channels), BF16),
        ],
        scratch_shapes=[pltpu.VMEM((tokens + 8, channels), F32)],
        compiler_params=params(),
        cost_estimate=cost(12 * tokens * channels, 26 * tokens * channels),
        name="gate_stream",
    )(features, saved_conv, out_grad, short_filter, bias_row, halo)


def state_kernel(later, feat, og, filt, rate, residue, bias, bias_row, halo, *refs):
    payloads = refs[:later]
    out, rounded, sums, dec, res, far, sig, prod, gp, first, second = refs[later:]
    tokens, channels = og.shape
    modes = rate.shape[1]
    fold = channels // LANES
    by_mode(rate, dec, fold, lambda r: jnp.exp(-r))
    by_mode(rate, far, fold, lambda r: jnp.exp(-(tokens - 2) * r))
    by_mode(residue, res, fold, lambda r: r)
    for j in range(fold):
        lanes = slice(j * LANES, (j + 1) * LANES)
        s = og[:, lanes] * feat[0, :, lanes]
        p = feat[1, :, lanes] * feat[2, :, lanes]
        sig[pl.ds(j, tokens, stride=fold), :] = s
        prod[pl.ds(j, tokens, stride=fold), :] = p
        sums[modes * fold + j : modes * fold + j + 1, :] = jnp.sum(s * p, axis=0, keepdims=True)

    def rows(ref, at):
        return ref[at * fold : (at + 1) * fold, :]

    direct = bias[...]
    group = 8
    for low in range(0, modes, group):
        chosen = range(low, min(low + group, modes))
        decay = [rows(dec, m) for m in chosen]
        weight = [rows(res, m) for m in chosen]
        reach = [rows(far, m) for m in chosen]
        state = [jnp.zeros((fold, LANES), F32) for _ in chosen]
        for n, payload in enumerate(reversed(payloads)):
            block_end = [rows(payload, m) + f * s for m, f, s in zip(chosen, reach, state)]
            if n < later - 1:
                s0, s1 = rows(payload, modes), rows(payload, modes + 1)
                state = [s0 + d * (s1 + d * s) for d, s in zip(decay, block_end)]
            else:
                state = block_end

        def corr(state, weight=weight):
            terms = [w * s for w, s in zip(weight, state)]
            while len(terms) > 1:
                terms = [a + b for a, b in zip(terms[::2], terms[1::2])] + terms[len(terms) // 2 * 2 :]
            return terms[0]

        def put(at, row, state, low=low):
            here = pl.ds(at * fold, fold)
            if low == 0:
                gp[here, :] = corr(state) + direct * row
            else:
                gp[here, :] = gp[here, :] + corr(state)

        for n in (1, 0):
            row = rows(payloads[0], modes + n)
            state = [row + d * s for d, s in zip(decay, state)]
            put(tokens + n, row, state)

        def step(i, carry, decay=decay, put=put):
            state, total = carry
            at = tokens - 1 - i
            row = sig[pl.ds(at * fold, fold), :]
            other = prod[pl.ds(at * fold, fold), :]
            state = [row + d * s for d, s in zip(decay, state)]
            total = [a + other * s for a, s in zip(total, state)]
            put(at, row, state)
            return state, total

        zero = [jnp.zeros((fold, LANES), F32) for _ in chosen]
        state, total = lax.fori_loop(0, tokens, step, (state, zero), unroll=4)
        for m, a in zip(chosen, total):
            sums[m * fold : (m + 1) * fold, :] = a

    taps = [[filt[p, j : j + 1, :] for j in range(3)] for p in range(3)]
    for j in range(fold):
        lanes = slice(j * LANES, (j + 1) * LANES)
        g = gp[pl.ds(j, tokens, stride=fold), :]
        rim = gp[pl.ds(tokens * fold + j, 2, stride=fold), :]
        first[0:tokens, lanes] = g * feat[2, :, lanes]
        first[tokens : tokens + 2, lanes] = rim * halo[4:6, lanes]
        second[0:tokens, lanes] = g * feat[1, :, lanes]
        second[tokens : tokens + 2, lanes] = rim * halo[2:4, lanes]
        for p, ext in ((1, first), (2, second)):
            total = tapped(ext, taps[p], lanes, tokens)
            out[p - 1, :, lanes] = total
            rounded[p - 1, :, lanes] = total.astype(BF16)


def state_streams(features, out_grad, short_filter, rate, residue, bias, bias_row, halo, payloads):
    tokens, channels = out_grad.shape
    modes = rate.shape[1]
    fold = channels // LANES
    return pl.pallas_call(
        functools.partial(state_kernel, len(payloads)),
        in_specs=[whole()] * (8 + len(payloads)),
        out_specs=[whole()] * 3,
        out_shape=[
            jax.ShapeDtypeStruct((2, tokens, channels), F32),
            jax.ShapeDtypeStruct((2, tokens, channels), BF16),
            jax.ShapeDtypeStruct(((modes + 1) * fold, LANES), F32),
        ],
        scratch_shapes=[pltpu.VMEM((modes * fold, LANES), F32)] * 3
        + [pltpu.VMEM((tokens * fold, LANES), F32)] * 2
        + [pltpu.VMEM(((tokens + 2) * fold, LANES), F32)]
        + [pltpu.VMEM((tokens + 8, channels), F32)] * 2,
        compiler_params=params(),
        cost_estimate=cost(8 * tokens * channels * modes, 40 * tokens * channels),
        name="state_streams",
    )(features, out_grad, short_filter, rate, residue, bias, bias_row, halo, *payloads)


def product_kernel(count, heights, split, source, *refs):
    xs = refs[:count]
    w, before, out = refs[count : count + 3]
    k = pl.program_id(1)

    @pl.when(k == 0)
    def _():
        out[...] = before[...]

    def add(x, rows):
        out[rows, :] += lax.dot_general(
            x, w[0], (((1,), (1,)), ((), ())), preferred_element_type=F32
        )

    if split:
        half = xs[0].shape[1]
        for n, x in enumerate(xs):
            for h in range(heights):

                @pl.when(k == h)
                def _(n=n, x=x, h=h):
                    add(x[h], slice(n * half, (n + 1) * half))

    else:
        for n, x in enumerate(xs):
            for h in range(heights):

                @pl.when(k == n * heights + h)
                def _(x=x, h=h):
                    add(x[h], slice(None))


def add_product(total, chunks, offsets, sources, w_proj, stream, split=False):
    tokens, features = total.shape
    heights, _, channels = chunks[0].shape
    steps = heights * (1 if split else len(chunks))
    wide = min(512, features)

    def w_index(i, k, source):
        lo = source[offsets[0]]
        for n in range(1, len(offsets)):
            lo = jnp.where(k >= n * heights, source[offsets[n]], lo)
        return stream, i, lax.rem(k, heights) * RING + lo

    return pl.pallas_call(
        functools.partial(product_kernel, len(chunks), heights, split),
        grid_spec=pltpu.PrefetchScalarGridSpec(
            num_scalar_prefetch=1,
            grid=(features // wide, steps),
            in_specs=[pl.BlockSpec(c.shape, lambda i, k, s: (0, 0, 0)) for c in chunks]
            + [
                pl.BlockSpec((1, wide, channels), w_index),
                pl.BlockSpec((tokens, wide), lambda i, k, s: (0, i)),
            ],
            out_specs=pl.BlockSpec((tokens, wide), lambda i, k, s: (0, i)),
        ),
        out_shape=jax.ShapeDtypeStruct(total.shape, F32),
        input_output_aliases={len(chunks) + 2: 0},
        compiler_params=params(),
        cost_estimate=cost(
            2 * tokens * features * channels * steps, 2 * features * channels * steps + 8 * tokens * features
        ),
        name="add_product",
    )(sources, *chunks, w_proj, total)


def ring_order(size):
    return list(range(0, size, 2)) + list(range(size - 1 - size % 2, 0, -2))


def gathered_product(total, block, sources, w_proj, stream, ring, heights):
    order = ring_order(ring)
    pairs = {
        by: [
            (h * ring + order[i], h * ring + order[(i + by) % ring])
            for h in range(heights)
            for i in range(ring)
        ]
        for by in (1, -1)
    }

    def send(x, by):
        return lax.ppermute(x, "chan", pairs[by])

    if heights > 1:
        groups = [[h * ring + i for h in range(heights)] for i in range(ring)]
        block = lax.all_gather(block, "chan", axis_index_groups=groups)
    else:
        block = block[None]
    up = down = block
    for hop in range(1, ring // 2):
        up, down = send(up, 1), send(down, -1)
        chunks = [up, down]
        offsets = [ring - hop, hop]
        if hop == 1:
            chunks, offsets = [block] + chunks, [0] + offsets
        total = add_product(total, chunks, offsets, sources, w_proj, stream)
    half = block.shape[1] // 2
    last = [send(up[:, :half], 1), send(down[:, half:], -1)]
    return add_product(total, last, [ring // 2], sources, w_proj, stream, split=True)


def body(features, saved_conv, out_grad, short_filter, residue, rate, bias, w_proj):
    tokens, channels = out_grad.shape
    modes = rate.shape[1]
    fold = channels // LANES
    blocks = lax.axis_size("ctx")
    groups = lax.axis_size("chan")
    ring = min(groups, RING)
    bias_row = bias[None]

    order = ring_order(ring)
    place = [order.index(i) for i in range(ring)]
    table = jnp.array([[order[(place[i] + d) % ring] for d in range(ring)] for i in range(ring)], jnp.int32)
    sources = lax.dynamic_index_in_dim(table, lax.rem(lax.axis_index("chan"), ring), 0, False)

    def from_later(array, by):
        return lax.ppermute(array, "ctx", [(i, i - by) for i in range(by, blocks)])

    rim = jnp.concatenate([features[:, 0:2].reshape(6, channels), saved_conv[0:2], out_grad[0:2]])
    halo = from_later(rim, 1)
    own = summary(features, out_grad, rate)
    payloads = [from_later(own, by) for by in range(1, blocks)]
    gate_grad, gate_round = gate_stream(features, saved_conv, out_grad, short_filter, bias_row, halo)
    grads, rounds, sums = state_streams(
        features, out_grad, short_filter, rate, residue, bias.reshape(fold, LANES), bias_row, halo, payloads
    )
    total = jnp.zeros((tokens, w_proj.shape[1]), F32)
    for stream, block in enumerate((gate_round, rounds[0], rounds[1])):
        total = gathered_product(total, block, sources, w_proj, stream, ring, groups // ring)

    by = 1
    while by < blocks:
        sums = sums + lax.ppermute(sums, "ctx", [(i, i ^ by) for i in range(blocks)])
        by *= 2
    sums = sums * (tokens * blocks) ** (-0.5)
    grad_residue = sums[: modes * fold].reshape(modes, channels).T
    grad_bias = sums[modes * fold :].reshape(channels)
    grad_inputs = jnp.concatenate([gate_grad[None], grads])
    return (grad_inputs, total, grad_residue, grad_bias)


def solution(mesh):
    return jax.shard_map(
        body,
        mesh=mesh,
        in_specs=(
            P(None, "ctx", "chan"),
            P("ctx", "chan"),
            P("ctx", "chan"),
            P(None, None, "chan"),
            P("chan", None),
            P("chan", None),
            P("chan"),
            P(None, "chan", None),
        ),
        out_specs=(P(None, "ctx", "chan"), P("ctx", "chan"), P("chan", None), P("chan")),
        check_vma=False,
    )
```

```python
import functools

import jax
import jax.numpy as jnp
from jax import lax
from jax.experimental import pallas as pl
from jax.experimental.pallas import tpu as pltpu
from jax.sharding import PartitionSpec as P

LANES = 128
RING = 8
VMEM = 40 * 1024 * 1024
F32 = jnp.float32
BF16 = jnp.bfloat16


def whole():
    return pl.BlockSpec(memory_space=pltpu.VMEM)


def params():
    return pltpu.CompilerParams(vmem_limit_bytes=VMEM)


def cost(flops, size):
    return pl.CostEstimate(flops=flops, bytes_accessed=size, transcendentals=0)


def by_mode(values, out, fold):
    for j in range(fold):
        out[pl.ds(j, values.shape[0], stride=fold), :] = values[:, j * LANES : (j + 1) * LANES]


def summary_kernel(feat, og, rate, out, dec, sig):
    tokens, channels = og.shape
    modes = rate.shape[0]
    fold = channels // LANES
    by_mode(jnp.exp(-rate[...]), dec, fold)
    for j in range(fold):
        lanes = slice(j * LANES, (j + 1) * LANES)
        sig[pl.ds(j, tokens, stride=fold), :] = og[:, lanes] * feat[0, :, lanes]
    decay = [dec[m * fold : (m + 1) * fold, :] for m in range(modes)]

    def step(i, states):
        row = sig[pl.ds((tokens - 1 - i) * fold, fold), :]
        return tuple(row + d * s for d, s in zip(decay, states))

    zero = tuple(jnp.zeros((fold, LANES), F32) for _ in range(modes))
    states = lax.fori_loop(0, tokens - 2, step, zero, unroll=6)
    for m in range(modes):
        out[m * fold : (m + 1) * fold, :] = states[m]
    out[modes * fold : (modes + 2) * fold, :] = sig[0 : 2 * fold, :]


def summary(features, out_grad, rate):
    tokens, channels = out_grad.shape
    modes = rate.shape[0]
    fold = channels // LANES
    return pl.pallas_call(
        summary_kernel,
        in_specs=[whole()] * 3,
        out_specs=whole(),
        out_shape=jax.ShapeDtypeStruct(((modes + 2) * fold, LANES), F32),
        scratch_shapes=[
            pltpu.VMEM((modes * fold, LANES), F32),
            pltpu.VMEM((tokens * fold, LANES), F32),
        ],
        compiler_params=params(),
        cost_estimate=cost(4 * tokens * channels * modes, 12 * tokens * channels),
        name="summary",
    )(features, out_grad, rate)


def tapped(ext, taps, lanes, tokens):
    total = taps[0][:, lanes] * ext[0:tokens, lanes]
    total = total + taps[1][:, lanes] * ext[1 : tokens + 1, lanes]
    return total + taps[2][:, lanes] * ext[2 : tokens + 2, lanes]


def gate_gradient(feat, conv, og, bias, halo, ext):
    tokens, channels = og.shape
    ext[tokens : tokens + 2, :] = halo[8:10] * (halo[6:8] + bias[...] * (halo[2:4] * halo[4:6]))
    for j in range(channels // LANES):
        lanes = slice(j * LANES, (j + 1) * LANES)
        product = feat[1, :, lanes] * feat[2, :, lanes]
        ext[0:tokens, lanes] = og[:, lanes] * (conv[:, lanes] + bias[:, lanes] * product)


def gate_kernel(feat, conv, og, filt, bias, halo, rounded, ext):
    tokens, channels = og.shape
    taps = [filt[0, j : j + 1, :] for j in range(3)]
    gate_gradient(feat, conv, og, bias, halo, ext)
    for j in range(channels // LANES):
        lanes = slice(j * LANES, (j + 1) * LANES)
        rounded[0, :, lanes] = tapped(ext, taps, lanes, tokens).astype(BF16)


def gate_stream(features, saved_conv, out_grad, short_filter, bias_row, halo):
    tokens, channels = out_grad.shape
    return pl.pallas_call(
        gate_kernel,
        in_specs=[whole()] * 6,
        out_specs=whole(),
        out_shape=jax.ShapeDtypeStruct((1, tokens, channels), BF16),
        scratch_shapes=[pltpu.VMEM((tokens + 8, channels), F32)],
        compiler_params=params(),
        cost_estimate=cost(12 * tokens * channels, 26 * tokens * channels),
        name="gate_stream",
    )(features, saved_conv, out_grad, short_filter, bias_row, halo)


def state_kernel(later, feat, conv, og, filt, rate, residue, bias, bias_row, halo, *refs):
    payloads = refs[:later]
    out, rounded, sums, dec, res, far, acc, sig, prod, gp, *exts = refs[later:]
    tokens, channels = og.shape
    modes = rate.shape[0]
    fold = channels // LANES
    by_mode(jnp.exp(-rate[...]), dec, fold)
    by_mode(jnp.exp(-(tokens - 2) * rate[...]), far, fold)
    by_mode(residue[...], res, fold)
    for j in range(fold):
        lanes = slice(j * LANES, (j + 1) * LANES)
        s = og[:, lanes] * feat[0, :, lanes]
        p = feat[1, :, lanes] * feat[2, :, lanes]
        sig[pl.ds(j, tokens, stride=fold), :] = s
        prod[pl.ds(j, tokens, stride=fold), :] = p
        sums[modes : modes + 1, lanes] = jnp.sum(s * p, axis=0, keepdims=True)

    def rows(ref, at):
        return ref[at * fold : (at + 1) * fold, :]

    direct = bias[...]
    group = 8
    for low in range(0, modes, group):
        chosen = range(low, min(low + group, modes))
        decay = [rows(dec, m) for m in chosen]
        weight = [rows(res, m) for m in chosen]
        reach = [rows(far, m) for m in chosen]
        state = [jnp.zeros((fold, LANES), F32) for _ in chosen]
        for n, payload in enumerate(reversed(payloads)):
            block_end = [rows(payload, m) + f * s for m, f, s in zip(chosen, reach, state)]
            if n < later - 1:
                s0, s1 = rows(payload, modes), rows(payload, modes + 1)
                state = [s0 + d * (s1 + d * s) for d, s in zip(decay, block_end)]
            else:
                state = block_end

        def corr(state, weight=weight):
            terms = [w * s for w, s in zip(weight, state)]
            while len(terms) > 1:
                terms = [a + b for a, b in zip(terms[::2], terms[1::2])] + terms[len(terms) // 2 * 2 :]
            return terms[0]

        def put(at, row, state, low=low):
            here = pl.ds(at * fold, fold)
            if low == 0:
                gp[here, :] = corr(state) + direct * row
            else:
                gp[here, :] = gp[here, :] + corr(state)

        for n in (1, 0):
            row = rows(payloads[0], modes + n)
            state = [row + d * s for d, s in zip(decay, state)]
            put(tokens + n, row, state)

        def step(i, carry, decay=decay, put=put):
            state, total = carry
            at = tokens - 1 - i
            row = sig[pl.ds(at * fold, fold), :]
            other = prod[pl.ds(at * fold, fold), :]
            state = [row + d * s for d, s in zip(decay, state)]
            total = [a + other * s for a, s in zip(total, state)]
            put(at, row, state)
            return state, total

        zero = [jnp.zeros((fold, LANES), F32) for _ in chosen]
        state, total = lax.fori_loop(0, tokens, step, (state, zero), unroll=4)
        for m, a in zip(chosen, total):
            acc[m * fold : (m + 1) * fold, :] = a

    taps = [[filt[p, j : j + 1, :] for j in range(3)] for p in range(3)]
    gate_gradient(feat, conv, og, bias_row, halo, exts[0])
    for j in range(fold):
        lanes = slice(j * LANES, (j + 1) * LANES)
        g = gp[pl.ds(j, tokens, stride=fold), :]
        rim = gp[pl.ds(tokens * fold + j, 2, stride=fold), :]
        exts[1][0:tokens, lanes] = g * feat[2, :, lanes]
        exts[1][tokens : tokens + 2, lanes] = rim * halo[4:6, lanes]
        exts[2][0:tokens, lanes] = g * feat[1, :, lanes]
        exts[2][tokens : tokens + 2, lanes] = rim * halo[2:4, lanes]
        for p, ext in enumerate(exts):
            total = tapped(ext, taps[p], lanes, tokens)
            out[p, :, lanes] = total
            if p:
                rounded[p - 1, :, lanes] = total.astype(BF16)
        sums[0:modes, lanes] = acc[pl.ds(j, modes, stride=fold), :]


def state_streams(features, saved_conv, out_grad, short_filter, rate, residue, bias, halo, payloads):
    tokens, channels = out_grad.shape
    modes = rate.shape[0]
    fold = channels // LANES
    return pl.pallas_call(
        functools.partial(state_kernel, len(payloads)),
        in_specs=[whole()] * (9 + len(payloads)),
        out_specs=[whole()] * 3,
        out_shape=[
            jax.ShapeDtypeStruct((3, tokens, channels), F32),
            jax.ShapeDtypeStruct((2, tokens, channels), BF16),
            jax.ShapeDtypeStruct((modes + 1, channels), F32),
        ],
        scratch_shapes=[pltpu.VMEM((modes * fold, LANES), F32)] * 4
        + [pltpu.VMEM((tokens * fold, LANES), F32)] * 2
        + [pltpu.VMEM(((tokens + 2) * fold, LANES), F32)]
        + [pltpu.VMEM((tokens + 8, channels), F32)] * 3,
        compiler_params=params(),
        cost_estimate=cost(8 * tokens * channels * modes, 40 * tokens * channels),
        name="state_streams",
    )(
        features, saved_conv, out_grad, short_filter, rate, residue,
        bias.reshape(fold, LANES), bias[None], halo, *payloads,
    )


def product_kernel(plan, first, last, source, *refs):
    *xs, w = refs[: len(refs) - 1 - (not first)]
    out = refs[-1]
    before = None if first else refs[-2]
    total = None
    k = pl.program_id(1)
    for at, parts in enumerate(plan):

        @pl.when(k == at)
        def _(at=at, parts=parts):
            x = [xs[n][h, p] for n, h, p in parts]
            x = x[0] if len(x) == 1 else jnp.concatenate(x, axis=0)
            y = lax.dot_general(w[0], x, (((1,), (1,)), ((), ())), preferred_element_type=F32)
            if at == 0:
                if not first:
                    y = y + before[...]
            else:
                y = y + (out[...].T if last else out[...])
            out[...] = y.T if last else y


def add_product(total, pieces, sources, w_proj, last=False):
    features = w_proj.shape[1]
    arrays, plan, where = [], [], []
    for array, stream, offset in pieces:
        halves = array if isinstance(array, tuple) else (array,)
        heights, streams, _, channels = halves[0].shape
        for h in range(heights):
            for p in range(streams):
                plan.append([(len(arrays) + n, h, p) for n in range(len(halves))])
                where.append((stream + p, h, offset))
        arrays += halves
    tokens = sum(arrays[n].shape[2] for n, _, _ in plan[0])
    wide = min(512, features)

    def w_index(i, k, source):
        stream, height, offset = (jnp.int32(v) for v in where[0])
        for at, (s, h, o) in enumerate(where):
            stream = jnp.where(k == at, s, stream)
            height = jnp.where(k == at, h, height)
            offset = jnp.where(k == at, o, offset)
        return stream, i, height * RING + source[offset]

    def kept(array):
        return pl.BlockSpec(array.shape, lambda i, k, s: (0,) * array.ndim)

    tile = pl.BlockSpec((wide, tokens), lambda i, k, s: (i, 0))
    first = total is None
    return pl.pallas_call(
        functools.partial(product_kernel, plan, first, last),
        grid_spec=pltpu.PrefetchScalarGridSpec(
            num_scalar_prefetch=1,
            grid=(features // wide, len(plan)),
            in_specs=[kept(a) for a in arrays]
            + [pl.BlockSpec((1, wide, channels), w_index)]
            + [tile] * (not first),
            out_specs=pl.BlockSpec((tokens, wide), lambda i, k, s: (0, i)) if last else tile,
        ),
        out_shape=jax.ShapeDtypeStruct((tokens, features) if last else (features, tokens), F32),
        compiler_params=params(),
        cost_estimate=cost(
            2 * tokens * features * channels * len(plan),
            2 * features * channels * len(plan) + 8 * tokens * features,
        ),
        name="add_product",
    )(sources, *arrays, w_proj, *([] if first else [total]))


def ring_order(size):
    return list(range(0, size, 2)) + list(range(size - 1 - size % 2, 0, -2))


def after(array, *others):
    return lax.optimization_barrier((array, *others))[0]


def body(features, saved_conv, out_grad, short_filter, residue, rate, bias, w_proj):
    tokens, channels = out_grad.shape
    modes = rate.shape[1]
    blocks = lax.axis_size("ctx")
    groups = lax.axis_size("chan")
    ring = min(groups, RING)
    heights = groups // ring

    order = ring_order(ring)
    place = [order.index(i) for i in range(ring)]
    table = jnp.array([[order[(place[i] + d) % ring] for d in range(ring)] for i in range(ring)], jnp.int32)
    sources = lax.dynamic_index_in_dim(table, lax.rem(lax.axis_index("chan"), ring), 0, False)
    pairs = {
        by: [
            (h * ring + order[i], h * ring + order[(i + by) % ring])
            for h in range(heights)
            for i in range(ring)
        ]
        for by in (1, -1)
    }

    def up(x):
        return lax.ppermute(x, "chan", pairs[1])

    def down(x):
        return lax.ppermute(x, "chan", pairs[-1])

    def stacked(block):
        if heights == 1:
            return block[None]
        groups = [[h * ring + i for h in range(heights)] for i in range(ring)]
        return lax.all_gather(block, "chan", axis_index_groups=groups)

    def from_later(array, by):
        return lax.ppermute(array, "ctx", [(i, i - by) for i in range(by, blocks)])

    rim = jnp.concatenate([features[:, 0:2].reshape(6, channels), saved_conv[0:2], out_grad[0:2]])
    halo = from_later(rim, 1)
    own = summary(features, out_grad, rate.T)
    gate = gate_stream(features, saved_conv, out_grad, short_filter, bias[None], halo)
    own = after(own, gate)
    payloads = [from_later(own, by) for by in range(1, blocks)]
    a0 = stacked(gate)
    a1, z1 = up(a0), down(a0)

    grads, rounds, sums = state_streams(
        features, saved_conv, out_grad, short_filter, rate.T, residue.T, bias, halo, payloads
    )
    b0 = stacked(rounds)
    half = tokens // 2
    back = ring // 2

    a2, z2 = up(a1), down(z1)
    b1, y1 = up(b0), down(b0)
    a3, z3 = up(after(a2, b0)), down(after(z2, b0))
    total = add_product(
        None, [(a0, 0, 0), (a1, 0, ring - 1), (z1, 0, 1), (a2, 0, ring - 2), (z2, 0, 2)], sources, w_proj
    )
    by = 1
    sums = after(sums, total)
    while by < blocks:
        sums = sums + lax.ppermute(sums, "ctx", [(i, i ^ by) for i in range(blocks)])
        by *= 2
    sums = sums * (tokens * blocks) ** (-0.5)

    a3, z3, total = lax.optimization_barrier((a3, z3, total))
    tail = (up(a3[:, :, :half]), down(z3[:, :, half:]))
    total = add_product(total, [(a3, 0, ring - 3), (z3, 0, 3)], sources, w_proj)
    b1, y1, total = lax.optimization_barrier((b1, y1, total))
    b2, y2 = up(b1), down(y1)
    total = add_product(total, [(b0, 1, 0), (b1, 1, ring - 1), (y1, 1, 1)], sources, w_proj)
    tail, total = lax.optimization_barrier((tail, total))
    total = add_product(total, [(tail, 0, back)], sources, w_proj)
    b2, y2, total = lax.optimization_barrier((b2, y2, total))
    b3, y3 = up(b2), down(y2)
    total = add_product(total, [(b2, 1, ring - 2), (y2, 1, 2)], sources, w_proj)
    b3, y3, total = lax.optimization_barrier((b3, y3, total))
    b4, y4 = up(b3[:, :1]), down(y3[:, 1:])
    total = add_product(total, [(b3, 1, ring - 3), (y3, 1, 3)], sources, w_proj)
    grad_x = add_product(total, [(b4, 1, back), (y4, 2, back)], sources, w_proj, last=True)
    return (grads, grad_x, sums[:modes].T, sums[modes])


def solution(mesh):
    return jax.shard_map(
        body,
        mesh=mesh,
        in_specs=(
            P(None, "ctx", "chan"),
            P("ctx", "chan"),
            P("ctx", "chan"),
            P(None, None, "chan"),
            P("chan", None),
            P("chan", None),
            P("chan"),
            P(None, "chan", None),
        ),
        out_specs=(P(None, "ctx", "chan"), P("ctx", "chan"), P("chan", None), P("chan")),
        check_vma=False,
    )
```

```python
import functools

import jax
import jax.numpy as jnp
from jax import lax
from jax.experimental import pallas as pl
from jax.experimental.pallas import tpu as pltpu
from jax.sharding import PartitionSpec as P

LANES = 128
RING = 8
VMEM = 40 * 1024 * 1024
F32 = jnp.float32
BF16 = jnp.bfloat16


def whole():
    return pl.BlockSpec(memory_space=pltpu.VMEM)


def in_hbm():
    return pl.BlockSpec(memory_space=pltpu.HBM)


def params():
    return pltpu.CompilerParams(vmem_limit_bytes=VMEM)


def cost(flops, size):
    return pl.CostEstimate(flops=flops, bytes_accessed=size, transcendentals=0)


def by_row(values, out, fold, base=0):
    for j in range(fold):
        out[pl.ds(base * fold + j, values.shape[0], stride=fold), :] = values[:, j * LANES : (j + 1) * LANES]


def front_kernel(features, saved_conv, out_grad, short_filter, residue, rate, bias, *refs):
    feat, conv, og, filt, bias_in, dec, far, res, sig, own, res_in, rate_in, sems = refs
    tokens, channels = og.shape
    modes = rate_in.shape[0]
    fold = channels // LANES
    moves = [
        pltpu.make_async_copy(source, target, sems.at[n])
        for n, (source, target) in enumerate((
            (rate, rate_in),
            (out_grad, og),
            (features, feat),
            (saved_conv, conv),
            (short_filter, filt),
            (residue, res_in),
            (bias, bias_in),
        ))
    ]
    for move in moves:
        move.start()
    moves[0].wait()
    by_row(jnp.exp(-rate_in[...]), dec, fold)
    by_row(jnp.exp(-(tokens - 2) * rate_in[...]), far, fold)
    moves[1].wait()
    moves[2].wait()
    for j in range(fold):
        lanes = slice(j * LANES, (j + 1) * LANES)
        sig[pl.ds(j, tokens, stride=fold), :] = og[:, lanes] * feat[0, :, lanes]
    decay = [dec[m * fold : (m + 1) * fold, :] for m in range(modes)]

    def step(i, states):
        row = sig[pl.ds((tokens - 1 - i) * fold, fold), :]
        return tuple(row + d * s for d, s in zip(decay, states))

    zero = tuple(jnp.zeros((fold, LANES), F32) for _ in range(modes))
    states = lax.fori_loop(0, tokens - 2, step, zero, unroll=6)
    for m in range(modes):
        own[m * fold : (m + 1) * fold, :] = states[m]
    own[modes * fold : (modes + 2) * fold, :] = sig[0 : 2 * fold, :]
    for n in range(3):
        by_row(feat[n, 0:2, :], own, fold, modes + 2 + 2 * n)
    by_row(og[0:2, :], own, fold, modes + 10)
    for n in range(3, 7):
        moves[n].wait()
    by_row(conv[0:2, :], own, fold, modes + 8)
    by_row(res_in[...], res, fold)


def front(features, saved_conv, out_grad, short_filter, residue, rate, bias):
    tokens, channels = out_grad.shape
    modes = rate.shape[0]
    fold = channels // LANES
    inputs = (features, saved_conv, out_grad, short_filter, residue, rate, bias)
    by_mode = pltpu.VMEM((modes * fold, LANES), F32)
    return pl.pallas_call(
        front_kernel,
        in_specs=[in_hbm()] * 7,
        out_specs=[whole()] * 10,
        out_shape=[pltpu.VMEM(a.shape, F32) for a in (*inputs[:4], bias)]
        + [by_mode] * 3
        + [pltpu.VMEM((tokens * fold, LANES), F32), pltpu.VMEM(((modes + 12) * fold, LANES), F32)],
        scratch_shapes=[pltpu.VMEM(rate.shape, F32)] * 2 + [pltpu.SemaphoreType.DMA((7,))],
        compiler_params=params(),
        cost_estimate=cost(4 * tokens * channels * modes, 20 * tokens * channels),
        name="front",
    )(*(pltpu.with_memory_space_constraint(a, pltpu.HBM) for a in inputs))


def tapped(ext, taps, lanes, tokens):
    total = taps[0][:, lanes] * ext[0:tokens, lanes]
    total = total + taps[1][:, lanes] * ext[1 : tokens + 1, lanes]
    return total + taps[2][:, lanes] * ext[2 : tokens + 2, lanes]


def rim_rows(later, which, j, fold):
    modes = later.shape[0] // fold - 12
    return later[pl.ds((modes + 2 + 2 * which) * fold + j, 2, stride=fold), :]


def gate_gradient(feat, conv, og, bias, later, ext):
    tokens, channels = og.shape
    fold = channels // LANES
    for j in range(fold):
        lanes = slice(j * LANES, (j + 1) * LANES)
        product = feat[1, :, lanes] * feat[2, :, lanes]
        ext[0:tokens, lanes] = og[:, lanes] * (conv[:, lanes] + bias[:, lanes] * product)
        key, value, held, cotangent = (rim_rows(later, n, j, fold) for n in (1, 2, 3, 4))
        ext[tokens : tokens + 2, lanes] = cotangent * (held + bias[:, lanes] * (key * value))


def gate_kernel(feat, conv, og, filt, bias, later, rounded, ext):
    tokens, channels = og.shape
    taps = [filt[0, j : j + 1, :] for j in range(3)]
    gate_gradient(feat, conv, og, bias, later, ext)
    for j in range(channels // LANES):
        lanes = slice(j * LANES, (j + 1) * LANES)
        rounded[0, :, lanes] = tapped(ext, taps, lanes, tokens).astype(BF16)


def gate_stream(feat, conv, og, filt, bias, later):
    tokens, channels = og.shape
    return pl.pallas_call(
        gate_kernel,
        in_specs=[whole()] * 6,
        out_specs=whole(),
        out_shape=jax.ShapeDtypeStruct((1, tokens, channels), BF16),
        scratch_shapes=[pltpu.VMEM((tokens + 8, channels), F32)],
        compiler_params=params(),
        cost_estimate=cost(12 * tokens * channels, 26 * tokens * channels),
        name="gate_stream",
    )(feat, conv, og, filt, bias, later)


def product_gradients(feat, gp, later, exts):
    tokens, channels = feat.shape[1:]
    fold = channels // LANES
    for j in range(fold):
        lanes = slice(j * LANES, (j + 1) * LANES)
        g = gp[pl.ds(j, tokens, stride=fold), :]
        rim = gp[pl.ds(tokens * fold + j, 2, stride=fold), :]
        for ext, n in zip(exts, (2, 1)):
            ext[0:tokens, lanes] = g * feat[n, :, lanes]
            ext[tokens : tokens + 2, lanes] = rim * rim_rows(later, n, j, fold)


def gradients_kernel(feat, conv, og, filt, bias, later, gp, out, first, second, third, ready, sems):
    tokens, channels = og.shape
    gate_gradient(feat, conv, og, bias, later, first)
    product_gradients(feat, gp, later, (second, third))
    moves = []
    for p, ext in enumerate((first, second, third)):
        taps = [filt[p, j : j + 1, :] for j in range(3)]
        for j in range(channels // LANES):
            lanes = slice(j * LANES, (j + 1) * LANES)
            ready[p, :, lanes] = tapped(ext, taps, lanes, tokens)
        moves.append(pltpu.make_async_copy(ready.at[p], out.at[p], sems.at[p]))
        moves[-1].start()
    for move in moves:
        move.wait()


def gradients(feat, conv, og, filt, bias, later, gp):
    tokens, channels = og.shape
    return pl.pallas_call(
        gradients_kernel,
        in_specs=[whole()] * 7,
        out_specs=in_hbm(),
        out_shape=jax.ShapeDtypeStruct((3, tokens, channels), F32),
        scratch_shapes=[pltpu.VMEM((tokens + 8, channels), F32)] * 3
        + [pltpu.VMEM((3, tokens, channels), F32), pltpu.SemaphoreType.DMA((3,))],
        compiler_params=params(),
        cost_estimate=cost(30 * tokens * channels, 40 * tokens * channels),
        name="gradients",
    )(feat, conv, og, filt, bias, later, gp)


def state_kernel(later, feat, og, filt, dec, far, res, bias, sig, *refs):
    payloads = refs[:later]
    rounded, sums, gp, acc, prod, *exts = refs[later:]
    tokens, channels = og.shape
    fold = channels // LANES
    modes = dec.shape[0] // fold
    for j in range(fold):
        lanes = slice(j * LANES, (j + 1) * LANES)
        p = feat[1, :, lanes] * feat[2, :, lanes]
        prod[pl.ds(j, tokens, stride=fold), :] = p
        s = og[:, lanes] * feat[0, :, lanes]
        sums[modes : modes + 1, lanes] = jnp.sum(s * p, axis=0, keepdims=True)

    def rows(ref, at):
        return ref[at * fold : (at + 1) * fold, :]

    direct = bias[...]
    group = 8
    for low in range(0, modes, group):
        chosen = range(low, min(low + group, modes))
        decay = [rows(dec, m) for m in chosen]
        weight = [rows(res, m) for m in chosen]
        reach = [rows(far, m) for m in chosen]
        state = [jnp.zeros((fold, LANES), F32) for _ in chosen]
        for n, payload in enumerate(reversed(payloads)):
            block_end = [rows(payload, m) + f * s for m, f, s in zip(chosen, reach, state)]
            if n < later - 1:
                s0, s1 = rows(payload, modes), rows(payload, modes + 1)
                state = [s0 + d * (s1 + d * s) for d, s in zip(decay, block_end)]
            else:
                state = block_end

        def corr(state, weight=weight):
            terms = [w * s for w, s in zip(weight, state)]
            while len(terms) > 1:
                terms = [a + b for a, b in zip(terms[::2], terms[1::2])] + terms[len(terms) // 2 * 2 :]
            return terms[0]

        def put(at, row, state, low=low, corr=corr):
            here = pl.ds(at * fold, fold)
            if low == 0:
                gp[here, :] = corr(state) + direct * row
            else:
                gp[here, :] = gp[here, :] + corr(state)

        for n in (1, 0):
            row = rows(payloads[0], modes + n)
            state = [row + d * s for d, s in zip(decay, state)]
            put(tokens + n, row, state)

        def step(i, carry, decay=decay, put=put):
            state, total = carry
            at = tokens - 1 - i
            row = sig[pl.ds(at * fold, fold), :]
            other = prod[pl.ds(at * fold, fold), :]
            state = [row + d * s for d, s in zip(decay, state)]
            total = [a + other * s for a, s in zip(total, state)]
            put(at, row, state)
            return state, total

        zero = [jnp.zeros((fold, LANES), F32) for _ in chosen]
        state, total = lax.fori_loop(0, tokens, step, (state, zero), unroll=4)
        for m, a in zip(chosen, total):
            acc[m * fold : (m + 1) * fold, :] = a

    product_gradients(feat, gp, payloads[0], exts)
    for p, ext in enumerate(exts):
        taps = [filt[p + 1, j : j + 1, :] for j in range(3)]
        for j in range(fold):
            lanes = slice(j * LANES, (j + 1) * LANES)
            rounded[p, :, lanes] = tapped(ext, taps, lanes, tokens).astype(BF16)
    for j in range(fold):
        sums[0:modes, j * LANES : (j + 1) * LANES] = acc[pl.ds(j, modes, stride=fold), :]


def state_streams(feat, og, filt, dec, far, res, bias, sig, payloads):
    tokens, channels = og.shape
    fold = channels // LANES
    modes = dec.shape[0] // fold
    return pl.pallas_call(
        functools.partial(state_kernel, len(payloads)),
        in_specs=[whole()] * (8 + len(payloads)),
        out_specs=[whole()] * 3,
        out_shape=[
            jax.ShapeDtypeStruct((2, tokens, channels), BF16),
            jax.ShapeDtypeStruct((modes + 1, channels), F32),
            jax.ShapeDtypeStruct(((tokens + 2) * fold, LANES), F32),
        ],
        scratch_shapes=[pltpu.VMEM((modes * fold, LANES), F32), pltpu.VMEM((tokens * fold, LANES), F32)]
        + [pltpu.VMEM((tokens + 8, channels), F32)] * 2,
        compiler_params=params(),
        cost_estimate=cost(8 * tokens * channels * modes, 40 * tokens * channels),
        name="state_streams",
    )(feat, og, filt, dec, far, res, bias, sig, *payloads)


def product_kernel(plan, first, last, source, *refs):
    *refs, w_all, sems = refs
    *refs, out = refs
    before = None if first else refs[-1]
    w = refs[-1 - (not first)]
    features, channels = w_all.shape[1:]
    wide = min(512, features)
    moves = []
    for k, (stream, height, offset, _) in enumerate(plan):
        begin = pl.multiple_of((height * RING + source[offset]) * channels, LANES)
        for d in range(0, features, wide):
            moves.append(pltpu.make_async_copy(
                w.at[stream, pl.ds(d, wide), pl.ds(begin, channels)],
                w_all.at[k, pl.ds(d, wide)],
                sems.at[k, d // wide],
            ))
            moves[-1].start()
    totals = {}
    for k, (_, _, _, parts) in enumerate(plan):
        x = [refs[n][h, p] for n, h, p in parts]
        x = x[0] if len(x) == 1 else jnp.concatenate(x, axis=0)
        for d in range(0, features, wide):
            moves.pop(0).wait()
            rows = slice(d, d + wide)
            y = lax.dot_general(w_all[k, rows], x, (((1,), (1,)), ((), ())), preferred_element_type=F32)
            if k:
                y = y + (out[:, rows].T if last else out[rows])
            elif not first:
                y = y + before[rows]
            if last:
                out[:, rows] = y.T
            else:
                out[rows] = y


def add_product(total, pieces, sources, w_proj, last=False):
    features = w_proj.shape[1]
    arrays, plan = [], []
    for array, stream, offset in pieces:
        halves = array if isinstance(array, tuple) else (array,)
        heights, streams, _, channels = halves[0].shape
        for h in range(heights):
            for p in range(streams):
                plan.append((stream + p, h, offset, [(len(arrays) + n, h, p) for n in range(len(halves))]))
        arrays += halves
    tokens = sum(arrays[n].shape[2] for n, _, _ in plan[0][3])
    first = total is None
    return pl.pallas_call(
        functools.partial(product_kernel, plan, first, last),
        in_specs=[pl.BlockSpec(memory_space=pltpu.SMEM)]
        + [whole()] * len(arrays)
        + [in_hbm()]
        + [whole()] * (not first),
        out_specs=whole(),
        out_shape=jax.ShapeDtypeStruct((tokens, features) if last else (features, tokens), F32),
        scratch_shapes=[
            pltpu.VMEM((len(plan), features, channels), BF16),
            pltpu.SemaphoreType.DMA((len(plan), max(1, features // 512))),
        ],
        compiler_params=params(),
        cost_estimate=cost(
            2 * tokens * features * channels * len(plan),
            2 * features * channels * len(plan) + 8 * tokens * features,
        ),
        name="add_product",
    )(sources, *arrays, w_proj, *([] if first else [total]))


def ring_order(size):
    return list(range(0, size, 2)) + list(range(size - 1 - size % 2, 0, -2))


def after(array, *others):
    return lax.optimization_barrier((array, *others))[0]


def body(features, saved_conv, out_grad, short_filter, residue, rate, bias, w_proj):
    tokens, channels = out_grad.shape
    modes = rate.shape[1]
    blocks = lax.axis_size("ctx")
    groups = lax.axis_size("chan")
    ring = min(groups, RING)
    heights = groups // ring

    order = ring_order(ring)
    place = [order.index(i) for i in range(ring)]
    table = jnp.array([[order[(place[i] + d) % ring] for d in range(ring)] for i in range(ring)], jnp.int32)
    sources = lax.dynamic_index_in_dim(table, lax.rem(lax.axis_index("chan"), ring), 0, False)
    pairs = {
        by: [
            (h * ring + order[i], h * ring + order[(i + by) % ring])
            for h in range(heights)
            for i in range(ring)
        ]
        for by in (1, -1)
    }

    def up(x):
        return lax.ppermute(x, "chan", pairs[1])

    def down(x):
        return lax.ppermute(x, "chan", pairs[-1])

    def stacked(block):
        if heights == 1:
            return block[None]
        groups = [[h * ring + i for h in range(heights)] for i in range(ring)]
        return lax.all_gather(block, "chan", axis_index_groups=groups)

    def from_later(array, by):
        return lax.ppermute(array, "ctx", [(i, i - by) for i in range(by, blocks)])

    fold = channels // LANES
    feat, conv, og, filt, bias_row, dec, far, res, sig, own = front(
        features, saved_conv, out_grad, short_filter, residue.T, rate.T, bias[None]
    )
    payloads = [from_later(own, by) for by in range(1, min(3, blocks))]
    gate = gate_stream(feat, conv, og, filt, bias_row, payloads[0])
    own, gate = lax.optimization_barrier((own, gate))
    payloads += [from_later(own, by) for by in range(3, blocks)]
    a0 = stacked(gate)
    a1, z1 = up(a0), down(a0)
    rounds, sums, gp = state_streams(
        feat, og, filt, dec, far, res, bias_row.reshape(fold, LANES), sig, payloads
    )
    b0 = stacked(rounds)
    half = tokens // 2
    back = ring // 2

    b1, y1 = up(b0), down(b0)
    a1, z1, b0 = lax.optimization_barrier((a1, z1, b0))
    a2, z2 = up(a1), down(z1)
    total = add_product(
        None, [(a0, 0, 0), (b0, 1, 0), (a1, 0, ring - 1), (z1, 0, 1)], sources, w_proj
    )
    a2, z2, total = lax.optimization_barrier((a2, z2, total))
    a3, z3 = up(a2), down(z2)
    total = add_product(total, [(a2, 0, ring - 2), (z2, 0, 2)], sources, w_proj)
    gp = after(gp, total)
    grads = gradients(feat, conv, og, filt, bias_row, payloads[0], gp)
    b1, y1, total, grads = lax.optimization_barrier((b1, y1, total, grads))
    b2, y2 = up(b1), down(y1)
    total = add_product(total, [(b1, 1, ring - 1), (y1, 1, 1)], sources, w_proj)
    a3, z3, total = lax.optimization_barrier((a3, z3, total))
    tail = (up(a3[:, :, :half]), down(z3[:, :, half:]))
    total = add_product(total, [(a3, 0, ring - 3), (z3, 0, 3)], sources, w_proj)
    sums = after(sums, total)
    by = 1
    while by < blocks:
        sums = sums + lax.ppermute(sums, "ctx", [(i, i ^ by) for i in range(blocks)])
        by *= 2
    sums = sums * (tokens * blocks) ** (-0.5)
    b2, y2, total, sums = lax.optimization_barrier((b2, y2, total, sums))
    b3, y3 = up(b2), down(y2)
    total = add_product(total, [(b2, 1, ring - 2), (y2, 1, 2)], sources, w_proj)
    tail, total = lax.optimization_barrier((tail, total))
    total = add_product(total, [(tail, 0, back)], sources, w_proj)
    b3, y3, total = lax.optimization_barrier((b3, y3, total))
    b4, y4 = up(b3[:, :1]), down(y3[:, 1:])
    total = add_product(total, [(b3, 1, ring - 3), (y3, 1, 3)], sources, w_proj)
    grad_x = add_product(total, [(b4, 1, back), (y4, 2, back)], sources, w_proj, last=True)
    return (grads, grad_x, sums[:modes].T, sums[modes])


def solution(mesh):
    return jax.shard_map(
        body,
        mesh=mesh,
        in_specs=(
            P(None, "ctx", "chan"),
            P("ctx", "chan"),
            P("ctx", "chan"),
            P(None, None, "chan"),
            P("chan", None),
            P("chan", None),
            P("chan"),
            P(None, "chan", None),
        ),
        out_specs=(P(None, "ctx", "chan"), P("ctx", "chan"), P("chan", None), P("chan")),
        check_vma=False,
    )
```

```python
import functools

import jax
import jax.numpy as jnp
from jax import lax
from jax.experimental import pallas as pl
from jax.experimental.pallas import tpu as pltpu
from jax.sharding import PartitionSpec as P

LANES = 128
RING = 8
LONG = 1 << 36
SHORT = 1 << 16
VMEM = 16 * 1024 * 1024
F32 = jnp.float32
BF16 = jnp.bfloat16


def whole():
    return pl.BlockSpec(memory_space=pltpu.VMEM)


def in_hbm():
    return pl.BlockSpec(memory_space=pltpu.HBM)


def params():
    return pltpu.CompilerParams(vmem_limit_bytes=VMEM)


def cost(flops, size):
    return pl.CostEstimate(flops=flops, bytes_accessed=size, transcendentals=0)


def by_row(values, out, fold, base=0):
    for j in range(fold):
        out[pl.ds(base * fold + j, values.shape[0], stride=fold), :] = values[:, j * LANES : (j + 1) * LANES]


def front_kernel(features, saved_conv, out_grad, short_filter, residue, rate, bias, *refs):
    feat, conv, og, filt, bias_in, dec, far, res, sig, own, res_in, rate_in, sems = refs
    tokens, channels = og.shape
    modes = rate_in.shape[0]
    fold = channels // LANES
    moves = [
        pltpu.make_async_copy(source, target, sems.at[n])
        for n, (source, target) in enumerate((
            (rate, rate_in),
            (out_grad, og),
            (features, feat),
            (saved_conv, conv),
            (short_filter, filt),
            (residue, res_in),
            (bias, bias_in),
        ))
    ]
    for move in moves:
        move.start()
    moves[0].wait()
    by_row(jnp.exp(-rate_in[...]), dec, fold)
    by_row(jnp.exp(-(tokens - 2) * rate_in[...]), far, fold)
    moves[1].wait()
    moves[2].wait()
    for j in range(fold):
        lanes = slice(j * LANES, (j + 1) * LANES)
        sig[pl.ds(j, tokens, stride=fold), :] = og[:, lanes] * feat[0, :, lanes]
    decay = [dec[m * fold : (m + 1) * fold, :] for m in range(modes)]

    def step(i, states):
        row = sig[pl.ds((tokens - 1 - i) * fold, fold), :]
        return tuple(row + d * s for d, s in zip(decay, states))

    zero = tuple(jnp.zeros((fold, LANES), F32) for _ in range(modes))
    states = lax.fori_loop(0, tokens - 2, step, zero, unroll=6)
    for m in range(modes):
        own[m * fold : (m + 1) * fold, :] = states[m]
    own[modes * fold : (modes + 2) * fold, :] = sig[0 : 2 * fold, :]
    for n in range(3):
        by_row(feat[n, 0:2, :], own, fold, modes + 2 + 2 * n)
    by_row(og[0:2, :], own, fold, modes + 10)
    for n in range(3, 7):
        moves[n].wait()
    by_row(conv[0:2, :], own, fold, modes + 8)
    by_row(res_in[...], res, fold)


def front(features, saved_conv, out_grad, short_filter, residue, rate, bias):
    tokens, channels = out_grad.shape
    modes = rate.shape[0]
    fold = channels // LANES
    inputs = (features, saved_conv, out_grad, short_filter, residue, rate, bias)
    by_mode = pltpu.VMEM((modes * fold, LANES), F32)
    return pl.pallas_call(
        front_kernel,
        in_specs=[in_hbm()] * 7,
        out_specs=[whole()] * 10,
        out_shape=[pltpu.VMEM(a.shape, F32) for a in (*inputs[:4], bias)]
        + [by_mode] * 3
        + [pltpu.VMEM((tokens * fold, LANES), F32), pltpu.VMEM(((modes + 12) * fold, LANES), F32)],
        scratch_shapes=[pltpu.VMEM(rate.shape, F32)] * 2 + [pltpu.SemaphoreType.DMA((7,))],
        compiler_params=params(),
        cost_estimate=cost(4 * tokens * channels * modes, 20 * tokens * channels),
        name="front",
    )(*(pltpu.with_memory_space_constraint(a, pltpu.HBM) for a in inputs))


def tapped(ext, taps, lanes, tokens):
    total = taps[0][:, lanes] * ext[0:tokens, lanes]
    total = total + taps[1][:, lanes] * ext[1 : tokens + 1, lanes]
    return total + taps[2][:, lanes] * ext[2 : tokens + 2, lanes]


def rim_rows(later, which, j, fold):
    modes = later.shape[0] // fold - 12
    return later[pl.ds((modes + 2 + 2 * which) * fold + j, 2, stride=fold), :]


def gate_gradient(feat, conv, og, bias, later, ext):
    tokens, channels = og.shape
    fold = channels // LANES
    for j in range(fold):
        lanes = slice(j * LANES, (j + 1) * LANES)
        product = feat[1, :, lanes] * feat[2, :, lanes]
        ext[0:tokens, lanes] = og[:, lanes] * (conv[:, lanes] + bias[:, lanes] * product)
        key, value, held, cotangent = (rim_rows(later, n, j, fold) for n in (1, 2, 3, 4))
        ext[tokens : tokens + 2, lanes] = cotangent * (held + bias[:, lanes] * (key * value))


def gate_kernel(feat, conv, og, filt, bias, later, rounded, ext):
    tokens, channels = og.shape
    taps = [filt[0, j : j + 1, :] for j in range(3)]
    gate_gradient(feat, conv, og, bias, later, ext)
    for j in range(channels // LANES):
        lanes = slice(j * LANES, (j + 1) * LANES)
        rounded[0, lanes, :] = tapped(ext, taps, lanes, tokens).T.astype(BF16)


def gate_stream(feat, conv, og, filt, bias, later):
    tokens, channels = og.shape
    return pl.pallas_call(
        gate_kernel,
        in_specs=[whole()] * 6,
        out_specs=whole(),
        out_shape=jax.ShapeDtypeStruct((1, channels, tokens), BF16),
        scratch_shapes=[pltpu.VMEM((tokens + 8, channels), F32)],
        compiler_params=params(),
        cost_estimate=cost(12 * tokens * channels, 26 * tokens * channels),
        name="gate_stream",
    )(feat, conv, og, filt, bias, later)


def product_gradients(feat, gp, later, exts):
    tokens, channels = feat.shape[1:]
    fold = channels // LANES
    for j in range(fold):
        lanes = slice(j * LANES, (j + 1) * LANES)
        g = gp[pl.ds(j, tokens, stride=fold), :]
        rim = gp[pl.ds(tokens * fold + j, 2, stride=fold), :]
        for ext, n in zip(exts, (2, 1)):
            ext[0:tokens, lanes] = g * feat[n, :, lanes]
            ext[tokens : tokens + 2, lanes] = rim * rim_rows(later, n, j, fold)


def gradients_kernel(feat, conv, og, filt, bias, later, gp, out, first, second, third, ready, sems):
    tokens, channels = og.shape
    gate_gradient(feat, conv, og, bias, later, first)
    product_gradients(feat, gp, later, (second, third))
    moves = []
    for p, ext in enumerate((first, second, third)):
        taps = [filt[p, j : j + 1, :] for j in range(3)]
        for j in range(channels // LANES):
            lanes = slice(j * LANES, (j + 1) * LANES)
            ready[p, :, lanes] = tapped(ext, taps, lanes, tokens)
        moves.append(pltpu.make_async_copy(ready.at[p], out.at[p], sems.at[p]))
        moves[-1].start()
    for move in moves:
        move.wait()


def gradients(feat, conv, og, filt, bias, later, gp):
    tokens, channels = og.shape
    return pl.pallas_call(
        gradients_kernel,
        in_specs=[whole()] * 7,
        out_specs=in_hbm(),
        out_shape=jax.ShapeDtypeStruct((3, tokens, channels), F32),
        scratch_shapes=[pltpu.VMEM((tokens + 8, channels), F32)] * 3
        + [pltpu.VMEM((3, tokens, channels), F32), pltpu.SemaphoreType.DMA((3,))],
        compiler_params=params(),
        cost_estimate=cost(30 * tokens * channels, 40 * tokens * channels),
        name="gradients",
    )(feat, conv, og, filt, bias, later, gp)


def fetches(plan, source, w_proj, ready, sems):
    channels = ready.shape[2]
    moves = []
    for k, (stream, height, offset, _) in enumerate(plan):
        begin = pl.multiple_of((height * RING + source[offset]) * channels, LANES)
        columns = w_proj.at[stream, :, pl.ds(begin, channels)]
        moves.append(pltpu.make_async_copy(columns, ready.at[k], sems.at[k]))
    return moves


def state_kernel(later, plan, source, feat, og, filt, dec, far, res, bias, sig, *refs):
    payloads = refs[:later]
    w_proj, rounded, sums, gp, ready, acc, prod, first_ext, second_ext, sems = refs[later:]
    exts = first_ext, second_ext
    moves = fetches(plan, source, w_proj, ready, sems)
    for move in moves:
        move.start()
    tokens, channels = og.shape
    fold = channels // LANES
    modes = dec.shape[0] // fold
    for j in range(fold):
        lanes = slice(j * LANES, (j + 1) * LANES)
        p = feat[1, :, lanes] * feat[2, :, lanes]
        prod[pl.ds(j, tokens, stride=fold), :] = p
        s = og[:, lanes] * feat[0, :, lanes]
        sums[modes : modes + 1, lanes] = jnp.sum(s * p, axis=0, keepdims=True)

    def rows(ref, at):
        return ref[at * fold : (at + 1) * fold, :]

    direct = bias[...]
    group = 8
    for low in range(0, modes, group):
        chosen = range(low, min(low + group, modes))
        decay = [rows(dec, m) for m in chosen]
        weight = [rows(res, m) for m in chosen]
        reach = [rows(far, m) for m in chosen]
        state = [jnp.zeros((fold, LANES), F32) for _ in chosen]
        for n, payload in enumerate(reversed(payloads)):
            block_end = [rows(payload, m) + f * s for m, f, s in zip(chosen, reach, state)]
            if n < later - 1:
                s0, s1 = rows(payload, modes), rows(payload, modes + 1)
                state = [s0 + d * (s1 + d * s) for d, s in zip(decay, block_end)]
            else:
                state = block_end

        def corr(state, weight=weight):
            terms = [w * s for w, s in zip(weight, state)]
            while len(terms) > 1:
                terms = [a + b for a, b in zip(terms[::2], terms[1::2])] + terms[len(terms) // 2 * 2 :]
            return terms[0]

        def put(at, row, state, low=low, corr=corr):
            here = pl.ds(at * fold, fold)
            if low == 0:
                gp[here, :] = corr(state) + direct * row
            else:
                gp[here, :] = gp[here, :] + corr(state)

        for n in (1, 0):
            row = rows(payloads[0], modes + n)
            state = [row + d * s for d, s in zip(decay, state)]
            put(tokens + n, row, state)

        def step(i, carry, decay=decay, put=put):
            state, total = carry
            at = tokens - 1 - i
            row = sig[pl.ds(at * fold, fold), :]
            other = prod[pl.ds(at * fold, fold), :]
            state = [row + d * s for d, s in zip(decay, state)]
            total = [a + other * s for a, s in zip(total, state)]
            put(at, row, state)
            return state, total

        zero = [jnp.zeros((fold, LANES), F32) for _ in chosen]
        state, total = lax.fori_loop(0, tokens, step, (state, zero), unroll=4)
        for m, a in zip(chosen, total):
            acc[m * fold : (m + 1) * fold, :] = a

    product_gradients(feat, gp, payloads[0], exts)
    for p, ext in enumerate(exts):
        taps = [filt[p + 1, j : j + 1, :] for j in range(3)]
        for j in range(fold):
            lanes = slice(j * LANES, (j + 1) * LANES)
            rounded[p, lanes, :] = tapped(ext, taps, lanes, tokens).T.astype(BF16)
    for j in range(fold):
        sums[0:modes, j * LANES : (j + 1) * LANES] = acc[pl.ds(j, modes, stride=fold), :]
    for move in moves:
        move.wait()


def state_streams(feat, og, filt, dec, far, res, bias, sig, payloads, plan, sources, w_proj):
    tokens, channels = og.shape
    fold = channels // LANES
    modes = dec.shape[0] // fold
    return pl.pallas_call(
        functools.partial(state_kernel, len(payloads), plan),
        in_specs=[pl.BlockSpec(memory_space=pltpu.SMEM)] + [whole()] * (8 + len(payloads)) + [in_hbm()],
        out_specs=[whole()] * 4,
        out_shape=[
            pltpu.VMEM((2, channels, tokens), BF16),
            pltpu.VMEM((modes + 1, channels), F32),
            pltpu.VMEM(((tokens + 2) * fold, LANES), F32),
            pltpu.VMEM((len(plan), w_proj.shape[1], channels), BF16),
        ],
        scratch_shapes=[pltpu.VMEM((modes * fold, LANES), F32), pltpu.VMEM((tokens * fold, LANES), F32)]
        + [pltpu.VMEM((tokens + 8, channels), F32)] * 2
        + [pltpu.SemaphoreType.DMA((len(plan),))],
        compiler_params=params(),
        cost_estimate=cost(8 * tokens * channels * modes, 40 * tokens * channels),
        name="state_streams",
    )(sources, feat, og, filt, dec, far, res, bias, sig, *payloads, w_proj)


def product_kernel(plan, later, first, source, w_proj, w, *refs):
    refs = list(refs)
    moves = []
    if later:
        sems = refs.pop()
        moves = fetches(later, source, w_proj, refs.pop(), sems)
    out = refs.pop()
    before = None if first else refs.pop()
    for move in moves:
        move.start()
    features = w.shape[1]
    wide = min(512, features)
    for d in range(0, features, wide):
        rows = slice(d, d + wide)
        total = None if first else before[rows]
        for k, (_, _, _, parts) in enumerate(plan):
            x = [refs[n][h, p] for n, h, p in parts]
            x = x[0] if len(x) == 1 else jnp.concatenate(x, axis=0)
            y = jnp.dot(w[k, rows], x, preferred_element_type=F32)
            total = y if total is None else total + y
        if later:
            out[rows] = total
        else:
            out[:, rows] = total.T
    for move in moves:
        move.wait()


def steps_of(pieces):
    arrays, plan = [], []
    for array, stream, offset in pieces:
        halves = array if isinstance(array, tuple) else (array,)
        heights, streams = halves[0].shape[:2]
        for h in range(heights):
            for p in range(streams):
                plan.append((stream + p, h, offset, [(len(arrays) + n, h, p) for n in range(len(halves))]))
        arrays += halves
    return arrays, plan


def add_product(total, ready, pieces, later, sources, w_proj, span):
    features = w_proj.shape[1]
    arrays, plan = steps_of(pieces)
    channels, tokens = ready.shape[2], arrays[0].shape[3]
    first = total is None
    out_shape = [jax.ShapeDtypeStruct((tokens, features), F32)]
    scratch = []
    if later:
        out_shape = [
            pltpu.VMEM((features, tokens), F32),
            pltpu.VMEM((len(later), features, channels), BF16),
        ]
        scratch = [pltpu.SemaphoreType.DMA((len(later),))]
    return pl.pallas_call(
        functools.partial(product_kernel, plan, later, first),
        in_specs=[pl.BlockSpec(memory_space=pltpu.SMEM), in_hbm()]
        + [whole()] * (1 + len(arrays) + (not first)),
        out_specs=[whole()] * len(out_shape),
        out_shape=out_shape,
        scratch_shapes=scratch,
        compiler_params=params(),
        cost_estimate=cost(span, span // 256),
        name="add_product",
    )(sources, w_proj, ready, *arrays, *([] if first else [total]))


def ring_order(size):
    return list(range(0, size, 2)) + list(range(size - 1 - size % 2, 0, -2))


def after(array, *others):
    return lax.optimization_barrier((array, *others))[0]


def body(features, saved_conv, out_grad, short_filter, residue, rate, bias, w_proj):
    tokens, channels = out_grad.shape
    modes = rate.shape[1]
    blocks = lax.axis_size("ctx")
    groups = lax.axis_size("chan")
    ring = min(groups, RING)
    heights = groups // ring

    order = ring_order(ring)
    place = [order.index(i) for i in range(ring)]
    table = jnp.array([[order[(place[i] + d) % ring] for d in range(ring)] for i in range(ring)], jnp.int32)
    sources = lax.dynamic_index_in_dim(table, lax.rem(lax.axis_index("chan"), ring), 0, False)
    pairs = {
        by: [
            (h * ring + order[i], h * ring + order[(i + by) % ring])
            for h in range(heights)
            for i in range(ring)
        ]
        for by in (1, -1)
    }

    def up(x):
        return lax.ppermute(x, "chan", pairs[1])

    def down(x):
        return lax.ppermute(x, "chan", pairs[-1])

    def stacked(block):
        if heights == 1:
            return block[None]
        groups = [[h * ring + i for h in range(heights)] for i in range(ring)]
        return lax.all_gather(block, "chan", axis_index_groups=groups)

    def from_later(array, by):
        return lax.ppermute(array, "ctx", [(i, i - by) for i in range(by, blocks)])

    def exchanged(sums, by):
        return sums + lax.ppermute(sums, "ctx", [(i, i ^ by) for i in range(blocks)])

    fold = channels // LANES
    feat, conv, og, filt, bias_row, dec, far, res, sig, own = front(
        features, saved_conv, out_grad, short_filter, residue.T, rate.T, bias[None]
    )
    payloads = [from_later(own, by) for by in range(1, blocks)]
    payloads = list(lax.optimization_barrier(tuple(payloads)))
    gate = gate_stream(feat, conv, og, filt, bias_row, payloads[0])
    a0 = stacked(gate)
    a1, z1 = up(a0), down(a0)

    half = channels // 2
    back = ring // 2

    def plan_of(streams, *offsets):
        shape = jax.ShapeDtypeStruct((heights, len(streams), channels, tokens), BF16)
        return steps_of([(shape, streams[0], o) for o in offsets])[1]

    start = plan_of((0,), 0) + plan_of((1, 2), 0) + plan_of((0,), ring - 1, 1)
    payloads[0], a0 = lax.optimization_barrier((payloads[0], a0))
    rounds, sums, gp, ready = state_streams(
        feat, og, filt, dec, far, res, bias_row.reshape(fold, LANES), sig, payloads, start, sources, w_proj
    )
    b0 = stacked(rounds)

    b1, y1 = up(b0), down(b0)
    a1, z1, b0 = lax.optimization_barrier((a1, z1, b0))
    a2, z2 = up(a1), down(z1)
    total, ready = add_product(
        None, ready, [(a0, 0, 0), (b0, 1, 0), (a1, 0, ring - 1), (z1, 0, 1)],
        plan_of((1, 2), ring - 1, 1), sources, w_proj, LONG,
    )
    grads = gradients(feat, conv, og, filt, bias_row, payloads[0], after(gp, total))

    b1, y1, total, grads = lax.optimization_barrier((b1, y1, total, grads))
    b2, y2 = up(b1), down(y1)
    total, ready = add_product(
        total, ready, [(b1, 1, ring - 1), (y1, 1, 1)], plan_of((0,), ring - 2, 2), sources, w_proj, SHORT
    )

    a2, z2, total, sums = lax.optimization_barrier((a2, z2, total, sums))
    a3, z3 = up(a2), down(z2)
    distances = [1 << n for n in range((blocks - 1).bit_length())]
    for by in distances[:-1]:
        sums = exchanged(sums, by)
    total, ready = add_product(
        total, ready, [(a2, 0, ring - 2), (z2, 0, 2)], plan_of((1, 2), ring - 2, 2), sources, w_proj, LONG
    )

    b2, y2, total, sums = lax.optimization_barrier((b2, y2, total, sums))
    b3, y3 = up(b2), down(y2)
    total, ready = add_product(
        total, ready, [(b2, 1, ring - 2), (y2, 1, 2)], plan_of((0,), ring - 3, 3), sources, w_proj, SHORT
    )

    a3, z3, total, sums = lax.optimization_barrier((a3, z3, total, sums))
    for by in distances[-1:]:
        sums = exchanged(sums, by)
    sums = sums * (tokens * blocks) ** (-0.5)
    a4 = up(a3[:, :, :half]), down(z3[:, :, half:])
    total, ready = add_product(
        total, ready, [(a3, 0, ring - 3), (z3, 0, 3)], plan_of((1, 2), ring - 3, 3), sources, w_proj, LONG
    )

    b3, y3, total, sums = lax.optimization_barrier((b3, y3, total, sums))
    b4, y4 = up(b3[:, :1]), down(y3[:, 1:])
    total, ready = add_product(
        total, ready, [(b3, 1, ring - 3), (y3, 1, 3)], plan_of((0,), back), sources, w_proj, 9 << 28
    )

    a4, total = lax.optimization_barrier((a4, total))
    total, ready = add_product(total, ready, [(a4, 0, back)], plan_of((1, 2), back), sources, w_proj, 3 << 28)
    (grad_x,) = add_product(total, ready, [(b4, 1, back), (y4, 2, back)], None, sources, w_proj, SHORT)
    return (grads, grad_x, sums[:modes].T, sums[modes])


def solution(mesh):
    return jax.shard_map(
        body,
        mesh=mesh,
        in_specs=(
            P(None, "ctx", "chan"),
            P("ctx", "chan"),
            P("ctx", "chan"),
            P(None, None, "chan"),
            P("chan", None),
            P("chan", None),
            P("chan"),
            P(None, "chan", None),
        ),
        out_specs=(P(None, "ctx", "chan"), P("ctx", "chan"), P("chan", None), P("chan")),
        check_vma=False,
    )
```

```python
import functools

import jax
import jax.numpy as jnp
from jax import lax
from jax.experimental import pallas as pl
from jax.experimental.pallas import tpu as pltpu
from jax.sharding import PartitionSpec as P

LANES = 128
RING = 8
LONG = 1 << 36, 1 << 28
SHORT = 1 << 16, 1 << 8
MIDDLE = 1 << 30, 9 << 20
SMALL = 1 << 28, 3 << 20
VMEM = 8 * 1024 * 1024
F32 = jnp.float32
BF16 = jnp.bfloat16


def whole():
    return pl.BlockSpec(memory_space=pltpu.VMEM)


def in_hbm():
    return pl.BlockSpec(memory_space=pltpu.HBM)


def params():
    return pltpu.CompilerParams(vmem_limit_bytes=VMEM)


def cost(flops, size):
    return pl.CostEstimate(flops=flops, bytes_accessed=size, transcendentals=0)


def by_row(values, out, fold, base=0):
    for j in range(fold):
        out[pl.ds(base * fold + j, values.shape[0], stride=fold), :] = values[:, j * LANES : (j + 1) * LANES]


def front_kernel(features, saved_conv, out_grad, short_filter, residue, rate, bias, *refs):
    feat, conv, og, filt, bias_in, tables, own, brief, res_in, rate_in, sems = refs
    tokens, channels = og.shape
    modes = rate_in.shape[0]
    fold = channels // LANES
    moves = [
        pltpu.make_async_copy(source, target, sems.at[n])
        for n, (source, target) in enumerate((
            (rate, rate_in),
            (out_grad, og),
            (features.at[0], feat.at[0]),
            (features.at[pl.ds(1, 2)], feat.at[pl.ds(1, 2)]),
            (saved_conv, conv),
            (short_filter, filt),
            (residue, res_in),
            (bias, bias_in),
        ))
    ]
    for move in moves:
        move.start()
    moves[0].wait()
    by_row(jnp.exp(-rate_in[...]), tables, fold, tokens)
    by_row(jnp.exp(-(tokens - 2) * rate_in[...]), tables, fold, tokens + modes)
    moves[1].wait()
    moves[2].wait()
    for j in range(fold):
        lanes = slice(j * LANES, (j + 1) * LANES)
        tables[pl.ds(j, tokens, stride=fold), :] = og[:, lanes] * feat[0, :, lanes]
    decay = [tables[(tokens + m) * fold : (tokens + m + 1) * fold, :] for m in range(modes)]

    def step(i, states):
        row = tables[pl.ds((tokens - 1 - i) * fold, fold), :]
        return tuple(row + d * s for d, s in zip(decay, states))

    zero = tuple(jnp.zeros((fold, LANES), F32) for _ in range(modes))
    states = lax.fori_loop(0, tokens - 2, step, zero, unroll=6)
    for target in (own, brief):
        for m in range(modes):
            target[m * fold : (m + 1) * fold, :] = states[m]
        target[modes * fold : (modes + 2) * fold, :] = tables[0 : 2 * fold, :]
    for n in range(3, 8):
        moves[n].wait()
    for n in range(3):
        by_row(feat[n, 0:2, :], own, fold, modes + 2 + 2 * n)
    by_row(conv[0:2, :], own, fold, modes + 8)
    by_row(og[0:2, :], own, fold, modes + 10)
    by_row(res_in[...], tables, fold, tokens + 2 * modes)


def front(features, saved_conv, out_grad, short_filter, residue, rate, bias):
    tokens, channels = out_grad.shape
    modes = rate.shape[0]
    fold = channels // LANES
    inputs = (features, saved_conv, out_grad, short_filter, residue, rate, bias)
    return pl.pallas_call(
        front_kernel,
        in_specs=[in_hbm()] * 7,
        out_specs=[whole()] * 8,
        out_shape=[pltpu.VMEM(a.shape, F32) for a in (*inputs[:4], bias)]
        + [pltpu.VMEM((n * fold, LANES), F32) for n in (tokens + 3 * modes, modes + 12, modes + 2)],
        scratch_shapes=[pltpu.VMEM(rate.shape, F32)] * 2 + [pltpu.SemaphoreType.DMA((8,))],
        compiler_params=params(),
        cost_estimate=cost(4 * tokens * channels * modes, 20 * tokens * channels),
        name="front",
    )(*(pltpu.with_memory_space_constraint(a, pltpu.HBM) for a in inputs))


def tapped(ext, taps, lanes, tokens):
    total = taps[0][:, lanes] * ext[0:tokens, lanes]
    total = total + taps[1][:, lanes] * ext[1 : tokens + 1, lanes]
    return total + taps[2][:, lanes] * ext[2 : tokens + 2, lanes]


def rim_rows(later, which, j, fold):
    modes = later.shape[0] // fold - 12
    return later[pl.ds((modes + 2 + 2 * which) * fold + j, 2, stride=fold), :]


def gate_gradient(feat, conv, og, bias, later, ext):
    tokens, channels = og.shape
    fold = channels // LANES
    for j in range(fold):
        lanes = slice(j * LANES, (j + 1) * LANES)
        product = feat[1, :, lanes] * feat[2, :, lanes]
        ext[0:tokens, lanes] = og[:, lanes] * (conv[:, lanes] + bias[:, lanes] * product)
        key, value, held, cotangent = (rim_rows(later, n, j, fold) for n in (1, 2, 3, 4))
        ext[tokens : tokens + 2, lanes] = cotangent * (held + bias[:, lanes] * (key * value))


def gate_kernel(feat, conv, og, filt, bias, later, rounded, ext):
    tokens, channels = og.shape
    taps = [filt[0, j : j + 1, :] for j in range(3)]
    gate_gradient(feat, conv, og, bias, later, ext)
    for j in range(channels // LANES):
        lanes = slice(j * LANES, (j + 1) * LANES)
        rounded[0, lanes, :] = tapped(ext, taps, lanes, tokens).astype(BF16).T


def gate_stream(feat, conv, og, filt, bias, later):
    tokens, channels = og.shape
    return pl.pallas_call(
        gate_kernel,
        in_specs=[whole()] * 6,
        out_specs=whole(),
        out_shape=pltpu.VMEM((1, channels, tokens), BF16),
        scratch_shapes=[pltpu.VMEM((tokens + 8, channels), F32)],
        compiler_params=params(),
        cost_estimate=cost(*LONG),
        name="gate_stream",
    )(feat, conv, og, filt, bias, later)


def product_gradients(feat, gp, later, exts):
    tokens, channels = feat.shape[1:]
    fold = channels // LANES
    for j in range(fold):
        lanes = slice(j * LANES, (j + 1) * LANES)
        g = gp[pl.ds(j, tokens, stride=fold), :]
        rim = gp[pl.ds(tokens * fold + j, 2, stride=fold), :]
        for ext, n in zip(exts, (2, 1)):
            ext[0:tokens, lanes] = g * feat[n, :, lanes]
            ext[tokens : tokens + 2, lanes] = rim * rim_rows(later, n, j, fold)


def gradients_kernel(feat, conv, og, filt, bias, later, gp, out, first, second, third, ready, sems):
    tokens, channels = og.shape
    gate_gradient(feat, conv, og, bias, later, first)
    product_gradients(feat, gp, later, (second, third))
    moves = []
    for p, ext in enumerate((first, second, third)):
        taps = [filt[p, j : j + 1, :] for j in range(3)]
        for j in range(channels // LANES):
            lanes = slice(j * LANES, (j + 1) * LANES)
            ready[p, :, lanes] = tapped(ext, taps, lanes, tokens)
        moves.append(pltpu.make_async_copy(ready.at[p], out.at[p], sems.at[p]))
        moves[-1].start()
    for move in moves:
        move.wait()


def gradients(feat, conv, og, filt, bias, later, gp):
    tokens, channels = og.shape
    return pl.pallas_call(
        gradients_kernel,
        in_specs=[whole()] * 7,
        out_specs=in_hbm(),
        out_shape=jax.ShapeDtypeStruct((3, tokens, channels), F32),
        scratch_shapes=[pltpu.VMEM((tokens + 8, channels), F32)] * 3
        + [pltpu.VMEM((3, tokens, channels), F32), pltpu.SemaphoreType.DMA((3,))],
        compiler_params=params(),
        cost_estimate=cost(30 * tokens * channels, 40 * tokens * channels),
        name="gradients",
    )(feat, conv, og, filt, bias, later, gp)


def fetches(plan, source, w_proj, ready, sems):
    channels = ready.shape[1] // len(plan)
    moves = []
    for k, (stream, height, offset, _) in enumerate(plan):
        begin = pl.multiple_of((height * RING + source[offset]) * channels, LANES)
        columns = w_proj.at[stream, :, pl.ds(begin, channels)]
        moves.append(pltpu.make_async_copy(columns, ready.at[:, pl.ds(k * channels, channels)], sems.at[k]))
    return moves


def state_kernel(later, plan, source, feat, og, filt, bias, tables, *refs):
    payloads = refs[:later]
    w_proj, rounded, sums, gp, ready, acc, prod, first_ext, second_ext, sems = refs[later:]
    exts = first_ext, second_ext
    moves = fetches(plan, source, w_proj, ready, sems)
    for move in moves:
        move.start()
    tokens, channels = og.shape
    fold = channels // LANES
    modes = (tables.shape[0] // fold - tokens) // 3
    dec, far, res = (tokens + n * modes for n in range(3))
    for j in range(fold):
        lanes = slice(j * LANES, (j + 1) * LANES)
        p = feat[1, :, lanes] * feat[2, :, lanes]
        prod[pl.ds(j, tokens, stride=fold), :] = p
        s = og[:, lanes] * feat[0, :, lanes]
        sums[modes : modes + 1, lanes] = jnp.sum(s * p, axis=0, keepdims=True)

    def rows(ref, at):
        return ref[at * fold : (at + 1) * fold, :]

    direct = bias[...]
    group = 8
    for low in range(0, modes, group):
        chosen = range(low, min(low + group, modes))
        decay, weight, reach = ([rows(tables, at + m) for m in chosen] for at in (dec, res, far))
        state = [jnp.zeros((fold, LANES), F32) for _ in chosen]
        for n, payload in enumerate(reversed(payloads)):
            block_end = [rows(payload, m) + f * s for m, f, s in zip(chosen, reach, state)]
            if n < later - 1:
                s0, s1 = rows(payload, modes), rows(payload, modes + 1)
                state = [s0 + d * (s1 + d * s) for d, s in zip(decay, block_end)]
            else:
                state = block_end

        def corr(state, weight=weight):
            terms = [w * s for w, s in zip(weight, state)]
            while len(terms) > 1:
                terms = [a + b for a, b in zip(terms[::2], terms[1::2])] + terms[len(terms) // 2 * 2 :]
            return terms[0]

        def put(at, row, state, low=low, corr=corr):
            here = pl.ds(at * fold, fold)
            if low == 0:
                gp[here, :] = corr(state) + direct * row
            else:
                gp[here, :] = gp[here, :] + corr(state)

        for n in (1, 0):
            row = rows(payloads[0], modes + n)
            state = [row + d * s for d, s in zip(decay, state)]
            put(tokens + n, row, state)

        def step(i, carry, decay=decay, put=put):
            state, total = carry
            at = tokens - 1 - i
            row = tables[pl.ds(at * fold, fold), :]
            other = prod[pl.ds(at * fold, fold), :]
            state = [row + d * s for d, s in zip(decay, state)]
            total = [a + other * s for a, s in zip(total, state)]
            put(at, row, state)
            return state, total

        zero = [jnp.zeros((fold, LANES), F32) for _ in chosen]
        state, total = lax.fori_loop(0, tokens, step, (state, zero), unroll=4)
        for m, a in zip(chosen, total):
            acc[m * fold : (m + 1) * fold, :] = a

    product_gradients(feat, gp, payloads[0], exts)
    for p, ext in enumerate(exts):
        taps = [filt[p + 1, j : j + 1, :] for j in range(3)]
        for j in range(fold):
            lanes = slice(j * LANES, (j + 1) * LANES)
            rounded[p, lanes, :] = tapped(ext, taps, lanes, tokens).astype(BF16).T
    for j in range(fold):
        sums[0:modes, j * LANES : (j + 1) * LANES] = acc[pl.ds(j, modes, stride=fold), :]
    for move in moves:
        move.wait()


def state_streams(feat, og, filt, bias, tables, payloads, plan, sources, w_proj):
    tokens, channels = og.shape
    fold = channels // LANES
    modes = (tables.shape[0] // fold - tokens) // 3
    return pl.pallas_call(
        functools.partial(state_kernel, len(payloads), plan),
        in_specs=[pl.BlockSpec(memory_space=pltpu.SMEM)] + [whole()] * (5 + len(payloads)) + [in_hbm()],
        out_specs=[whole()] * 4,
        out_shape=[
            pltpu.VMEM((2, channels, tokens), BF16),
            pltpu.VMEM((modes + 1, channels), F32),
            pltpu.VMEM(((tokens + 2) * fold, LANES), F32),
            pltpu.VMEM((w_proj.shape[1], len(plan) * channels), BF16),
        ],
        scratch_shapes=[pltpu.VMEM((modes * fold, LANES), F32), pltpu.VMEM((tokens * fold, LANES), F32)]
        + [pltpu.VMEM((tokens + 8, channels), F32)] * 2
        + [pltpu.SemaphoreType.DMA((len(plan),))],
        compiler_params=params(),
        cost_estimate=cost(8 * tokens * channels * modes, 40 * tokens * channels),
        name="state_streams",
    )(sources, feat, og, filt, bias, tables, *payloads, w_proj)


def product_kernel(plan, base, later, first, last, source, w_proj, w, *refs):
    refs = list(refs)
    moves = []
    if later:
        sems = refs.pop()
        moves = fetches(later, source, w_proj, refs.pop(), sems)
    elif last:
        sems = refs.pop()
        turned = refs.pop()
    out = refs.pop()
    before = None if first else refs.pop()
    for move in moves:
        move.start()
    x = jnp.concatenate([refs[n][h, p] for *_, parts in plan for n, h, p in parts], axis=0)
    columns = slice(base * (x.shape[0] // len(plan)), (base + len(plan)) * (x.shape[0] // len(plan)))
    features = w.shape[0]
    wide = min(512, features)
    for d in range(0, features, wide):
        rows = slice(d, d + wide)
        y = jnp.dot(w[rows, columns], x, preferred_element_type=F32)
        if not first:
            y = y + before[rows]
        if last:
            turned[:, rows] = y.T
            moves.append(pltpu.make_async_copy(
                turned.at[:, pl.ds(d, wide)], out.at[:, pl.ds(d, wide)], sems.at[d // wide]
            ))
            moves[-1].start()
        else:
            out[rows] = y
    for move in moves:
        move.wait()


def steps_of(pieces):
    arrays, plan = [], []
    for array, places, stream, offset in pieces:
        halves = array if isinstance(array, tuple) else (array,)
        for h in range(halves[0].shape[0]):
            for p in places:
                plan.append((stream + p, h, offset, [(len(arrays) + n, h, p) for n in range(len(halves))]))
        arrays += halves
    return arrays, plan


def add_product(total, ready, base, pieces, later, last, sources, w_proj, span):
    features = w_proj.shape[1]
    arrays, plan = steps_of(pieces)
    channels, tokens = w_proj.shape[2] // lax.axis_size("chan"), arrays[0].shape[3]
    first = total is None
    out_specs = [whole()]
    out_shape = [pltpu.VMEM((features, tokens), F32)]
    scratch = []
    if last:
        out_specs = [in_hbm()]
        out_shape = [jax.ShapeDtypeStruct((tokens, features), F32)]
        scratch = [pltpu.VMEM((tokens, features), F32), pltpu.SemaphoreType.DMA((max(1, features // 512),))]
    elif later:
        out_specs += [whole()]
        out_shape += [pltpu.VMEM((features, len(later) * channels), BF16)]
        scratch = [pltpu.SemaphoreType.DMA((len(later),))]
    return pl.pallas_call(
        functools.partial(product_kernel, plan, base, later, first, last),
        in_specs=[pl.BlockSpec(memory_space=pltpu.SMEM), in_hbm()]
        + [whole()] * (1 + len(arrays) + (not first)),
        out_specs=out_specs,
        out_shape=out_shape,
        scratch_shapes=scratch,
        compiler_params=params(),
        cost_estimate=cost(*span),
        name="add_product",
    )(sources, w_proj, ready, *arrays, *([] if first else [total]))


def ring_order(size):
    return list(range(0, size, 2)) + list(range(size - 1 - size % 2, 0, -2))


def after(array, *others):
    return lax.optimization_barrier((array, *others))[0]


def body(features, saved_conv, out_grad, short_filter, residue, rate, bias, w_proj):
    tokens, channels = out_grad.shape
    modes = rate.shape[1]
    blocks = lax.axis_size("ctx")
    groups = lax.axis_size("chan")
    ring = min(groups, RING)
    heights = groups // ring

    order = ring_order(ring)
    place = [order.index(i) for i in range(ring)]
    table = jnp.array([[order[(place[i] + d) % ring] for d in range(ring)] for i in range(ring)], jnp.int32)
    sources = lax.dynamic_index_in_dim(table, lax.rem(lax.axis_index("chan"), ring), 0, False)
    pairs = {
        by: [
            (h * ring + order[i], h * ring + order[(i + by) % ring])
            for h in range(heights)
            for i in range(ring)
        ]
        for by in (1, -1)
    }

    def up(x):
        return lax.ppermute(x, "chan", pairs[1])

    def down(x):
        return lax.ppermute(x, "chan", pairs[-1])

    def stacked(block):
        if heights == 1:
            return block[None]
        groups = [[h * ring + i for h in range(heights)] for i in range(ring)]
        return lax.all_gather(block, "chan", axis_index_groups=groups)

    def from_later(array, by):
        return lax.ppermute(array, "ctx", [(i, i - by) for i in range(by, blocks)])

    def exchanged(sums, by):
        return sums + lax.ppermute(sums, "ctx", [(i, i ^ by) for i in range(blocks)])

    fold = channels // LANES
    feat, conv, og, filt, bias_row, tables, own, brief = front(
        features, saved_conv, out_grad, short_filter, residue.T, rate.T, bias[None]
    )
    payloads = [from_later(own, 1)] + [from_later(brief, by) for by in range(2, blocks)]
    gate = gate_stream(feat, conv, og, filt, bias_row, payloads[0])
    a0 = stacked(gate)
    a1, z1 = up(a0), down(a0)

    half = channels // 2
    back = ring // 2

    a, b = (0,), (0, 1)
    sets = [
        [("a0", a, 0, 0), ("b0", b, 1, 0)],
        [("a1", a, 0, ring - 1), ("z1", a, 0, 1)],
        [("b1", b, 1, ring - 1), ("y1", (0,), 1, 1)],
        [("y1", (1,), 1, 1), ("a2", a, 0, ring - 2), ("z2", a, 0, 2)],
        [("b2", b, 1, ring - 2), ("y2", (0,), 1, 2)],
        [("y2", (1,), 1, 2), ("a3", a, 0, ring - 3), ("z3", a, 0, 3)],
        [("b3", b, 1, ring - 3), ("y3", (0,), 1, 3)],
        [("y3", (1,), 1, 3), ("a4", a, 0, back)],
        [("b4", a, 1, back), ("y4", a, 2, back)],
    ]
    spans = [LONG, LONG, SHORT, LONG, SHORT, LONG, MIDDLE, SMALL, SHORT]
    hollow = jax.ShapeDtypeStruct((heights, 2, channels, tokens), BF16)

    def plan_of(n):
        return steps_of([(hollow, *piece[1:]) for piece in sets[n]])[1]

    def times(n, total, ready, **arrays):
        pieces = [(arrays[name], *rest) for name, *rest in sets[n]]
        later = plan_of(n + 1) if n < 6 else plan_of(7) + plan_of(8) if n == 6 else None
        base = len(plan_of(7)) if n == 8 else 0
        return add_product(total, ready, base, pieces, later, n == 8, sources, w_proj, spans[n])

    payloads[0], a0 = lax.optimization_barrier((payloads[0], a0))
    rounds, sums, gp, ready = state_streams(
        feat, og, filt, bias_row.reshape(fold, LANES), tables, payloads, plan_of(0), sources, w_proj
    )
    b0 = stacked(rounds)

    b1, y1 = up(b0), down(b0)
    a1, z1, b0 = lax.optimization_barrier((a1, z1, b0))
    a2, z2 = up(a1), down(z1)
    total, ready = times(0, None, ready, a0=a0, b0=b0)
    total, ready = times(1, total, ready, a1=a1, z1=z1)
    grads = gradients(feat, saved_conv, og, filt, bias_row, payloads[0], after(gp, total))

    b1, y1, total, grads = lax.optimization_barrier((b1, y1, total, grads))
    b2, y2 = up(b1), down(y1)
    total, ready = times(2, total, ready, b1=b1, y1=y1)

    a2, z2, total, sums = lax.optimization_barrier((a2, z2, total, sums))
    a3, z3 = up(a2), down(z2)
    distances = [1 << n for n in range((blocks - 1).bit_length())]
    for by in distances[:-1]:
        sums = exchanged(sums, by)
    total, ready = times(3, total, ready, y1=y1, a2=a2, z2=z2)

    b2, y2, total, sums = lax.optimization_barrier((b2, y2, total, sums))
    b3, y3 = up(b2), down(y2)
    total, ready = times(4, total, ready, b2=b2, y2=y2)

    a3, z3, total, sums = lax.optimization_barrier((a3, z3, total, sums))
    for by in distances[-1:]:
        sums = exchanged(sums, by)
    sums = sums * (tokens * blocks) ** (-0.5)
    a4 = up(a3[:, :, :half]), down(z3[:, :, half:])
    total, ready = times(5, total, ready, y2=y2, a3=a3, z3=z3)

    b3, y3, total, sums = lax.optimization_barrier((b3, y3, total, sums))
    b4, y4 = up(b3[:, :1]), down(y3[:, 1:])
    total, ready = times(6, total, ready, b3=b3, y3=y3)

    a4, total = lax.optimization_barrier((a4, total))
    (total,) = times(7, total, ready, y3=y3, a4=a4)
    (grad_x,) = times(8, total, ready, b4=b4, y4=y4)
    return (grads, grad_x, sums[:modes].T, sums[modes])


def solution(mesh):
    return jax.shard_map(
        body,
        mesh=mesh,
        in_specs=(
            P(None, "ctx", "chan"),
            P("ctx", "chan"),
            P("ctx", "chan"),
            P(None, None, "chan"),
            P("chan", None),
            P("chan", None),
            P("chan"),
            P(None, "chan", None),
        ),
        out_specs=(P(None, "ctx", "chan"), P("ctx", "chan"), P("chan", None), P("chan")),
        check_vma=False,
    )
```

```python
import functools

import jax
import jax.numpy as jnp
from jax import lax
from jax.experimental import pallas as pl
from jax.experimental.pallas import tpu as pltpu
from jax.sharding import PartitionSpec as P

LANES = 128
RING = 8
LONG = 1 << 36, 1 << 28
SHORT = 1 << 16, 1 << 8
MIDDLE = 1 << 30, 9 << 20
TAIL = 7 << 28, 13 << 20
VMEM = 8 * 1024 * 1024
F32 = jnp.float32
BF16 = jnp.bfloat16


def whole():
    return pl.BlockSpec(memory_space=pltpu.VMEM)


def in_hbm():
    return pl.BlockSpec(memory_space=pltpu.HBM)


def params():
    return pltpu.CompilerParams(vmem_limit_bytes=VMEM)


def cost(flops, size):
    return pl.CostEstimate(flops=flops, bytes_accessed=size, transcendentals=0)


def by_row(values, out, fold, base=0):
    for j in range(fold):
        out[pl.ds(base * fold + j, values.shape[0], stride=fold), :] = values[:, j * LANES : (j + 1) * LANES]


def front_kernel(features, saved_conv, out_grad, short_filter, residue, rate, bias, *refs):
    feat, conv, og, filt, bias_in, tables, own, res_in, rate_in, sems = refs
    tokens, channels = og.shape
    modes = rate_in.shape[0]
    fold = channels // LANES
    moves = [
        pltpu.make_async_copy(source, target, sems.at[n])
        for n, (source, target) in enumerate((
            (rate, rate_in),
            (out_grad, og),
            (features.at[0], feat.at[0]),
            (features.at[pl.ds(1, 2)], feat.at[pl.ds(1, 2)]),
            (saved_conv, conv),
            (short_filter, filt),
            (residue, res_in),
            (bias, bias_in),
        ))
    ]
    for move in moves:
        move.start()
    moves[0].wait()
    by_row(jnp.exp(-rate_in[...]), tables, fold, tokens)
    by_row(rate_in[...], tables, fold, tokens + modes)
    moves[1].wait()
    moves[2].wait()
    for j in range(fold):
        lanes = slice(j * LANES, (j + 1) * LANES)
        tables[pl.ds(j, tokens, stride=fold), :] = og[:, lanes] * feat[0, :, lanes]
    decay = [tables[(tokens + m) * fold : (tokens + m + 1) * fold, :] for m in range(modes)]

    def step(i, states):
        row = tables[pl.ds((tokens - 1 - i) * fold, fold), :]
        return tuple(row + d * s for d, s in zip(decay, states))

    zero = tuple(jnp.zeros((fold, LANES), F32) for _ in range(modes))
    states = lax.fori_loop(0, tokens - 2, step, zero, unroll=6)
    for m in range(modes):
        own[m * fold : (m + 1) * fold, :] = states[m]
    own[modes * fold : (modes + 2) * fold, :] = tables[0 : 2 * fold, :]
    for n in range(3, 8):
        moves[n].wait()
    for n in range(3):
        by_row(feat[n, 0:2, :], own, fold, modes + 2 + 2 * n)
    by_row(conv[0:2, :], own, fold, modes + 8)
    by_row(og[0:2, :], own, fold, modes + 10)
    by_row(res_in[...], tables, fold, tokens + 2 * modes)


def front(features, saved_conv, out_grad, short_filter, residue, rate, bias):
    tokens, channels = out_grad.shape
    modes = rate.shape[0]
    fold = channels // LANES
    inputs = (features, saved_conv, out_grad, short_filter, residue, rate, bias)
    return pl.pallas_call(
        front_kernel,
        in_specs=[in_hbm()] * 7,
        out_specs=[whole()] * 7,
        out_shape=[pltpu.VMEM(a.shape, F32) for a in (*inputs[:4], bias)]
        + [pltpu.VMEM((n * fold, LANES), F32) for n in (tokens + 3 * modes, modes + 12)],
        scratch_shapes=[pltpu.VMEM(rate.shape, F32)] * 2 + [pltpu.SemaphoreType.DMA((8,))],
        compiler_params=params(),
        cost_estimate=cost(4 * tokens * channels * modes, 20 * tokens * channels),
        name="front",
    )(*(pltpu.with_memory_space_constraint(a, pltpu.HBM) for a in inputs))


def tapped(ext, taps, lanes, tokens):
    total = taps[0][:, lanes] * ext[0:tokens, lanes]
    total = total + taps[1][:, lanes] * ext[1 : tokens + 1, lanes]
    return total + taps[2][:, lanes] * ext[2 : tokens + 2, lanes]


def rim_rows(later, which, j, fold):
    modes = later.shape[0] // fold - 12
    return later[pl.ds((modes + 2 + 2 * which) * fold + j, 2, stride=fold), :]


def gate_gradient(feat, conv, og, bias, later, ext):
    tokens, channels = og.shape
    fold = channels // LANES
    for j in range(fold):
        lanes = slice(j * LANES, (j + 1) * LANES)
        product = feat[1, :, lanes] * feat[2, :, lanes]
        ext[0:tokens, lanes] = og[:, lanes] * (conv[:, lanes] + bias[:, lanes] * product)
        key, value, held, cotangent = (rim_rows(later, n, j, fold) for n in (1, 2, 3, 4))
        ext[tokens : tokens + 2, lanes] = cotangent * (held + bias[:, lanes] * (key * value))


def carried(own, m, later, state, decay, rate, span, fold):
    modes = later.shape[0] // fold - 2
    s0, s1 = (later[(modes + n) * fold : (modes + n + 1) * fold, :] for n in (0, 1))
    return own[m * fold : (m + 1) * fold, :] + jnp.exp(-(span - 2) * rate) * (s0 + decay * (s1 + decay * state))


def joined(own, later, tables, span, modes, tokens, out):
    fold = out.shape[0] // (modes + 2)
    brief = later.at[pl.ds(0, (modes + 2) * fold)]
    for m in range(modes):
        here = slice(m * fold, (m + 1) * fold)
        decay, rate = (tables[(tokens + n * modes + m) * fold : (tokens + n * modes + m + 1) * fold, :] for n in (0, 1))
        out[here, :] = carried(own, m, brief, later[here, :], decay, rate, span, fold)
    out[modes * fold : (modes + 2) * fold, :] = own[modes * fold : (modes + 2) * fold, :]


def join(own, later, tables, span, modes, tokens):
    def kernel(own, later, tables, out):
        joined(own, later, tables, span, modes, tokens, out)

    return pl.pallas_call(
        kernel,
        in_specs=[whole()] * 3,
        out_specs=whole(),
        out_shape=pltpu.VMEM(own.shape, F32),
        compiler_params=params(),
        name="join",
    )(own, later, tables)


def gate_kernel(feat, conv, og, filt, bias, later, own, tables, rounded, joint, ext):
    tokens, channels = og.shape
    fold = channels // LANES
    joined(own, later, tables, tokens, joint.shape[0] // fold - 2, tokens, joint)
    taps = [filt[0, j : j + 1, :] for j in range(3)]
    gate_gradient(feat, conv, og, bias, later, ext)
    for j in range(channels // LANES):
        lanes = slice(j * LANES, (j + 1) * LANES)
        rounded[0, lanes, :] = tapped(ext, taps, lanes, tokens).astype(BF16).T


def gate_stream(feat, conv, og, filt, bias, later, own, tables):
    tokens, channels = og.shape
    fold = channels // LANES
    return pl.pallas_call(
        gate_kernel,
        in_specs=[whole()] * 8,
        out_specs=[whole()] * 2,
        out_shape=[pltpu.VMEM((1, channels, tokens), BF16), pltpu.VMEM((own.shape[0] - 10 * fold, LANES), F32)],
        scratch_shapes=[pltpu.VMEM((tokens + 8, channels), F32)],
        compiler_params=params(),
        cost_estimate=cost(*LONG),
        name="gate_stream",
    )(feat, conv, og, filt, bias, later, own, tables)


def product_gradients(feat, gp, later, exts):
    tokens, channels = feat.shape[1:]
    fold = channels // LANES
    for j in range(fold):
        lanes = slice(j * LANES, (j + 1) * LANES)
        g = gp[pl.ds(j, tokens, stride=fold), :]
        rim = gp[pl.ds(tokens * fold + j, 2, stride=fold), :]
        for ext, n in zip(exts, (2, 1)):
            ext[0:tokens, lanes] = g * feat[n, :, lanes]
            ext[tokens : tokens + 2, lanes] = rim * rim_rows(later, n, j, fold)


def gradients_kernel(feat, conv, og, filt, bias, later, gp, out, first, second, third, ready, sems):
    tokens, channels = og.shape
    gate_gradient(feat, conv, og, bias, later, first)
    product_gradients(feat, gp, later, (second, third))
    moves = []
    for p, ext in enumerate((first, second, third)):
        taps = [filt[p, j : j + 1, :] for j in range(3)]
        for j in range(channels // LANES):
            lanes = slice(j * LANES, (j + 1) * LANES)
            ready[p, :, lanes] = tapped(ext, taps, lanes, tokens)
        moves.append(pltpu.make_async_copy(ready.at[p], out.at[p], sems.at[p]))
        moves[-1].start()
    for move in moves:
        move.wait()


def gradients(feat, conv, og, filt, bias, later, gp):
    tokens, channels = og.shape
    return pl.pallas_call(
        gradients_kernel,
        in_specs=[whole()] * 7,
        out_specs=in_hbm(),
        out_shape=jax.ShapeDtypeStruct((3, tokens, channels), F32),
        scratch_shapes=[pltpu.VMEM((tokens + 8, channels), F32)] * 3
        + [pltpu.VMEM((3, tokens, channels), F32), pltpu.SemaphoreType.DMA((3,))],
        compiler_params=params(),
        cost_estimate=cost(30 * tokens * channels, 40 * tokens * channels),
        name="gradients",
    )(feat, conv, og, filt, bias, later, gp)


def on_ring(offset, ring):
    own = lax.rem(lax.axis_index("chan"), ring)
    place = jnp.where(lax.rem(own, 2) == 0, own // 2, ring - 1 - own // 2)
    place = lax.rem(place + offset, ring)
    return jnp.where(place < (ring + 1) // 2, 2 * place, 2 * (ring - 1 - place) + 1)


def fetches(plan, ring, w_proj, ready, sems):
    channels = ready.shape[1] // len(plan)
    moves = []
    for k, (stream, height, offset, _) in enumerate(plan):
        begin = pl.multiple_of((height * ring + on_ring(offset, ring)) * channels, LANES)
        columns = w_proj.at[stream, :, pl.ds(begin, channels)]
        moves.append(pltpu.make_async_copy(columns, ready.at[:, pl.ds(k * channels, channels)], sems.at[k]))
    return moves


def state_kernel(later, plan, ring, feat, og, filt, bias, tables, *refs):
    payloads = refs[:later]
    w_proj, rounded, sums, gp, ready, acc, prod, first_ext, second_ext, sems = refs[later:]
    exts = first_ext, second_ext
    moves = fetches(plan, ring, w_proj, ready, sems)
    for move in moves:
        move.start()
    tokens, channels = og.shape
    fold = channels // LANES
    modes = (tables.shape[0] // fold - tokens) // 3
    dec, raw, res = (tokens + n * modes for n in range(3))
    for j in range(fold):
        lanes = slice(j * LANES, (j + 1) * LANES)
        p = feat[1, :, lanes] * feat[2, :, lanes]
        prod[pl.ds(j, tokens, stride=fold), :] = p
        s = og[:, lanes] * feat[0, :, lanes]
        sums[modes : modes + 1, lanes] = jnp.sum(s * p, axis=0, keepdims=True)

    def rows(ref, at):
        return ref[at * fold : (at + 1) * fold, :]

    direct = bias[...]
    group = 8
    for low in range(0, modes, group):
        chosen = range(low, min(low + group, modes))
        decay, weight, rate = ([rows(tables, at + m) for m in chosen] for at in (dec, res, raw))
        state = [rows(payloads[-1], m) for m in chosen]
        for n in reversed(range(later - 1)):
            brief = payloads[n + 1].at[pl.ds(0, (modes + 2) * fold)]
            state = [
                carried(payloads[n], m, brief, s, d, r, tokens << n, fold)
                for m, s, d, r in zip(chosen, state, decay, rate)
            ]

        def corr(state, weight=weight):
            terms = [w * s for w, s in zip(weight, state)]
            while len(terms) > 1:
                terms = [a + b for a, b in zip(terms[::2], terms[1::2])] + terms[len(terms) // 2 * 2 :]
            return terms[0]

        def put(at, row, state, low=low, corr=corr):
            here = pl.ds(at * fold, fold)
            if low == 0:
                gp[here, :] = corr(state) + direct * row
            else:
                gp[here, :] = gp[here, :] + corr(state)

        for n in (1, 0):
            row = rows(payloads[0], modes + n)
            state = [row + d * s for d, s in zip(decay, state)]
            put(tokens + n, row, state)

        def step(i, carry, decay=decay, put=put):
            state, total = carry
            at = tokens - 1 - i
            row = tables[pl.ds(at * fold, fold), :]
            other = prod[pl.ds(at * fold, fold), :]
            state = [row + d * s for d, s in zip(decay, state)]
            total = [a + other * s for a, s in zip(total, state)]
            put(at, row, state)
            return state, total

        zero = [jnp.zeros((fold, LANES), F32) for _ in chosen]
        state, total = lax.fori_loop(0, tokens, step, (state, zero), unroll=4)
        for m, a in zip(chosen, total):
            acc[m * fold : (m + 1) * fold, :] = a

    product_gradients(feat, gp, payloads[0], exts)
    for p, ext in enumerate(exts):
        taps = [filt[p + 1, j : j + 1, :] for j in range(3)]
        for j in range(fold):
            lanes = slice(j * LANES, (j + 1) * LANES)
            rounded[p, lanes, :] = tapped(ext, taps, lanes, tokens).astype(BF16).T
    for j in range(fold):
        sums[0:modes, j * LANES : (j + 1) * LANES] = acc[pl.ds(j, modes, stride=fold), :]
    for move in moves:
        move.wait()


def state_streams(feat, og, filt, bias, tables, payloads, plan, ring, w_proj):
    tokens, channels = og.shape
    fold = channels // LANES
    modes = (tables.shape[0] // fold - tokens) // 3
    return pl.pallas_call(
        functools.partial(state_kernel, len(payloads), plan, ring),
        in_specs=[whole()] * (5 + len(payloads)) + [in_hbm()],
        out_specs=[whole()] * 4,
        out_shape=[
            pltpu.VMEM((2, channels, tokens), BF16),
            pltpu.VMEM((modes + 1, channels), F32),
            pltpu.VMEM(((tokens + 2) * fold, LANES), F32),
            pltpu.VMEM((w_proj.shape[1], len(plan) * channels), BF16),
        ],
        scratch_shapes=[pltpu.VMEM((modes * fold, LANES), F32), pltpu.VMEM((tokens * fold, LANES), F32)]
        + [pltpu.VMEM((tokens + 8, channels), F32)] * 2
        + [pltpu.SemaphoreType.DMA((len(plan),))],
        compiler_params=params(),
        cost_estimate=cost(8 * tokens * channels * modes, 40 * tokens * channels),
        name="state_streams",
    )(feat, og, filt, bias, tables, *payloads, w_proj)


def product_kernel(plan, base, later, first, last, ring, w_proj, w, *refs):
    refs = list(refs)
    moves = []
    if later:
        sems = refs.pop()
        moves = fetches(later, ring, w_proj, refs.pop(), sems)
    elif last:
        sems = refs.pop()
        turned = refs.pop()
    out = refs.pop()
    before = None if first else refs.pop()
    for move in moves:
        move.start()
    x = jnp.concatenate([refs[n][h, p] for *_, parts in plan for n, h, p in parts], axis=0)
    columns = slice(base * (x.shape[0] // len(plan)), (base + len(plan)) * (x.shape[0] // len(plan)))
    features = w.shape[0]
    wide = min(512, features)
    for d in range(0, features, wide):
        rows = slice(d, d + wide)
        y = jnp.dot(w[rows, columns], x, preferred_element_type=F32)
        if not first:
            y = y + before[rows]
        if last:
            turned[:, rows] = y.T
            moves.append(pltpu.make_async_copy(
                turned.at[:, pl.ds(d, wide)], out.at[:, pl.ds(d, wide)], sems.at[d // wide]
            ))
            moves[-1].start()
        else:
            out[rows] = y
    for move in moves:
        move.wait()


def steps_of(pieces):
    arrays, plan = [], []
    for array, places, stream, offset in pieces:
        halves = array if isinstance(array, tuple) else (array,)
        for h in range(halves[0].shape[0]):
            for p in places:
                plan.append((stream + p, h, offset, [(len(arrays) + n, h, p) for n in range(len(halves))]))
        arrays += halves
    return arrays, plan


def add_product(total, ready, base, pieces, later, last, ring, w_proj, span):
    features = w_proj.shape[1]
    arrays, plan = steps_of(pieces)
    channels, tokens = w_proj.shape[2] // lax.axis_size("chan"), arrays[0].shape[3]
    first = total is None
    out_specs = [whole()]
    out_shape = [pltpu.VMEM((features, tokens), F32)]
    scratch = []
    if last:
        out_specs = [in_hbm()]
        out_shape = [jax.ShapeDtypeStruct((tokens, features), F32)]
        scratch = [pltpu.VMEM((tokens, features), F32), pltpu.SemaphoreType.DMA((max(1, features // 512),))]
    elif later:
        out_specs += [whole()]
        out_shape += [pltpu.VMEM((features, len(later) * channels), BF16)]
        scratch = [pltpu.SemaphoreType.DMA((len(later),))]
    return pl.pallas_call(
        functools.partial(product_kernel, plan, base, later, first, last, ring),
        in_specs=[in_hbm()]
        + [whole()] * (1 + len(arrays) + (not first)),
        out_specs=out_specs,
        out_shape=out_shape,
        scratch_shapes=scratch,
        compiler_params=params(),
        cost_estimate=cost(*span),
        name="add_product",
    )(w_proj, ready, *arrays, *([] if first else [total]))


def ring_order(size):
    return list(range(0, size, 2)) + list(range(size - 1 - size % 2, 0, -2))


def after(array, *others):
    return lax.optimization_barrier((array, *others))[0]


def body(features, saved_conv, out_grad, short_filter, residue, rate, bias, w_proj):
    tokens, channels = out_grad.shape
    modes = rate.shape[1]
    blocks = lax.axis_size("ctx")
    groups = lax.axis_size("chan")
    ring = min(groups, RING)
    heights = groups // ring

    order = ring_order(ring)
    pairs = {
        by: [
            (h * ring + order[i], h * ring + order[(i + by) % ring])
            for h in range(heights)
            for i in range(ring)
        ]
        for by in (1, -1)
    }

    def up(x):
        return lax.ppermute(x, "chan", pairs[1])

    def down(x):
        return lax.ppermute(x, "chan", pairs[-1])

    def stacked(block):
        if heights == 1:
            return block[None]
        groups = [[h * ring + i for h in range(heights)] for i in range(ring)]
        return lax.all_gather(block, "chan", axis_index_groups=groups)

    def from_later(array, by):
        return lax.ppermute(array, "ctx", [(i, i - by) for i in range(by, blocks)])

    def exchanged(sums, by):
        return sums + lax.ppermute(sums, "ctx", [(i, i ^ by) for i in range(blocks)])

    fold = channels // LANES
    feat, conv, og, filt, bias_row, tables, own = front(
        features, saved_conv, out_grad, short_filter, residue.T, rate.T, bias[None]
    )
    payloads = [from_later(own, 1)]
    gate, joint = gate_stream(feat, conv, og, filt, bias_row, payloads[0], own, tables)
    by = 2
    while by < blocks:
        payloads.append(from_later(joint, by))
        if 2 * by < blocks:
            joint = join(joint, payloads[-1], tables, by * tokens, modes, tokens)
        by *= 2
    a0 = stacked(gate)
    a1, z1 = up(a0), down(a0)

    half = channels // 2
    back = ring // 2

    a, b = (0,), (0, 1)
    sets = [
        [("a0", a, 0, 0), ("b0", b, 1, 0)],
        [("a1", a, 0, ring - 1), ("z1", a, 0, 1)],
        [("b1", b, 1, ring - 1), ("y1", (0,), 1, 1)],
        [("y1", (1,), 1, 1), ("a2", a, 0, ring - 2), ("z2", a, 0, 2)],
        [("b2", b, 1, ring - 2), ("y2", (0,), 1, 2)],
        [("y2", (1,), 1, 2), ("a3", a, 0, ring - 3), ("z3", a, 0, 3)],
        [("b3", b, 1, ring - 3), ("y3", b, 1, 3)],
        [("a4", a, 0, back)],
        [("b4", a, 1, back), ("y4", a, 2, back)],
    ]
    spans = [LONG, LONG, SHORT, LONG, SHORT, LONG, MIDDLE, TAIL, SHORT]
    hollow = jax.ShapeDtypeStruct((heights, 2, channels, tokens), BF16)

    def plan_of(n):
        return steps_of([(hollow, *piece[1:]) for piece in sets[n]])[1]

    def times(n, total, ready, **arrays):
        pieces = [(arrays[name], *rest) for name, *rest in sets[n]]
        later = plan_of(n + 1) if n < 6 else plan_of(7) + plan_of(8) if n == 6 else None
        base = len(plan_of(7)) if n == 8 else 0
        return add_product(total, ready, base, pieces, later, n == 8, ring, w_proj, spans[n])

    payloads[0], a0 = lax.optimization_barrier((payloads[0], a0))
    rounds, sums, gp, ready = state_streams(
        feat, og, filt, bias_row.reshape(fold, LANES), tables, payloads, plan_of(0), ring, w_proj
    )
    b0 = stacked(rounds)

    b1, y1 = up(b0), down(b0)
    a1, z1, b0 = lax.optimization_barrier((a1, z1, b0))
    a2, z2 = up(a1), down(z1)
    total, ready = times(0, None, ready, a0=a0, b0=b0)
    total, ready = times(1, total, ready, a1=a1, z1=z1)
    grads = gradients(feat, saved_conv, og, filt, bias_row, payloads[0], after(gp, total))

    b1, y1, total, grads = lax.optimization_barrier((b1, y1, total, grads))
    b2, y2 = up(b1), down(y1)
    total, ready = times(2, total, ready, b1=b1, y1=y1)

    a2, z2, total, sums = lax.optimization_barrier((a2, z2, total, sums))
    a3, z3 = up(a2), down(z2)
    distances = [1 << n for n in range((blocks - 1).bit_length())]
    for by in distances[:-1]:
        sums = exchanged(sums, by)
    total, ready = times(3, total, ready, y1=y1, a2=a2, z2=z2)

    b2, y2, total, sums = lax.optimization_barrier((b2, y2, total, sums))
    b3, y3 = up(b2), down(y2)
    total, ready = times(4, total, ready, b2=b2, y2=y2)

    a3, z3, total, sums = lax.optimization_barrier((a3, z3, total, sums))
    for by in distances[-1:]:
        sums = exchanged(sums, by)
    sums = sums * (tokens * blocks) ** (-0.5)
    a4 = up(a3[:, :, :half]), down(z3[:, :, half:])
    total, ready = times(5, total, ready, y2=y2, a3=a3, z3=z3)

    grad_residue, grad_bias = sums[:modes].T, sums[modes]
    b3, y3, total, grad_residue, grad_bias = lax.optimization_barrier((b3, y3, total, grad_residue, grad_bias))
    b4, y4 = up(b3[:, :1]), down(y3[:, 1:])
    total, ready = times(6, total, ready, b3=b3, y3=y3)

    a4, total = lax.optimization_barrier((a4, total))
    (total,) = times(7, total, ready, a4=a4)
    (grad_x,) = times(8, total, ready, b4=b4, y4=y4)
    return (grads, grad_x, grad_residue, grad_bias)


def solution(mesh):
    return jax.shard_map(
        body,
        mesh=mesh,
        in_specs=(
            P(None, "ctx", "chan"),
            P("ctx", "chan"),
            P("ctx", "chan"),
            P(None, None, "chan"),
            P("chan", None),
            P("chan", None),
            P("chan"),
            P(None, "chan", None),
        ),
        out_specs=(P(None, "ctx", "chan"), P("ctx", "chan"), P("chan", None), P("chan")),
        check_vma=False,
    )
```

```python
import functools

import jax
import jax.numpy as jnp
from jax import lax
from jax.experimental import pallas as pl
from jax.experimental.pallas import tpu as pltpu
from jax.sharding import PartitionSpec as P

LANES = 128
RING = 8
LONG = 1 << 36, 1 << 28
SHORT = 1 << 16, 1 << 8
MIDDLE = 1 << 30, 9 << 20
TAIL = 7 << 28, 13 << 20
VMEM = 8 * 1024 * 1024
F32 = jnp.float32
BF16 = jnp.bfloat16


def whole():
    return pl.BlockSpec(memory_space=pltpu.VMEM)


def in_hbm():
    return pl.BlockSpec(memory_space=pltpu.HBM)


def params():
    return pltpu.CompilerParams(vmem_limit_bytes=VMEM)


def cost(flops, size):
    return pl.CostEstimate(flops=flops, bytes_accessed=size, transcendentals=0)


def by_row(values, out, fold, base=0):
    for j in range(fold):
        out[pl.ds(base * fold + j, values.shape[0], stride=fold), :] = values[:, j * LANES : (j + 1) * LANES]


def front_kernel(features, saved_conv, out_grad, short_filter, residue, rate, bias, *refs):
    feat, conv, og, filt, bias_in, tables, own, res_in, rate_in, sems = refs
    tokens, channels = og.shape
    modes = rate_in.shape[0]
    fold = channels // LANES
    moves = [
        pltpu.make_async_copy(source, target, sems.at[n])
        for n, (source, target) in enumerate((
            (rate, rate_in),
            (out_grad, og),
            (features.at[0], feat.at[0]),
            (features.at[pl.ds(1, 2)], feat.at[pl.ds(1, 2)]),
            (saved_conv, conv),
            (short_filter, filt),
            (residue, res_in),
            (bias, bias_in),
        ))
    ]
    for move in moves:
        move.start()
    moves[0].wait()
    by_row(jnp.exp(-rate_in[...]), tables, fold, tokens)
    by_row(rate_in[...], tables, fold, tokens + modes)
    moves[1].wait()
    moves[2].wait()
    for j in range(fold):
        lanes = slice(j * LANES, (j + 1) * LANES)
        tables[pl.ds(j, tokens, stride=fold), :] = og[:, lanes] * feat[0, :, lanes]
    decay = [tables[(tokens + m) * fold : (tokens + m + 1) * fold, :] for m in range(modes)]

    def step(i, states):
        row = tables[pl.ds((tokens - 1 - i) * fold, fold), :]
        return tuple(row + d * s for d, s in zip(decay, states))

    zero = tuple(jnp.zeros((fold, LANES), F32) for _ in range(modes))
    states = lax.fori_loop(0, tokens - 2, step, zero, unroll=6)
    for m in range(modes):
        own[m * fold : (m + 1) * fold, :] = states[m]
    own[modes * fold : (modes + 2) * fold, :] = tables[0 : 2 * fold, :]
    for n in range(3, 8):
        moves[n].wait()
    for n in range(3):
        by_row(feat[n, 0:2, :], own, fold, modes + 2 + 2 * n)
    by_row(conv[0:2, :], own, fold, modes + 8)
    by_row(og[0:2, :], own, fold, modes + 10)
    by_row(res_in[...], tables, fold, tokens + 2 * modes)


def front(features, saved_conv, out_grad, short_filter, residue, rate, bias):
    tokens, channels = out_grad.shape
    modes = rate.shape[0]
    fold = channels // LANES
    inputs = (features, saved_conv, out_grad, short_filter, residue, rate, bias)
    return pl.pallas_call(
        front_kernel,
        in_specs=[in_hbm()] * 7,
        out_specs=[whole()] * 7,
        out_shape=[pltpu.VMEM(a.shape, F32) for a in (*inputs[:4], bias)]
        + [pltpu.VMEM((n * fold, LANES), F32) for n in (tokens + 3 * modes, modes + 12)],
        scratch_shapes=[pltpu.VMEM(rate.shape, F32)] * 2 + [pltpu.SemaphoreType.DMA((8,))],
        compiler_params=params(),
        cost_estimate=cost(4 * tokens * channels * modes, 20 * tokens * channels),
        name="front",
    )(*(pltpu.with_memory_space_constraint(a, pltpu.HBM) for a in inputs))


def tapped(ext, taps, lanes, tokens):
    total = taps[0][:, lanes] * ext[0:tokens, lanes]
    total = total + taps[1][:, lanes] * ext[1 : tokens + 1, lanes]
    return total + taps[2][:, lanes] * ext[2 : tokens + 2, lanes]


def rim_rows(later, which, j, fold):
    modes = later.shape[0] // fold - 12
    return later[pl.ds((modes + 2 + 2 * which) * fold + j, 2, stride=fold), :]


def gate_gradient(feat, conv, og, bias, later, ext):
    tokens, channels = og.shape
    fold = channels // LANES
    for j in range(fold):
        lanes = slice(j * LANES, (j + 1) * LANES)
        product = feat[1, :, lanes] * feat[2, :, lanes]
        ext[0:tokens, lanes] = og[:, lanes] * (conv[:, lanes] + bias[:, lanes] * product)
        key, value, held, cotangent = (rim_rows(later, n, j, fold) for n in (1, 2, 3, 4))
        ext[tokens : tokens + 2, lanes] = cotangent * (held + bias[:, lanes] * (key * value))


def carried(own, m, later, state, decay, rate, span, fold):
    modes = later.shape[0] // fold - 2
    s0, s1 = (later[(modes + n) * fold : (modes + n + 1) * fold, :] for n in (0, 1))
    return own[m * fold : (m + 1) * fold, :] + jnp.exp(-(span - 2) * rate) * (s0 + decay * (s1 + decay * state))


def joined(own, later, tables, span, modes, tokens, out):
    fold = out.shape[0] // (modes + 2)
    brief = later.at[pl.ds(0, (modes + 2) * fold)]
    for m in range(modes):
        here = slice(m * fold, (m + 1) * fold)
        decay, rate = (tables[(tokens + n * modes + m) * fold : (tokens + n * modes + m + 1) * fold, :] for n in (0, 1))
        out[here, :] = carried(own, m, brief, later[here, :], decay, rate, span, fold)
    out[modes * fold : (modes + 2) * fold, :] = own[modes * fold : (modes + 2) * fold, :]


def join(own, later, tables, span, modes, tokens):
    def kernel(own, later, tables, out):
        joined(own, later, tables, span, modes, tokens, out)

    return pl.pallas_call(
        kernel,
        in_specs=[whole()] * 3,
        out_specs=whole(),
        out_shape=pltpu.VMEM(own.shape, F32),
        compiler_params=params(),
        name="join",
    )(own, later, tables)


def gate_kernel(feat, conv, og, filt, bias, later, own, tables, rounded, joint, ext):
    tokens, channels = og.shape
    fold = channels // LANES
    joined(own, later, tables, tokens, joint.shape[0] // fold - 2, tokens, joint)
    taps = [filt[0, j : j + 1, :] for j in range(3)]
    gate_gradient(feat, conv, og, bias, later, ext)
    for j in range(channels // LANES):
        lanes = slice(j * LANES, (j + 1) * LANES)
        rounded[0, lanes, :] = tapped(ext, taps, lanes, tokens).astype(BF16).T


def gate_stream(feat, conv, og, filt, bias, later, own, tables):
    tokens, channels = og.shape
    fold = channels // LANES
    return pl.pallas_call(
        gate_kernel,
        in_specs=[whole()] * 8,
        out_specs=[whole()] * 2,
        out_shape=[pltpu.VMEM((1, channels, tokens), BF16), pltpu.VMEM((own.shape[0] - 10 * fold, LANES), F32)],
        scratch_shapes=[pltpu.VMEM((tokens + 8, channels), F32)],
        compiler_params=params(),
        cost_estimate=cost(*LONG),
        name="gate_stream",
    )(feat, conv, og, filt, bias, later, own, tables)


def product_gradients(feat, gp, later, exts):
    tokens, channels = feat.shape[1:]
    fold = channels // LANES
    for j in range(fold):
        lanes = slice(j * LANES, (j + 1) * LANES)
        g = gp[pl.ds(j, tokens, stride=fold), :]
        rim = gp[pl.ds(tokens * fold + j, 2, stride=fold), :]
        for ext, n in zip(exts, (2, 1)):
            ext[0:tokens, lanes] = g * feat[n, :, lanes]
            ext[tokens : tokens + 2, lanes] = rim * rim_rows(later, n, j, fold)


def gradients_kernel(feat, conv, og, filt, bias, later, gp, out, first, second, third, ready, sems):
    tokens, channels = og.shape
    gate_gradient(feat, conv, og, bias, later, first)
    product_gradients(feat, gp, later, (second, third))
    moves = []
    for p, ext in enumerate((first, second, third)):
        taps = [filt[p, j : j + 1, :] for j in range(3)]
        for j in range(channels // LANES):
            lanes = slice(j * LANES, (j + 1) * LANES)
            ready[p, :, lanes] = tapped(ext, taps, lanes, tokens)
        moves.append(pltpu.make_async_copy(ready.at[p], out.at[p], sems.at[p]))
        moves[-1].start()
    for move in moves:
        move.wait()


def gradients(feat, conv, og, filt, bias, later, gp):
    tokens, channels = og.shape
    return pl.pallas_call(
        gradients_kernel,
        in_specs=[whole()] * 7,
        out_specs=in_hbm(),
        out_shape=jax.ShapeDtypeStruct((3, tokens, channels), F32),
        scratch_shapes=[pltpu.VMEM((tokens + 8, channels), F32)] * 3
        + [pltpu.VMEM((3, tokens, channels), F32), pltpu.SemaphoreType.DMA((3,))],
        compiler_params=params(),
        cost_estimate=cost(30 * tokens * channels, 40 * tokens * channels),
        name="gradients",
    )(feat, conv, og, filt, bias, later, gp)


def on_ring(offset, ring):
    own = lax.rem(lax.axis_index("chan"), ring)
    place = jnp.where(lax.rem(own, 2) == 0, own // 2, ring - 1 - own // 2)
    place = lax.rem(place + offset, ring)
    return jnp.where(place < (ring + 1) // 2, 2 * place, 2 * (ring - 1 - place) + 1)


def fetches(plan, ring, w_proj, ready, sems):
    channels = ready.shape[1] // len(plan)
    moves = []
    for k, (stream, height, offset, _) in enumerate(plan):
        begin = pl.multiple_of((height * ring + on_ring(offset, ring)) * channels, LANES)
        columns = w_proj.at[stream, :, pl.ds(begin, channels)]
        moves.append(pltpu.make_async_copy(columns, ready.at[:, pl.ds(k * channels, channels)], sems.at[k]))
    return moves


def state_kernel(later, plan, ring, feat, og, filt, bias, tables, *refs):
    payloads = refs[:later]
    w_proj, rounded, sums, gp, ready, acc, prod, first_ext, second_ext, sems = refs[later:]
    exts = first_ext, second_ext
    moves = fetches(plan, ring, w_proj, ready, sems)
    for move in moves:
        move.start()
    tokens, channels = og.shape
    fold = channels // LANES
    modes = (tables.shape[0] // fold - tokens) // 3
    dec, raw, res = (tokens + n * modes for n in range(3))
    for j in range(fold):
        lanes = slice(j * LANES, (j + 1) * LANES)
        p = feat[1, :, lanes] * feat[2, :, lanes]
        prod[pl.ds(j, tokens, stride=fold), :] = p
        s = og[:, lanes] * feat[0, :, lanes]
        sums[modes : modes + 1, lanes] = jnp.sum(s * p, axis=0, keepdims=True)

    def rows(ref, at):
        return ref[at * fold : (at + 1) * fold, :]

    direct = bias[...]
    group = 8
    for low in range(0, modes, group):
        chosen = range(low, min(low + group, modes))
        decay, weight, rate = ([rows(tables, at + m) for m in chosen] for at in (dec, res, raw))
        state = [rows(payloads[-1], m) for m in chosen]
        for n in reversed(range(later - 1)):
            brief = payloads[n + 1].at[pl.ds(0, (modes + 2) * fold)]
            state = [
                carried(payloads[n], m, brief, s, d, r, tokens << n, fold)
                for m, s, d, r in zip(chosen, state, decay, rate)
            ]

        def corr(state, weight=weight):
            terms = [w * s for w, s in zip(weight, state)]
            while len(terms) > 1:
                terms = [a + b for a, b in zip(terms[::2], terms[1::2])] + terms[len(terms) // 2 * 2 :]
            return terms[0]

        def put(at, row, state, low=low, corr=corr):
            here = pl.ds(at * fold, fold)
            if low == 0:
                gp[here, :] = corr(state) + direct * row
            else:
                gp[here, :] = gp[here, :] + corr(state)

        for n in (1, 0):
            row = rows(payloads[0], modes + n)
            state = [row + d * s for d, s in zip(decay, state)]
            put(tokens + n, row, state)

        def step(i, carry, decay=decay, put=put):
            state, total = carry
            at = tokens - 1 - i
            row = tables[pl.ds(at * fold, fold), :]
            other = prod[pl.ds(at * fold, fold), :]
            state = [row + d * s for d, s in zip(decay, state)]
            total = [a + other * s for a, s in zip(total, state)]
            put(at, row, state)
            return state, total

        zero = [jnp.zeros((fold, LANES), F32) for _ in chosen]
        state, total = lax.fori_loop(0, tokens, step, (state, zero), unroll=4)
        for m, a in zip(chosen, total):
            acc[m * fold : (m + 1) * fold, :] = a

    product_gradients(feat, gp, payloads[0], exts)
    for p, ext in enumerate(exts):
        taps = [filt[p + 1, j : j + 1, :] for j in range(3)]
        for j in range(fold):
            lanes = slice(j * LANES, (j + 1) * LANES)
            rounded[p, lanes, :] = tapped(ext, taps, lanes, tokens).astype(BF16).T
    for j in range(fold):
        sums[0:modes, j * LANES : (j + 1) * LANES] = acc[pl.ds(j, modes, stride=fold), :]
    for move in moves:
        move.wait()


def state_streams(feat, og, filt, bias, tables, payloads, plan, ring, w_proj):
    tokens, channels = og.shape
    fold = channels // LANES
    modes = (tables.shape[0] // fold - tokens) // 3
    return pl.pallas_call(
        functools.partial(state_kernel, len(payloads), plan, ring),
        in_specs=[whole()] * (5 + len(payloads)) + [in_hbm()],
        out_specs=[whole()] * 4,
        out_shape=[
            pltpu.VMEM((2, channels, tokens), BF16),
            pltpu.VMEM((modes + 1, channels), F32),
            pltpu.VMEM(((tokens + 2) * fold, LANES), F32),
            pltpu.VMEM((w_proj.shape[1], len(plan) * channels), BF16),
        ],
        scratch_shapes=[pltpu.VMEM((modes * fold, LANES), F32), pltpu.VMEM((tokens * fold, LANES), F32)]
        + [pltpu.VMEM((tokens + 8, channels), F32)] * 2
        + [pltpu.SemaphoreType.DMA((len(plan),))],
        compiler_params=params(),
        cost_estimate=cost(4 << 30, 16 << 20),
        name="state_streams",
    )(feat, og, filt, bias, tables, *payloads, w_proj)


def product_kernel(plan, base, later, first, last, ring, w_proj, w, *refs):
    refs = list(refs)
    moves = []
    if later:
        sems = refs.pop()
        moves = fetches(later, ring, w_proj, refs.pop(), sems)
    elif last:
        sems = refs.pop()
        turned = refs.pop()
    out = refs.pop()
    before = None if first else refs.pop()
    for move in moves:
        move.start()
    x = jnp.concatenate([refs[n][h, p] for *_, parts in plan for n, h, p in parts], axis=0)
    columns = slice(base * (x.shape[0] // len(plan)), (base + len(plan)) * (x.shape[0] // len(plan)))
    features = w.shape[0]
    wide = min(512, features)
    for d in range(0, features, wide):
        rows = slice(d, d + wide)
        y = jnp.dot(w[rows, columns], x, preferred_element_type=F32)
        if not first:
            y = y + before[rows]
        if last:
            turned[:, rows] = y.T
            moves.append(pltpu.make_async_copy(
                turned.at[:, pl.ds(d, wide)], out.at[:, pl.ds(d, wide)], sems.at[d // wide]
            ))
            moves[-1].start()
        else:
            out[rows] = y
    for move in moves:
        move.wait()


def steps_of(pieces):
    arrays, plan = [], []
    for array, places, stream, offset in pieces:
        halves = array if isinstance(array, tuple) else (array,)
        for h in range(halves[0].shape[0]):
            for p in places:
                plan.append((stream + p, h, offset, [(len(arrays) + n, h, p) for n in range(len(halves))]))
        arrays += halves
    return arrays, plan


def add_product(total, ready, base, pieces, later, last, ring, w_proj, span):
    features = w_proj.shape[1]
    arrays, plan = steps_of(pieces)
    channels, tokens = w_proj.shape[2] // lax.axis_size("chan"), arrays[0].shape[3]
    first = total is None
    out_specs = [whole()]
    out_shape = [pltpu.VMEM((features, tokens), F32)]
    scratch = []
    if last:
        out_specs = [in_hbm()]
        out_shape = [jax.ShapeDtypeStruct((tokens, features), F32)]
        scratch = [pltpu.VMEM((tokens, features), F32), pltpu.SemaphoreType.DMA((max(1, features // 512),))]
    elif later:
        out_specs += [whole()]
        out_shape += [pltpu.VMEM((features, len(later) * channels), BF16)]
        scratch = [pltpu.SemaphoreType.DMA((len(later),))]
    return pl.pallas_call(
        functools.partial(product_kernel, plan, base, later, first, last, ring),
        in_specs=[in_hbm()]
        + [whole()] * (1 + len(arrays) + (not first)),
        out_specs=out_specs,
        out_shape=out_shape,
        scratch_shapes=scratch,
        compiler_params=params(),
        cost_estimate=cost(*span),
        name="add_product",
    )(w_proj, ready, *arrays, *([] if first else [total]))


def ring_order(size):
    return list(range(0, size, 2)) + list(range(size - 1 - size % 2, 0, -2))


def after(array, *others):
    return lax.optimization_barrier((array, *others))[0]


def body(features, saved_conv, out_grad, short_filter, residue, rate, bias, w_proj):
    tokens, channels = out_grad.shape
    modes = rate.shape[1]
    blocks = lax.axis_size("ctx")
    groups = lax.axis_size("chan")
    ring = min(groups, RING)
    heights = groups // ring

    order = ring_order(ring)
    pairs = {
        by: [
            (h * ring + order[i], h * ring + order[(i + by) % ring])
            for h in range(heights)
            for i in range(ring)
        ]
        for by in (1, -1)
    }

    def up(x):
        return lax.ppermute(x, "chan", pairs[1])

    def down(x):
        return lax.ppermute(x, "chan", pairs[-1])

    def stacked(block):
        if heights == 1:
            return block[None]
        groups = [[h * ring + i for h in range(heights)] for i in range(ring)]
        return lax.all_gather(block, "chan", axis_index_groups=groups)

    def from_later(array, by):
        return lax.ppermute(array, "ctx", [(i, i - by) for i in range(by, blocks)])

    def exchanged(sums, by):
        return sums + lax.ppermute(sums, "ctx", [(i, i ^ by) for i in range(blocks)])

    fold = channels // LANES
    feat, conv, og, filt, bias_row, tables, own = front(
        features, saved_conv, out_grad, short_filter, residue.T, rate.T, bias[None]
    )
    payloads = [from_later(own, 1)]
    gate, joint = gate_stream(feat, conv, og, filt, bias_row, payloads[0], own, tables)
    by = 2
    while by < blocks:
        payloads.append(from_later(joint, by))
        if 2 * by < blocks:
            joint = join(joint, payloads[-1], tables, by * tokens, modes, tokens)
        by *= 2
    a0 = stacked(gate)
    a1, z1 = up(a0), down(a0)

    half = channels // 2
    back = ring // 2

    a, b = (0,), (0, 1)
    sets = [
        [("a0", a, 0, 0), ("b0", b, 1, 0)],
        [("a1", a, 0, ring - 1), ("z1", a, 0, 1)],
        [("b1", b, 1, ring - 1), ("y1", (0,), 1, 1)],
        [("y1", (1,), 1, 1), ("a2", a, 0, ring - 2), ("z2", a, 0, 2)],
        [("b2", b, 1, ring - 2), ("y2", (0,), 1, 2)],
        [("y2", (1,), 1, 2), ("a3", a, 0, ring - 3), ("z3", a, 0, 3)],
        [("b3", b, 1, ring - 3), ("y3", b, 1, 3)],
        [("a4", a, 0, back)],
        [("b4", a, 1, back)],
        [("y4", a, 2, back)],
    ]
    spans = [LONG, LONG, SHORT, LONG, SHORT, LONG, MIDDLE, TAIL, SHORT, SHORT]
    hollow = jax.ShapeDtypeStruct((heights, 2, channels, tokens), BF16)

    def plan_of(n):
        return steps_of([(hollow, *piece[1:]) for piece in sets[n]])[1]

    def times(n, total, ready, **arrays):
        pieces = [(arrays[name], *rest) for name, *rest in sets[n]]
        after_next = [plan_of(k) for k in range(7, len(sets))]
        later = plan_of(n + 1) if n < 6 else sum(after_next, []) if n == 6 else None
        base = sum(len(plan) for plan in after_next[: max(0, n - 7)])
        return add_product(total, ready, base, pieces, later, n == len(sets) - 1, ring, w_proj, spans[n])

    payloads[0], a0 = lax.optimization_barrier((payloads[0], a0))
    rounds, sums, gp, ready = state_streams(
        feat, og, filt, bias_row.reshape(fold, LANES), tables, payloads, plan_of(0), ring, w_proj
    )
    b0 = stacked(rounds)

    b1, y1 = up(b0), down(b0)
    a1, z1, b0 = lax.optimization_barrier((a1, z1, b0))
    a2, z2 = up(a1), down(z1)
    total, ready = times(0, None, ready, a0=a0, b0=b0)
    total, ready = times(1, total, ready, a1=a1, z1=z1)
    grads = gradients(feat, saved_conv, og, filt, bias_row, payloads[0], after(gp, total))

    b1, y1, total, grads = lax.optimization_barrier((b1, y1, total, grads))
    b2, y2 = up(b1), down(y1)
    total, ready = times(2, total, ready, b1=b1, y1=y1)

    a2, z2, total, sums = lax.optimization_barrier((a2, z2, total, sums))
    a3, z3 = up(a2), down(z2)
    distances = [1 << n for n in range((blocks - 1).bit_length())]
    for by in distances[:-1]:
        sums = exchanged(sums, by)
    total, ready = times(3, total, ready, y1=y1, a2=a2, z2=z2)

    b2, y2, total, sums = lax.optimization_barrier((b2, y2, total, sums))
    b3, y3 = up(b2), down(y2)
    total, ready = times(4, total, ready, b2=b2, y2=y2)

    a3, z3, total, sums = lax.optimization_barrier((a3, z3, total, sums))
    for by in distances[-1:]:
        sums = exchanged(sums, by)
    sums = sums * (tokens * blocks) ** (-0.5)
    a4 = up(a3[:, :, :half]), down(z3[:, :, half:])
    total, ready = times(5, total, ready, y2=y2, a3=a3, z3=z3)

    grad_residue, grad_bias = sums[:modes].T, sums[modes]
    b3, y3, total, grad_residue, grad_bias = lax.optimization_barrier((b3, y3, total, grad_residue, grad_bias))
    b4, y4 = up(b3[:, :1]), down(y3[:, 1:])
    total, ready = times(6, total, ready, b3=b3, y3=y3)

    a4, total = lax.optimization_barrier((a4, total))
    (total,) = times(7, total, ready, a4=a4)
    (total,) = times(8, total, ready, b4=b4)
    (grad_x,) = times(9, total, ready, y4=y4)
    return (grads, grad_x, grad_residue, grad_bias)


def solution(mesh):
    return jax.shard_map(
        body,
        mesh=mesh,
        in_specs=(
            P(None, "ctx", "chan"),
            P("ctx", "chan"),
            P("ctx", "chan"),
            P(None, None, "chan"),
            P("chan", None),
            P("chan", None),
            P("chan"),
            P(None, "chan", None),
        ),
        out_specs=(P(None, "ctx", "chan"), P("ctx", "chan"), P("chan", None), P("chan")),
        check_vma=False,
    )
```

```python
import functools

import jax
import jax.numpy as jnp
from jax import lax
from jax.experimental import pallas as pl
from jax.experimental.pallas import tpu as pltpu
from jax.sharding import PartitionSpec as P

LANES = 128
RING = 8
LONG = 1 << 36, 1 << 28
SHORT = 1 << 16, 1 << 8
MIDDLE = 1 << 30, 9 << 20
TAIL = 7 << 28, 13 << 20
VMEM = 8 * 1024 * 1024
F32 = jnp.float32
BF16 = jnp.bfloat16


def whole():
    return pl.BlockSpec(memory_space=pltpu.VMEM)


def in_hbm():
    return pl.BlockSpec(memory_space=pltpu.HBM)


def params():
    return pltpu.CompilerParams(vmem_limit_bytes=VMEM)


def cost(flops, size):
    return pl.CostEstimate(flops=flops, bytes_accessed=size, transcendentals=0)


def by_row(values, out, fold, base=0):
    for j in range(fold):
        out[pl.ds(base * fold + j, values.shape[0], stride=fold), :] = values[:, j * LANES : (j + 1) * LANES]


def front_kernel(features, saved_conv, out_grad, short_filter, residue, rate, bias, *refs):
    feat, conv, og, filt, bias_in, tables, own, brief, res_in, rate_in, sems = refs
    tokens, channels = og.shape
    modes = rate_in.shape[0]
    fold = channels // LANES
    moves = [
        pltpu.make_async_copy(source, target, sems.at[n])
        for n, (source, target) in enumerate((
            (rate, rate_in),
            (out_grad, og),
            (features.at[0], feat.at[0]),
            (features.at[pl.ds(1, 2)], feat.at[pl.ds(1, 2)]),
            (saved_conv, conv),
            (short_filter, filt),
            (residue, res_in),
            (bias, bias_in),
        ))
    ]
    for move in moves:
        move.start()
    moves[0].wait()
    by_row(jnp.exp(-rate_in[...]), tables, fold, tokens)
    by_row(rate_in[...], tables, fold, tokens + modes)
    moves[1].wait()
    moves[2].wait()
    for j in range(fold):
        lanes = slice(j * LANES, (j + 1) * LANES)
        tables[pl.ds(j, tokens, stride=fold), :] = og[:, lanes] * feat[0, :, lanes]
    decay = [tables[(tokens + m) * fold : (tokens + m + 1) * fold, :] for m in range(modes)]

    def step(i, states):
        row = tables[pl.ds((tokens - 1 - i) * fold, fold), :]
        return tuple(row + d * s for d, s in zip(decay, states))

    zero = tuple(jnp.zeros((fold, LANES), F32) for _ in range(modes))
    states = lax.fori_loop(0, tokens - 2, step, zero, unroll=6)
    for target in (own, brief):
        for m in range(modes):
            target[m * fold : (m + 1) * fold, :] = states[m]
        target[modes * fold : (modes + 2) * fold, :] = tables[0 : 2 * fold, :]
    for n in range(3, 8):
        moves[n].wait()
    for n in range(3):
        by_row(feat[n, 0:2, :], own, fold, modes + 2 + 2 * n)
    by_row(conv[0:2, :], own, fold, modes + 8)
    by_row(og[0:2, :], own, fold, modes + 10)
    by_row(res_in[...], tables, fold, tokens + 2 * modes)


def front(features, saved_conv, out_grad, short_filter, residue, rate, bias):
    tokens, channels = out_grad.shape
    modes = rate.shape[0]
    fold = channels // LANES
    inputs = (features, saved_conv, out_grad, short_filter, residue, rate, bias)
    return pl.pallas_call(
        front_kernel,
        in_specs=[in_hbm()] * 7,
        out_specs=[whole()] * 8,
        out_shape=[pltpu.VMEM(a.shape, F32) for a in (*inputs[:4], bias)]
        + [pltpu.VMEM((n * fold, LANES), F32) for n in (tokens + 3 * modes, modes + 12, modes + 2)],
        scratch_shapes=[pltpu.VMEM(rate.shape, F32)] * 2 + [pltpu.SemaphoreType.DMA((8,))],
        compiler_params=params(),
        cost_estimate=cost(4 * tokens * channels * modes, 20 * tokens * channels),
        name="front",
    )(*(pltpu.with_memory_space_constraint(a, pltpu.HBM) for a in inputs))


def tapped(ext, taps, lanes, tokens):
    total = taps[0][:, lanes] * ext[0:tokens, lanes]
    total = total + taps[1][:, lanes] * ext[1 : tokens + 1, lanes]
    return total + taps[2][:, lanes] * ext[2 : tokens + 2, lanes]


def rim_rows(later, which, j, fold):
    modes = later.shape[0] // fold - 12
    return later[pl.ds((modes + 2 + 2 * which) * fold + j, 2, stride=fold), :]


def gate_gradient(feat, conv, og, bias, later, ext):
    tokens, channels = og.shape
    fold = channels // LANES
    for j in range(fold):
        lanes = slice(j * LANES, (j + 1) * LANES)
        product = feat[1, :, lanes] * feat[2, :, lanes]
        ext[0:tokens, lanes] = og[:, lanes] * (conv[:, lanes] + bias[:, lanes] * product)
        key, value, held, cotangent = (rim_rows(later, n, j, fold) for n in (1, 2, 3, 4))
        ext[tokens : tokens + 2, lanes] = cotangent * (held + bias[:, lanes] * (key * value))


def carried(own, m, later, state, decay, rate, span, fold):
    modes = own.shape[0] // fold - 2
    s0, s1 = (later[(modes + n) * fold : (modes + n + 1) * fold, :] for n in (0, 1))
    return own[m * fold : (m + 1) * fold, :] + jnp.exp(-(span - 2) * rate) * (s0 + decay * (s1 + decay * state))


def all_carried(summaries, spans, m, tables, tokens, fold):
    modes = summaries[0].shape[0] // fold - 2
    decay, rate = (tables[(tokens + n * modes + m) * fold : (tokens + n * modes + m + 1) * fold, :] for n in (0, 1))
    state = summaries[-1][m * fold : (m + 1) * fold, :]
    for own, later, span in reversed(list(zip(summaries, summaries[1:], spans))):
        state = carried(own, m, later, state, decay, rate, span, fold)
    return state


def join(summaries, span, tables, tokens, fold):
    def kernel(tables, *refs):
        *refs, out = refs
        modes = out.shape[0] // fold - 2
        for m in range(modes):
            out[m * fold : (m + 1) * fold, :] = all_carried(refs, [span] * (len(refs) - 1), m, tables, tokens, fold)
        out[modes * fold : (modes + 2) * fold, :] = refs[0][modes * fold : (modes + 2) * fold, :]

    return pl.pallas_call(
        kernel,
        in_specs=[whole()] * (1 + len(summaries)),
        out_specs=whole(),
        out_shape=pltpu.VMEM(summaries[0].shape, F32),
        compiler_params=params(),
        name="join",
    )(tables, *summaries)


def gate_kernel(feat, conv, og, filt, bias, later, rounded, ext):
    tokens, channels = og.shape
    taps = [filt[0, j : j + 1, :] for j in range(3)]
    gate_gradient(feat, conv, og, bias, later, ext)
    for j in range(channels // LANES):
        lanes = slice(j * LANES, (j + 1) * LANES)
        rounded[0, lanes, :] = tapped(ext, taps, lanes, tokens).astype(BF16).T


def gate_stream(feat, conv, og, filt, bias, later):
    tokens, channels = og.shape
    return pl.pallas_call(
        gate_kernel,
        in_specs=[whole()] * 6,
        out_specs=whole(),
        out_shape=pltpu.VMEM((1, channels, tokens), BF16),
        scratch_shapes=[pltpu.VMEM((tokens + 8, channels), F32)],
        compiler_params=params(),
        cost_estimate=cost(*LONG),
        name="gate_stream",
    )(feat, conv, og, filt, bias, later)


def product_gradients(feat, gp, later, exts):
    tokens, channels = feat.shape[1:]
    fold = channels // LANES
    for j in range(fold):
        lanes = slice(j * LANES, (j + 1) * LANES)
        g = gp[pl.ds(j, tokens, stride=fold), :]
        rim = gp[pl.ds(tokens * fold + j, 2, stride=fold), :]
        for ext, n in zip(exts, (2, 1)):
            ext[0:tokens, lanes] = g * feat[n, :, lanes]
            ext[tokens : tokens + 2, lanes] = rim * rim_rows(later, n, j, fold)


def gradients_kernel(feat, conv, og, filt, bias, later, gp, out, first, second, third, ready, sems):
    tokens, channels = og.shape
    gate_gradient(feat, conv, og, bias, later, first)
    product_gradients(feat, gp, later, (second, third))
    moves = []
    for p, ext in enumerate((first, second, third)):
        taps = [filt[p, j : j + 1, :] for j in range(3)]
        for j in range(channels // LANES):
            lanes = slice(j * LANES, (j + 1) * LANES)
            ready[p, :, lanes] = tapped(ext, taps, lanes, tokens)
        moves.append(pltpu.make_async_copy(ready.at[p], out.at[p], sems.at[p]))
        moves[-1].start()
    for move in moves:
        move.wait()


def gradients(feat, conv, og, filt, bias, later, gp):
    tokens, channels = og.shape
    return pl.pallas_call(
        gradients_kernel,
        in_specs=[whole()] * 7,
        out_specs=in_hbm(),
        out_shape=jax.ShapeDtypeStruct((3, tokens, channels), F32),
        scratch_shapes=[pltpu.VMEM((tokens + 8, channels), F32)] * 3
        + [pltpu.VMEM((3, tokens, channels), F32), pltpu.SemaphoreType.DMA((3,))],
        compiler_params=params(),
        cost_estimate=cost(30 * tokens * channels, 40 * tokens * channels),
        name="gradients",
    )(feat, conv, og, filt, bias, later, gp)


def on_ring(offset, ring):
    own = lax.rem(lax.axis_index("chan"), ring)
    place = jnp.where(lax.rem(own, 2) == 0, own // 2, ring - 1 - own // 2)
    place = lax.rem(place + offset, ring)
    return jnp.where(place < (ring + 1) // 2, 2 * place, 2 * (ring - 1 - place) + 1)


def fetches(plan, ring, w_proj, ready, sems):
    channels = ready.shape[1] // len(plan)
    moves = []
    for k, (stream, height, offset, _) in enumerate(plan):
        begin = pl.multiple_of((height * ring + on_ring(offset, ring)) * channels, LANES)
        columns = w_proj.at[stream, :, pl.ds(begin, channels)]
        moves.append(pltpu.make_async_copy(columns, ready.at[:, pl.ds(k * channels, channels)], sems.at[k]))
    return moves


def state_kernel(spans, plan, ring, feat, og, filt, bias, tables, *refs):
    later = len(spans)
    payloads = refs[:later]
    w_proj, rounded, sums, gp, ready, acc, prod, first_ext, second_ext, sems = refs[later:]
    exts = first_ext, second_ext
    moves = fetches(plan, ring, w_proj, ready, sems)
    for move in moves:
        move.start()
    tokens, channels = og.shape
    fold = channels // LANES
    modes = (tables.shape[0] // fold - tokens) // 3
    dec, res = tokens, tokens + 2 * modes
    briefs = [payloads[0].at[pl.ds(0, (modes + 2) * fold)], *payloads[1:]]
    for j in range(fold):
        lanes = slice(j * LANES, (j + 1) * LANES)
        p = feat[1, :, lanes] * feat[2, :, lanes]
        prod[pl.ds(j, tokens, stride=fold), :] = p
        s = og[:, lanes] * feat[0, :, lanes]
        sums[modes : modes + 1, lanes] = jnp.sum(s * p, axis=0, keepdims=True)

    def rows(ref, at):
        return ref[at * fold : (at + 1) * fold, :]

    direct = bias[...]
    group = 8
    for low in range(0, modes, group):
        chosen = range(low, min(low + group, modes))
        decay, weight = ([rows(tables, at + m) for m in chosen] for at in (dec, res))
        state = [all_carried(briefs, spans, m, tables, tokens, fold) for m in chosen]

        def corr(state, weight=weight):
            terms = [w * s for w, s in zip(weight, state)]
            while len(terms) > 1:
                terms = [a + b for a, b in zip(terms[::2], terms[1::2])] + terms[len(terms) // 2 * 2 :]
            return terms[0]

        def put(at, row, state, low=low, corr=corr):
            here = pl.ds(at * fold, fold)
            if low == 0:
                gp[here, :] = corr(state) + direct * row
            else:
                gp[here, :] = gp[here, :] + corr(state)

        for n in (1, 0):
            row = rows(payloads[0], modes + n)
            state = [row + d * s for d, s in zip(decay, state)]
            put(tokens + n, row, state)

        def step(i, carry, decay=decay, put=put):
            state, total = carry
            at = tokens - 1 - i
            row = tables[pl.ds(at * fold, fold), :]
            other = prod[pl.ds(at * fold, fold), :]
            state = [row + d * s for d, s in zip(decay, state)]
            total = [a + other * s for a, s in zip(total, state)]
            put(at, row, state)
            return state, total

        zero = [jnp.zeros((fold, LANES), F32) for _ in chosen]
        state, total = lax.fori_loop(0, tokens, step, (state, zero), unroll=4)
        for m, a in zip(chosen, total):
            acc[m * fold : (m + 1) * fold, :] = a

    product_gradients(feat, gp, payloads[0], exts)
    for p, ext in enumerate(exts):
        taps = [filt[p + 1, j : j + 1, :] for j in range(3)]
        for j in range(fold):
            lanes = slice(j * LANES, (j + 1) * LANES)
            rounded[p, lanes, :] = tapped(ext, taps, lanes, tokens).astype(BF16).T
    for j in range(fold):
        sums[0:modes, j * LANES : (j + 1) * LANES] = acc[pl.ds(j, modes, stride=fold), :]
    for move in moves:
        move.wait()


def state_streams(feat, og, filt, bias, tables, payloads, spans, plan, ring, w_proj):
    tokens, channels = og.shape
    fold = channels // LANES
    modes = (tables.shape[0] // fold - tokens) // 3
    return pl.pallas_call(
        functools.partial(state_kernel, spans, plan, ring),
        in_specs=[whole()] * (5 + len(payloads)) + [in_hbm()],
        out_specs=[whole()] * 4,
        out_shape=[
            pltpu.VMEM((2, channels, tokens), BF16),
            pltpu.VMEM((modes + 1, channels), F32),
            pltpu.VMEM(((tokens + 2) * fold, LANES), F32),
            pltpu.VMEM((w_proj.shape[1], len(plan) * channels), BF16),
        ],
        scratch_shapes=[pltpu.VMEM((modes * fold, LANES), F32), pltpu.VMEM((tokens * fold, LANES), F32)]
        + [pltpu.VMEM((tokens + 8, channels), F32)] * 2
        + [pltpu.SemaphoreType.DMA((len(plan),))],
        compiler_params=params(),
        cost_estimate=cost(4 << 30, 16 << 20),
        name="state_streams",
    )(feat, og, filt, bias, tables, *payloads, w_proj)


def product_kernel(plan, base, later, first, last, ring, w_proj, w, *refs):
    refs = list(refs)
    moves = []
    if later:
        sems = refs.pop()
        moves = fetches(later, ring, w_proj, refs.pop(), sems)
    elif last:
        sems = refs.pop()
        turned = refs.pop()
    out = refs.pop()
    before = None if first else refs.pop()
    for move in moves:
        move.start()
    x = jnp.concatenate([refs[n][h, p] for *_, parts in plan for n, h, p in parts], axis=0)
    columns = slice(base * (x.shape[0] // len(plan)), (base + len(plan)) * (x.shape[0] // len(plan)))
    features = w.shape[0]
    wide = min(512, features)
    for d in range(0, features, wide):
        rows = slice(d, d + wide)
        y = jnp.dot(w[rows, columns], x, preferred_element_type=F32)
        if not first:
            y = y + before[rows]
        if last:
            turned[:, rows] = y.T
            moves.append(pltpu.make_async_copy(
                turned.at[:, pl.ds(d, wide)], out.at[:, pl.ds(d, wide)], sems.at[d // wide]
            ))
            moves[-1].start()
        else:
            out[rows] = y
    for move in moves:
        move.wait()


def steps_of(pieces):
    arrays, plan = [], []
    for array, places, stream, offset in pieces:
        halves = array if isinstance(array, tuple) else (array,)
        for h in range(halves[0].shape[0]):
            for p in places:
                plan.append((stream + p, h, offset, [(len(arrays) + n, h, p) for n in range(len(halves))]))
        arrays += halves
    return arrays, plan


def add_product(total, ready, base, pieces, later, last, ring, w_proj, span):
    features = w_proj.shape[1]
    arrays, plan = steps_of(pieces)
    channels, tokens = w_proj.shape[2] // lax.axis_size("chan"), arrays[0].shape[3]
    first = total is None
    out_specs = [whole()]
    out_shape = [pltpu.VMEM((features, tokens), F32)]
    scratch = []
    if last:
        out_specs = [in_hbm()]
        out_shape = [jax.ShapeDtypeStruct((tokens, features), F32)]
        scratch = [pltpu.VMEM((tokens, features), F32), pltpu.SemaphoreType.DMA((max(1, features // 512),))]
    elif later:
        out_specs += [whole()]
        out_shape += [pltpu.VMEM((features, len(later) * channels), BF16)]
        scratch = [pltpu.SemaphoreType.DMA((len(later),))]
    return pl.pallas_call(
        functools.partial(product_kernel, plan, base, later, first, last, ring),
        in_specs=[in_hbm()]
        + [whole()] * (1 + len(arrays) + (not first)),
        out_specs=out_specs,
        out_shape=out_shape,
        scratch_shapes=scratch,
        compiler_params=params(),
        cost_estimate=cost(*span),
        name="add_product",
    )(w_proj, ready, *arrays, *([] if first else [total]))


def ring_order(size):
    return list(range(0, size, 2)) + list(range(size - 1 - size % 2, 0, -2))


def after(array, *others):
    return lax.optimization_barrier((array, *others))[0]


def body(features, saved_conv, out_grad, short_filter, residue, rate, bias, w_proj):
    tokens, channels = out_grad.shape
    modes = rate.shape[1]
    blocks = lax.axis_size("ctx")
    groups = lax.axis_size("chan")
    ring = min(groups, RING)
    heights = groups // ring

    order = ring_order(ring)
    pairs = {
        by: [
            (h * ring + order[i], h * ring + order[(i + by) % ring])
            for h in range(heights)
            for i in range(ring)
        ]
        for by in (1, -1)
    }

    def up(x):
        return lax.ppermute(x, "chan", pairs[1])

    def down(x):
        return lax.ppermute(x, "chan", pairs[-1])

    def stacked(block):
        if heights == 1:
            return block[None]
        groups = [[h * ring + i for h in range(heights)] for i in range(ring)]
        return lax.all_gather(block, "chan", axis_index_groups=groups)

    def from_later(array, by):
        return lax.ppermute(array, "ctx", [(i, i - by) for i in range(by, blocks)])

    def exchanged(sums, by):
        return sums + lax.ppermute(sums, "ctx", [(i, i ^ by) for i in range(blocks)])

    fold = channels // LANES
    feat, conv, og, filt, bias_row, tables, own, brief = front(
        features, saved_conv, out_grad, short_filter, residue.T, rate.T, bias[None]
    )
    payloads, spans = [from_later(own, 1)], [tokens]
    unit, window = 1, brief
    while unit < blocks:
        for by in range(len(payloads) % 3 + 1, 4):
            if by * unit < blocks:
                payloads.append(from_later(window, by * unit))
                spans.append(unit * tokens)
        unit *= 4
        if unit < blocks:
            near = [window, *payloads[-3:]]
            near[1] = near[1][: window.shape[0]]
            window = join(near, unit // 4 * tokens, tables, tokens, fold)
    gate = gate_stream(feat, conv, og, filt, bias_row, payloads[0])
    a0 = stacked(gate)
    a1, z1 = up(a0), down(a0)

    half = channels // 2
    back = ring // 2

    a, b = (0,), (0, 1)
    sets = [
        [("a0", a, 0, 0), ("b0", b, 1, 0)],
        [("a1", a, 0, ring - 1), ("z1", a, 0, 1)],
        [("b1", b, 1, ring - 1), ("y1", (0,), 1, 1)],
        [("y1", (1,), 1, 1), ("a2", a, 0, ring - 2), ("z2", a, 0, 2)],
        [("b2", b, 1, ring - 2), ("y2", (0,), 1, 2)],
        [("y2", (1,), 1, 2), ("a3", a, 0, ring - 3), ("z3", a, 0, 3)],
        [("b3", b, 1, ring - 3), ("y3", b, 1, 3)],
        [("a4", a, 0, back)],
        [("b4", a, 1, back)],
        [("y4", a, 2, back)],
    ]
    costs = [LONG, LONG, SHORT, LONG, SHORT, LONG, MIDDLE, TAIL, SHORT, SHORT]
    hollow = jax.ShapeDtypeStruct((heights, 2, channels, tokens), BF16)

    def plan_of(n):
        return steps_of([(hollow, *piece[1:]) for piece in sets[n]])[1]

    def times(n, total, ready, **arrays):
        pieces = [(arrays[name], *rest) for name, *rest in sets[n]]
        after_next = [plan_of(k) for k in range(7, len(sets))]
        later = plan_of(n + 1) if n < 6 else sum(after_next, []) if n == 6 else None
        base = sum(len(plan) for plan in after_next[: max(0, n - 7)])
        return add_product(total, ready, base, pieces, later, n == len(sets) - 1, ring, w_proj, costs[n])

    payloads[0], a0 = lax.optimization_barrier((payloads[0], a0))
    rounds, sums, gp, ready = state_streams(
        feat, og, filt, bias_row.reshape(fold, LANES), tables, payloads, spans, plan_of(0), ring, w_proj
    )
    b0 = stacked(rounds)

    b1, y1 = up(b0), down(b0)
    a1, z1, b0 = lax.optimization_barrier((a1, z1, b0))
    a2, z2 = up(a1), down(z1)
    total, ready = times(0, None, ready, a0=a0, b0=b0)
    total, ready = times(1, total, ready, a1=a1, z1=z1)
    grads = gradients(feat, saved_conv, og, filt, bias_row, payloads[0], after(gp, total))

    b1, y1, total, grads = lax.optimization_barrier((b1, y1, total, grads))
    b2, y2 = up(b1), down(y1)
    total, ready = times(2, total, ready, b1=b1, y1=y1)

    a2, z2, total, sums = lax.optimization_barrier((a2, z2, total, sums))
    a3, z3 = up(a2), down(z2)
    distances = [1 << n for n in range((blocks - 1).bit_length())]
    for by in distances[:-1]:
        sums = exchanged(sums, by)
    total, ready = times(3, total, ready, y1=y1, a2=a2, z2=z2)

    b2, y2, total, sums = lax.optimization_barrier((b2, y2, total, sums))
    b3, y3 = up(b2), down(y2)
    total, ready = times(4, total, ready, b2=b2, y2=y2)

    a3, z3, total, sums = lax.optimization_barrier((a3, z3, total, sums))
    for by in distances[-1:]:
        sums = exchanged(sums, by)
    sums = sums * (tokens * blocks) ** (-0.5)
    a4 = up(a3[:, :, :half]), down(z3[:, :, half:])
    total, ready = times(5, total, ready, y2=y2, a3=a3, z3=z3)

    grad_residue, grad_bias = sums[:modes].T, sums[modes]
    b3, y3, total, grad_residue, grad_bias = lax.optimization_barrier((b3, y3, total, grad_residue, grad_bias))
    b4, y4 = up(b3[:, :1]), down(y3[:, 1:])
    total, ready = times(6, total, ready, b3=b3, y3=y3)

    a4, total = lax.optimization_barrier((a4, total))
    (total,) = times(7, total, ready, a4=a4)
    (total,) = times(8, total, ready, b4=b4)
    (grad_x,) = times(9, total, ready, y4=y4)
    return (grads, grad_x, grad_residue, grad_bias)


def solution(mesh):
    return jax.shard_map(
        body,
        mesh=mesh,
        in_specs=(
            P(None, "ctx", "chan"),
            P("ctx", "chan"),
            P("ctx", "chan"),
            P(None, None, "chan"),
            P("chan", None),
            P("chan", None),
            P("chan"),
            P(None, "chan", None),
        ),
        out_specs=(P(None, "ctx", "chan"), P("ctx", "chan"), P("chan", None), P("chan")),
        check_vma=False,
    )
```

```python
import functools

import jax
import jax.numpy as jnp
from jax import lax
from jax.experimental import pallas as pl
from jax.experimental.pallas import tpu as pltpu
from jax.sharding import PartitionSpec as P

LANES = 128
RING = 8
LONG = 1 << 36, 1 << 28
SHORT = 1 << 16, 1 << 8
VMEM = 8 * 1024 * 1024
F32 = jnp.float32
BF16 = jnp.bfloat16


def whole():
    return pl.BlockSpec(memory_space=pltpu.VMEM)


def in_hbm():
    return pl.BlockSpec(memory_space=pltpu.HBM)


def params():
    return pltpu.CompilerParams(vmem_limit_bytes=VMEM)


def cost(flops, size):
    return pl.CostEstimate(flops=flops, bytes_accessed=size, transcendentals=0)


def by_row(values, out, fold, base=0):
    for j in range(fold):
        out[pl.ds(base * fold + j, values.shape[0], stride=fold), :] = values[:, j * LANES : (j + 1) * LANES]


def front_kernel(features, saved_conv, out_grad, short_filter, residue, rate, bias, *refs):
    feat, conv, og, filt, bias_in, tables, own, brief, res_in, rate_in, sems = refs
    tokens, channels = og.shape
    modes = rate_in.shape[0]
    fold = channels // LANES
    moves = [
        pltpu.make_async_copy(source, target, sems.at[n])
        for n, (source, target) in enumerate((
            (rate, rate_in),
            (out_grad, og),
            (features.at[0], feat.at[0]),
            (features.at[pl.ds(1, 2)], feat.at[pl.ds(1, 2)]),
            (saved_conv, conv),
            (short_filter, filt),
            (residue, res_in),
            (bias, bias_in),
        ))
    ]
    for move in moves:
        move.start()
    moves[0].wait()
    by_row(jnp.exp(-rate_in[...]), tables, fold, tokens)
    by_row(rate_in[...], tables, fold, tokens + modes)
    moves[1].wait()
    moves[2].wait()
    for j in range(fold):
        lanes = slice(j * LANES, (j + 1) * LANES)
        tables[pl.ds(j, tokens, stride=fold), :] = og[:, lanes] * feat[0, :, lanes]
    decay = [tables[(tokens + m) * fold : (tokens + m + 1) * fold, :] for m in range(modes)]

    def step(i, states):
        row = tables[pl.ds((tokens - 1 - i) * fold, fold), :]
        return tuple(row + d * s for d, s in zip(decay, states))

    zero = tuple(jnp.zeros((fold, LANES), F32) for _ in range(modes))
    states = lax.fori_loop(0, tokens - 2, step, zero, unroll=6)
    for target in (own, brief):
        for m in range(modes):
            target[m * fold : (m + 1) * fold, :] = states[m]
        target[modes * fold : (modes + 2) * fold, :] = tables[0 : 2 * fold, :]
    for n in range(3, 8):
        moves[n].wait()
    for n in range(3):
        by_row(feat[n, 0:2, :], own, fold, modes + 2 + 2 * n)
    by_row(conv[0:2, :], own, fold, modes + 8)
    by_row(og[0:2, :], own, fold, modes + 10)
    by_row(res_in[...], tables, fold, tokens + 2 * modes)


def front(features, saved_conv, out_grad, short_filter, residue, rate, bias):
    tokens, channels = out_grad.shape
    modes = rate.shape[0]
    fold = channels // LANES
    inputs = (features, saved_conv, out_grad, short_filter, residue, rate, bias)
    return pl.pallas_call(
        front_kernel,
        in_specs=[in_hbm()] * 7,
        out_specs=[whole()] * 8,
        out_shape=[pltpu.VMEM(a.shape, F32) for a in (*inputs[:4], bias)]
        + [pltpu.VMEM((n * fold, LANES), F32) for n in (tokens + 3 * modes, modes + 12, modes + 2)],
        scratch_shapes=[pltpu.VMEM(rate.shape, F32)] * 2 + [pltpu.SemaphoreType.DMA((8,))],
        compiler_params=params(),
        cost_estimate=cost(4 * tokens * channels * modes, 20 * tokens * channels),
        name="front",
    )(*(pltpu.with_memory_space_constraint(a, pltpu.HBM) for a in inputs))


def tapped(ext, taps, lanes, tokens):
    total = taps[0][:, lanes] * ext[0:tokens, lanes]
    total = total + taps[1][:, lanes] * ext[1 : tokens + 1, lanes]
    return total + taps[2][:, lanes] * ext[2 : tokens + 2, lanes]


def rim_rows(later, which, j, fold):
    modes = later.shape[0] // fold - 12
    return later[pl.ds((modes + 2 + 2 * which) * fold + j, 2, stride=fold), :]


def gate_gradient(feat, conv, og, bias, later, ext):
    tokens, channels = og.shape
    fold = channels // LANES
    for j in range(fold):
        lanes = slice(j * LANES, (j + 1) * LANES)
        product = feat[1, :, lanes] * feat[2, :, lanes]
        ext[0:tokens, lanes] = og[:, lanes] * (conv[:, lanes] + bias[:, lanes] * product)
        key, value, held, cotangent = (rim_rows(later, n, j, fold) for n in (1, 2, 3, 4))
        ext[tokens : tokens + 2, lanes] = cotangent * (held + bias[:, lanes] * (key * value))


def carried(own, m, later, state, decay, rate, span, fold):
    modes = own.shape[0] // fold - 2
    s0, s1 = (later[(modes + n) * fold : (modes + n + 1) * fold, :] for n in (0, 1))
    return own[m * fold : (m + 1) * fold, :] + jnp.exp(-(span - 2) * rate) * (s0 + decay * (s1 + decay * state))


def all_carried(summaries, spans, m, tables, tokens, fold):
    modes = summaries[0].shape[0] // fold - 2
    decay, rate = (tables[(tokens + n * modes + m) * fold : (tokens + n * modes + m + 1) * fold, :] for n in (0, 1))
    state = summaries[-1][m * fold : (m + 1) * fold, :]
    for own, later, span in reversed(list(zip(summaries, summaries[1:], spans))):
        state = carried(own, m, later, state, decay, rate, span, fold)
    return state


def join(summaries, span, tables, tokens, fold):
    def kernel(tables, *refs):
        *refs, out = refs
        modes = out.shape[0] // fold - 2
        for m in range(modes):
            out[m * fold : (m + 1) * fold, :] = all_carried(refs, [span] * (len(refs) - 1), m, tables, tokens, fold)
        out[modes * fold : (modes + 2) * fold, :] = refs[0][modes * fold : (modes + 2) * fold, :]

    return pl.pallas_call(
        kernel,
        in_specs=[whole()] * (1 + len(summaries)),
        out_specs=whole(),
        out_shape=pltpu.VMEM(summaries[0].shape, F32),
        compiler_params=params(),
        name="join",
    )(tables, *summaries)


def gate_kernel(feat, conv, og, filt, bias, later, rounded, ext):
    tokens, channels = og.shape
    taps = [filt[0, j : j + 1, :] for j in range(3)]
    gate_gradient(feat, conv, og, bias, later, ext)
    for j in range(channels // LANES):
        lanes = slice(j * LANES, (j + 1) * LANES)
        rounded[0, lanes, :] = tapped(ext, taps, lanes, tokens).astype(BF16).T


def gate_stream(feat, conv, og, filt, bias, later):
    tokens, channels = og.shape
    return pl.pallas_call(
        gate_kernel,
        in_specs=[whole()] * 6,
        out_specs=whole(),
        out_shape=pltpu.VMEM((1, channels, tokens), BF16),
        scratch_shapes=[pltpu.VMEM((tokens + 8, channels), F32)],
        compiler_params=params(),
        cost_estimate=cost(*LONG),
        name="gate_stream",
    )(feat, conv, og, filt, bias, later)


def product_gradients(feat, gp, later, exts):
    tokens, channels = feat.shape[1:]
    fold = channels // LANES
    for j in range(fold):
        lanes = slice(j * LANES, (j + 1) * LANES)
        g = gp[pl.ds(j, tokens, stride=fold), :]
        rim = gp[pl.ds(tokens * fold + j, 2, stride=fold), :]
        for ext, n in zip(exts, (2, 1)):
            ext[0:tokens, lanes] = g * feat[n, :, lanes]
            ext[tokens : tokens + 2, lanes] = rim * rim_rows(later, n, j, fold)


def gradients_kernel(feat, conv, og, filt, bias, later, gp, out, first, second, third, ready, sems):
    tokens, channels = og.shape
    gate_gradient(feat, conv, og, bias, later, first)
    product_gradients(feat, gp, later, (second, third))
    moves = []
    for p, ext in enumerate((first, second, third)):
        taps = [filt[p, j : j + 1, :] for j in range(3)]
        for j in range(channels // LANES):
            lanes = slice(j * LANES, (j + 1) * LANES)
            ready[p, :, lanes] = tapped(ext, taps, lanes, tokens)
        moves.append(pltpu.make_async_copy(ready.at[p], out.at[p], sems.at[p]))
        moves[-1].start()
    for move in moves:
        move.wait()


def gradients(feat, conv, og, filt, bias, later, gp):
    tokens, channels = og.shape
    return pl.pallas_call(
        gradients_kernel,
        in_specs=[whole()] * 7,
        out_specs=in_hbm(),
        out_shape=jax.ShapeDtypeStruct((3, tokens, channels), F32),
        scratch_shapes=[pltpu.VMEM((tokens + 8, channels), F32)] * 3
        + [pltpu.VMEM((3, tokens, channels), F32), pltpu.SemaphoreType.DMA((3,))],
        compiler_params=params(),
        cost_estimate=cost(30 * tokens * channels, 40 * tokens * channels),
        name="gradients",
    )(feat, conv, og, filt, bias, later, gp)


def on_ring(offset, ring):
    own = lax.rem(lax.axis_index("chan"), ring)
    place = jnp.where(lax.rem(own, 2) == 0, own // 2, ring - 1 - own // 2)
    place = lax.rem(place + offset, ring)
    return jnp.where(place < (ring + 1) // 2, 2 * place, 2 * (ring - 1 - place) + 1)


def fetches(plan, ring, w_proj, ready, sems):
    channels = ready.shape[1] // len(plan)
    moves = []
    for k, (stream, height, offset, _) in enumerate(plan):
        begin = pl.multiple_of((height * ring + on_ring(offset, ring)) * channels, LANES)
        columns = w_proj.at[stream, :, pl.ds(begin, channels)]
        moves.append(pltpu.make_async_copy(columns, ready.at[:, pl.ds(k * channels, channels)], sems.at[k]))
    return moves


def state_kernel(spans, plan, ring, feat, og, filt, bias, tables, *refs):
    later = len(spans)
    payloads = refs[:later]
    w_proj, rounded, sums, gp, ready, acc, prod, first_ext, second_ext, sems = refs[later:]
    exts = first_ext, second_ext
    moves = fetches(plan, ring, w_proj, ready, sems)
    for move in moves:
        move.start()
    tokens, channels = og.shape
    fold = channels // LANES
    modes = (tables.shape[0] // fold - tokens) // 3
    dec, res = tokens, tokens + 2 * modes
    briefs = [payloads[0].at[pl.ds(0, (modes + 2) * fold)], *payloads[1:]]
    for j in range(fold):
        lanes = slice(j * LANES, (j + 1) * LANES)
        p = feat[1, :, lanes] * feat[2, :, lanes]
        prod[pl.ds(j, tokens, stride=fold), :] = p
        s = og[:, lanes] * feat[0, :, lanes]
        sums[modes : modes + 1, lanes] = jnp.sum(s * p, axis=0, keepdims=True)

    def rows(ref, at):
        return ref[at * fold : (at + 1) * fold, :]

    direct = bias[...]
    group = 8
    for low in range(0, modes, group):
        chosen = range(low, min(low + group, modes))
        decay, weight = ([rows(tables, at + m) for m in chosen] for at in (dec, res))
        state = [all_carried(briefs, spans, m, tables, tokens, fold) for m in chosen]

        def corr(state, weight=weight):
            terms = [w * s for w, s in zip(weight, state)]
            while len(terms) > 1:
                terms = [a + b for a, b in zip(terms[::2], terms[1::2])] + terms[len(terms) // 2 * 2 :]
            return terms[0]

        def put(at, row, state, low=low, corr=corr):
            here = pl.ds(at * fold, fold)
            if low == 0:
                gp[here, :] = corr(state) + direct * row
            else:
                gp[here, :] = gp[here, :] + corr(state)

        for n in (1, 0):
            row = rows(payloads[0], modes + n)
            state = [row + d * s for d, s in zip(decay, state)]
            put(tokens + n, row, state)

        def step(i, carry, decay=decay, put=put):
            state, total = carry
            at = tokens - 1 - i
            row = tables[pl.ds(at * fold, fold), :]
            other = prod[pl.ds(at * fold, fold), :]
            state = [row + d * s for d, s in zip(decay, state)]
            total = [a + other * s for a, s in zip(total, state)]
            put(at, row, state)
            return state, total

        zero = [jnp.zeros((fold, LANES), F32) for _ in chosen]
        state, total = lax.fori_loop(0, tokens, step, (state, zero), unroll=4)
        for m, a in zip(chosen, total):
            acc[m * fold : (m + 1) * fold, :] = a

    product_gradients(feat, gp, payloads[0], exts)
    for p, ext in enumerate(exts):
        taps = [filt[p + 1, j : j + 1, :] for j in range(3)]
        for j in range(fold):
            lanes = slice(j * LANES, (j + 1) * LANES)
            rounded[p, lanes, :] = tapped(ext, taps, lanes, tokens).astype(BF16).T
    for j in range(fold):
        sums[0:modes, j * LANES : (j + 1) * LANES] = acc[pl.ds(j, modes, stride=fold), :]
    for move in moves:
        move.wait()


def state_streams(feat, og, filt, bias, tables, payloads, spans, plan, ring, w_proj):
    tokens, channels = og.shape
    fold = channels // LANES
    modes = (tables.shape[0] // fold - tokens) // 3
    return pl.pallas_call(
        functools.partial(state_kernel, spans, plan, ring),
        in_specs=[whole()] * (5 + len(payloads)) + [in_hbm()],
        out_specs=[whole()] * 4,
        out_shape=[
            pltpu.VMEM((2, channels, tokens), BF16),
            pltpu.VMEM((modes + 1, channels), F32),
            pltpu.VMEM(((tokens + 2) * fold, LANES), F32),
            pltpu.VMEM((w_proj.shape[1], len(plan) * channels), BF16),
        ],
        scratch_shapes=[pltpu.VMEM((modes * fold, LANES), F32), pltpu.VMEM((tokens * fold, LANES), F32)]
        + [pltpu.VMEM((tokens + 8, channels), F32)] * 2
        + [pltpu.SemaphoreType.DMA((len(plan),))],
        compiler_params=params(),
        cost_estimate=cost(4 << 30, 16 << 20),
        name="state_streams",
    )(feat, og, filt, bias, tables, *payloads, w_proj)


def product_kernel(plan, base, later, first, last, ring, w_proj, w, *refs):
    refs = list(refs)
    moves = []
    if later:
        sems = refs.pop()
        moves = fetches(later, ring, w_proj, refs.pop(), sems)
    elif last:
        sems = refs.pop()
        turned = refs.pop()
    out = refs.pop()
    before = None if first else refs.pop()
    for move in moves:
        move.start()
    x = jnp.concatenate([refs[n][h, p] for *_, parts in plan for n, h, p in parts], axis=0)
    columns = slice(base * (x.shape[0] // len(plan)), (base + len(plan)) * (x.shape[0] // len(plan)))
    features = w.shape[0]
    wide = min(512, features)
    for d in range(0, features, wide):
        rows = slice(d, d + wide)
        y = jnp.dot(w[rows, columns], x, preferred_element_type=F32)
        if not first:
            y = y + before[rows]
        if last:
            turned[:, rows] = y.T
            moves.append(pltpu.make_async_copy(
                turned.at[:, pl.ds(d, wide)], out.at[:, pl.ds(d, wide)], sems.at[d // wide]
            ))
            moves[-1].start()
        else:
            out[rows] = y
    for move in moves:
        move.wait()


def steps_of(pieces):
    arrays, plan = [], []
    for array, places, stream, offset in pieces:
        halves = array if isinstance(array, tuple) else (array,)
        for h in range(halves[0].shape[0]):
            for p in places:
                plan.append((stream + p, h, offset, [(len(arrays) + n, h, p) for n in range(len(halves))]))
        arrays += halves
    return arrays, plan


def add_product(total, ready, base, pieces, later, last, ring, w_proj, span):
    features = w_proj.shape[1]
    arrays, plan = steps_of(pieces)
    channels, tokens = w_proj.shape[2] // lax.axis_size("chan"), arrays[0].shape[3]
    first = total is None
    out_specs = [whole()]
    out_shape = [pltpu.VMEM((features, tokens), F32)]
    scratch = []
    if last:
        out_specs = [in_hbm()]
        out_shape = [jax.ShapeDtypeStruct((tokens, features), F32)]
        scratch = [pltpu.VMEM((tokens, features), F32), pltpu.SemaphoreType.DMA((max(1, features // 512),))]
    elif later:
        out_specs += [whole()]
        out_shape += [pltpu.VMEM((features, len(later) * channels), BF16)]
        scratch = [pltpu.SemaphoreType.DMA((len(later),))]
    return pl.pallas_call(
        functools.partial(product_kernel, plan, base, later, first, last, ring),
        in_specs=[in_hbm()]
        + [whole()] * (1 + len(arrays) + (not first)),
        out_specs=out_specs,
        out_shape=out_shape,
        scratch_shapes=scratch,
        compiler_params=params(),
        cost_estimate=cost(*span),
        name="add_product",
    )(w_proj, ready, *arrays, *([] if first else [total]))


def ring_order(size):
    return list(range(0, size, 2)) + list(range(size - 1 - size % 2, 0, -2))


def after(array, *others):
    return lax.optimization_barrier((array, *others))[0]


def body(features, saved_conv, out_grad, short_filter, residue, rate, bias, w_proj):
    tokens, channels = out_grad.shape
    modes = rate.shape[1]
    blocks = lax.axis_size("ctx")
    groups = lax.axis_size("chan")
    ring = min(groups, RING)
    heights = groups // ring

    order = ring_order(ring)
    pairs = {
        by: [
            (h * ring + order[i], h * ring + order[(i + by) % ring])
            for h in range(heights)
            for i in range(ring)
        ]
        for by in (1, -1)
    }

    def up(x):
        return lax.ppermute(x, "chan", pairs[1])

    def down(x):
        return lax.ppermute(x, "chan", pairs[-1])

    def stacked(block):
        if heights == 1:
            return block[None]
        groups = [[h * ring + i for h in range(heights)] for i in range(ring)]
        return lax.all_gather(block, "chan", axis_index_groups=groups)

    def from_later(array, by):
        return lax.ppermute(array, "ctx", [(i, i - by) for i in range(by, blocks)])

    def exchanged(sums, by):
        return sums + lax.ppermute(sums, "ctx", [(i, i ^ by) for i in range(blocks)])

    fold = channels // LANES
    feat, conv, og, filt, bias_row, tables, own, brief = front(
        features, saved_conv, out_grad, short_filter, residue.T, rate.T, bias[None]
    )
    payloads, spans = [from_later(own, 1)], [tokens]
    unit, window = 1, brief
    while unit < blocks:
        for by in range(len(payloads) % 3 + 1, 4):
            if by * unit < blocks:
                payloads.append(from_later(window, by * unit))
                spans.append(unit * tokens)
        unit *= 4
        if unit < blocks:
            near = [window, *payloads[-3:]]
            near[1] = near[1][: window.shape[0]]
            window = join(near, unit // 4 * tokens, tables, tokens, fold)
    gate = gate_stream(feat, conv, og, filt, bias_row, payloads[0])
    a0 = stacked(gate)
    a1, z1 = up(a0), down(a0)

    half = channels // 2
    back = ring // 2

    a, b = (0,), (0, 1)
    sets = [
        [("a0", a, 0, 0), ("b0", b, 1, 0)],
        [("a1", a, 0, ring - 1), ("z1", a, 0, 1)],
        [("b1", b, 1, ring - 1), ("y1", (0,), 1, 1)],
        [("y1", (1,), 1, 1), ("a2", a, 0, ring - 2), ("z2", a, 0, 2)],
        [("b2", b, 1, ring - 2), ("y2", (0,), 1, 2)],
        [("y2", (1,), 1, 2), ("a3", a, 0, ring - 3), ("z3", a, 0, 3)],
        [("b3", a, 1, ring - 3), ("y3", a, 2, 3), ("c3", a, 2, ring - 3), ("x3", a, 1, 3)],
        [("b4", a, 1, back), ("y4", a, 2, back)],
        [("a4", a, 0, back)],
    ]
    costs = [LONG, LONG, SHORT, LONG, SHORT, SHORT, SHORT, SHORT, SHORT]
    hollow = jax.ShapeDtypeStruct((heights, 2, channels, tokens), BF16)

    def plan_of(n):
        return steps_of([(hollow, *piece[1:]) for piece in sets[n]])[1]

    def times(n, total, ready, **arrays):
        pieces = [(arrays[name], *rest) for name, *rest in sets[n]]
        after_next = [plan_of(k) for k in range(7, len(sets))]
        later = plan_of(n + 1) if n < 6 else sum(after_next, []) if n == 6 else None
        base = sum(len(plan) for plan in after_next[: max(0, n - 7)])
        return add_product(total, ready, base, pieces, later, n == len(sets) - 1, ring, w_proj, costs[n])

    payloads[0], a0 = lax.optimization_barrier((payloads[0], a0))
    rounds, sums, gp, ready = state_streams(
        feat, og, filt, bias_row.reshape(fold, LANES), tables, payloads, spans, plan_of(0), ring, w_proj
    )
    b0 = stacked(rounds)

    b1, y1 = up(b0), down(b0)
    a1, z1, b0, sums = lax.optimization_barrier((a1, z1, b0, sums))
    a2, z2 = up(a1), down(z1)
    distances = [1 << n for n in range((blocks - 1).bit_length())]
    for by in distances[:1]:
        sums = exchanged(sums, by)
    total, ready = times(0, None, ready, a0=a0, b0=b0)
    total, ready = times(1, total, ready, a1=a1, z1=z1)

    b1, y1, total, sums = lax.optimization_barrier((b1, y1, total, sums))
    b2, y2 = up(b1), down(y1)
    total, ready = times(2, total, ready, b1=b1, y1=y1)

    a2, z2, total, sums = lax.optimization_barrier((a2, z2, total, sums))
    a3, z3 = up(a2), down(z2)
    for by in distances[1:]:
        sums = exchanged(sums, by)
    total, ready = times(3, total, ready, y1=y1, a2=a2, z2=z2)
    grads = gradients(features, saved_conv, out_grad, short_filter, bias[None], payloads[0], after(gp, total))

    b2, y2, total, sums, grads = lax.optimization_barrier((b2, y2, total, sums, grads))
    b3, y3 = up(b2[:, :1]), down(y2[:, 1:])
    c3 = up(b2[:, 1:])
    total, ready = times(4, total, ready, b2=b2, y2=y2)
    x3 = down(after(y2[:, :1], total))
    a3, z3, total = lax.optimization_barrier((a3, z3, total))
    total, ready = times(5, total, ready, y2=y2, a3=a3, z3=z3)

    b3, y3, total, sums = lax.optimization_barrier((b3, y3, total, sums))
    b4, y4 = up(b3), down(y3)
    a4 = up(a3[:, :, :half]), down(z3[:, :, half:])
    sums = sums * (tokens * blocks) ** (-0.5)
    total, ready = times(6, total, ready, b3=b3, y3=y3, c3=c3, x3=x3)

    b4, y4, total, sums = lax.optimization_barrier((b4, y4, total, sums))
    (total,) = times(7, total, ready, b4=b4, y4=y4)
    grad_residue, grad_bias = sums[:modes].T, sums[modes]
    a4, total, grad_residue, grad_bias = lax.optimization_barrier((a4, total, grad_residue, grad_bias))
    (grad_x,) = times(8, total, ready, a4=a4)
    return (grads, grad_x, grad_residue, grad_bias)


def solution(mesh):
    return jax.shard_map(
        body,
        mesh=mesh,
        in_specs=(
            P(None, "ctx", "chan"),
            P("ctx", "chan"),
            P("ctx", "chan"),
            P(None, None, "chan"),
            P("chan", None),
            P("chan", None),
            P("chan"),
            P(None, "chan", None),
        ),
        out_specs=(P(None, "ctx", "chan"), P("ctx", "chan"), P("chan", None), P("chan")),
        check_vma=False,
    )
```

```python
import functools

import jax
import jax.numpy as jnp
from jax import lax
from jax.experimental import pallas as pl
from jax.experimental.pallas import tpu as pltpu
from jax.sharding import PartitionSpec as P

LANES = 128
RING = 8
LONG = 1 << 36, 1 << 28
SHORT = 1 << 16, 1 << 8
MIDDLE = 1 << 30, 9 << 20
TAIL = 7 << 28, 13 << 20
VMEM = 8 * 1024 * 1024
F32 = jnp.float32
BF16 = jnp.bfloat16


def whole():
    return pl.BlockSpec(memory_space=pltpu.VMEM)


def in_hbm():
    return pl.BlockSpec(memory_space=pltpu.HBM)


def params():
    return pltpu.CompilerParams(vmem_limit_bytes=VMEM)


def cost(flops, size):
    return pl.CostEstimate(flops=flops, bytes_accessed=size, transcendentals=0)


def by_row(values, out, fold, base=0):
    for j in range(fold):
        out[pl.ds(base * fold + j, values.shape[0], stride=fold), :] = values[:, j * LANES : (j + 1) * LANES]


def front_kernel(features, saved_conv, out_grad, short_filter, residue, rate, bias, *refs):
    feat, conv, og, filt, bias_in, tables, own, brief, res_in, rate_in, sems = refs
    tokens, channels = og.shape
    modes = rate_in.shape[0]
    fold = channels // LANES
    moves = [
        pltpu.make_async_copy(source, target, sems.at[n])
        for n, (source, target) in enumerate((
            (rate, rate_in),
            (out_grad, og),
            (features.at[0], feat.at[0]),
            (features.at[pl.ds(1, 2)], feat.at[pl.ds(1, 2)]),
            (saved_conv, conv),
            (short_filter, filt),
            (residue, res_in),
            (bias, bias_in),
        ))
    ]
    for move in moves:
        move.start()
    moves[0].wait()
    by_row(jnp.exp(-rate_in[...]), tables, fold, tokens)
    by_row(rate_in[...], tables, fold, tokens + modes)
    moves[1].wait()
    moves[2].wait()
    for j in range(fold):
        lanes = slice(j * LANES, (j + 1) * LANES)
        tables[pl.ds(j, tokens, stride=fold), :] = og[:, lanes] * feat[0, :, lanes]
    decay = [tables[(tokens + m) * fold : (tokens + m + 1) * fold, :] for m in range(modes)]

    def step(i, states):
        row = tables[pl.ds((tokens - 1 - i) * fold, fold), :]
        return tuple(row + d * s for d, s in zip(decay, states))

    zero = tuple(jnp.zeros((fold, LANES), F32) for _ in range(modes))
    states = lax.fori_loop(0, tokens - 2, step, zero, unroll=6)
    for target in (own, brief):
        for m in range(modes):
            target[m * fold : (m + 1) * fold, :] = states[m]
        target[modes * fold : (modes + 2) * fold, :] = tables[0 : 2 * fold, :]
    for n in range(3, 8):
        moves[n].wait()
    for n in range(3):
        by_row(feat[n, 0:2, :], own, fold, modes + 2 + 2 * n)
    by_row(conv[0:2, :], own, fold, modes + 8)
    by_row(og[0:2, :], own, fold, modes + 10)
    by_row(res_in[...], tables, fold, tokens + 2 * modes)


def front(features, saved_conv, out_grad, short_filter, residue, rate, bias):
    tokens, channels = out_grad.shape
    modes = rate.shape[0]
    fold = channels // LANES
    inputs = (features, saved_conv, out_grad, short_filter, residue, rate, bias)
    return pl.pallas_call(
        front_kernel,
        in_specs=[in_hbm()] * 7,
        out_specs=[whole()] * 8,
        out_shape=[pltpu.VMEM(a.shape, F32) for a in (*inputs[:4], bias)]
        + [pltpu.VMEM((n * fold, LANES), F32) for n in (tokens + 3 * modes, modes + 12, modes + 2)],
        scratch_shapes=[pltpu.VMEM(rate.shape, F32)] * 2 + [pltpu.SemaphoreType.DMA((8,))],
        compiler_params=params(),
        cost_estimate=cost(4 * tokens * channels * modes, 20 * tokens * channels),
        name="front",
    )(*(pltpu.with_memory_space_constraint(a, pltpu.HBM) for a in inputs))


def tapped(ext, taps, lanes, tokens):
    total = taps[0][:, lanes] * ext[0:tokens, lanes]
    total = total + taps[1][:, lanes] * ext[1 : tokens + 1, lanes]
    return total + taps[2][:, lanes] * ext[2 : tokens + 2, lanes]


def rim_rows(later, which, j, fold):
    modes = later.shape[0] // fold - 12
    return later[pl.ds((modes + 2 + 2 * which) * fold + j, 2, stride=fold), :]


def gate_gradient(feat, conv, og, bias, later, ext):
    tokens, channels = og.shape
    fold = channels // LANES
    for j in range(fold):
        lanes = slice(j * LANES, (j + 1) * LANES)
        product = feat[1, :, lanes] * feat[2, :, lanes]
        ext[0:tokens, lanes] = og[:, lanes] * (conv[:, lanes] + bias[:, lanes] * product)
        key, value, held, cotangent = (rim_rows(later, n, j, fold) for n in (1, 2, 3, 4))
        ext[tokens : tokens + 2, lanes] = cotangent * (held + bias[:, lanes] * (key * value))


def carried(own, m, later, state, decay, rate, span, fold):
    modes = own.shape[0] // fold - 2
    s0, s1 = (later[(modes + n) * fold : (modes + n + 1) * fold, :] for n in (0, 1))
    return own[m * fold : (m + 1) * fold, :] + jnp.exp(-(span - 2) * rate) * (s0 + decay * (s1 + decay * state))


def all_carried(summaries, spans, m, tables, tokens, fold):
    modes = summaries[0].shape[0] // fold - 2
    decay, rate = (tables[(tokens + n * modes + m) * fold : (tokens + n * modes + m + 1) * fold, :] for n in (0, 1))
    state = summaries[-1][m * fold : (m + 1) * fold, :]
    for own, later, span in reversed(list(zip(summaries, summaries[1:], spans))):
        state = carried(own, m, later, state, decay, rate, span, fold)
    return state


def join(summaries, span, tables, tokens, fold):
    def kernel(tables, *refs):
        *refs, out = refs
        modes = out.shape[0] // fold - 2
        for m in range(modes):
            out[m * fold : (m + 1) * fold, :] = all_carried(refs, [span] * (len(refs) - 1), m, tables, tokens, fold)
        out[modes * fold : (modes + 2) * fold, :] = refs[0][modes * fold : (modes + 2) * fold, :]

    return pl.pallas_call(
        kernel,
        in_specs=[whole()] * (1 + len(summaries)),
        out_specs=whole(),
        out_shape=pltpu.VMEM(summaries[0].shape, F32),
        compiler_params=params(),
        name="join",
    )(tables, *summaries)


def gate_kernel(feat, conv, og, filt, bias, later, rounded, ext):
    tokens, channels = og.shape
    taps = [filt[0, j : j + 1, :] for j in range(3)]
    gate_gradient(feat, conv, og, bias, later, ext)
    for j in range(channels // LANES):
        lanes = slice(j * LANES, (j + 1) * LANES)
        rounded[0, lanes, :] = tapped(ext, taps, lanes, tokens).astype(BF16).T


def gate_stream(feat, conv, og, filt, bias, later):
    tokens, channels = og.shape
    return pl.pallas_call(
        gate_kernel,
        in_specs=[whole()] * 6,
        out_specs=whole(),
        out_shape=pltpu.VMEM((1, channels, tokens), BF16),
        scratch_shapes=[pltpu.VMEM((tokens + 8, channels), F32)],
        compiler_params=params(),
        cost_estimate=cost(*LONG),
        name="gate_stream",
    )(feat, conv, og, filt, bias, later)


def product_gradients(feat, gp, later, exts):
    tokens, channels = feat.shape[1:]
    fold = channels // LANES
    for j in range(fold):
        lanes = slice(j * LANES, (j + 1) * LANES)
        g = gp[pl.ds(j, tokens, stride=fold), :]
        rim = gp[pl.ds(tokens * fold + j, 2, stride=fold), :]
        for ext, n in zip(exts, (2, 1)):
            ext[0:tokens, lanes] = g * feat[n, :, lanes]
            ext[tokens : tokens + 2, lanes] = rim * rim_rows(later, n, j, fold)


def gradients_kernel(feat, conv, og, filt, bias, later, gp, out, first, second, third, ready, sems):
    tokens, channels = og.shape
    gate_gradient(feat, conv, og, bias, later, first)
    product_gradients(feat, gp, later, (second, third))
    moves = []
    for p, ext in enumerate((first, second, third)):
        taps = [filt[p, j : j + 1, :] for j in range(3)]
        for j in range(channels // LANES):
            lanes = slice(j * LANES, (j + 1) * LANES)
            ready[p, :, lanes] = tapped(ext, taps, lanes, tokens)
        moves.append(pltpu.make_async_copy(ready.at[p], out.at[p], sems.at[p]))
        moves[-1].start()
    for move in moves:
        move.wait()


def gradients(feat, conv, og, filt, bias, later, gp):
    tokens, channels = og.shape
    return pl.pallas_call(
        gradients_kernel,
        in_specs=[whole()] * 7,
        out_specs=in_hbm(),
        out_shape=jax.ShapeDtypeStruct((3, tokens, channels), F32),
        scratch_shapes=[pltpu.VMEM((tokens + 8, channels), F32)] * 3
        + [pltpu.VMEM((3, tokens, channels), F32), pltpu.SemaphoreType.DMA((3,))],
        compiler_params=params(),
        cost_estimate=cost(30 * tokens * channels, 40 * tokens * channels),
        name="gradients",
    )(feat, conv, og, filt, bias, later, gp)


def on_ring(offset, ring):
    own = lax.rem(lax.axis_index("chan"), ring)
    place = jnp.where(lax.rem(own, 2) == 0, own // 2, ring - 1 - own // 2)
    place = lax.rem(place + offset, ring)
    return jnp.where(place < (ring + 1) // 2, 2 * place, 2 * (ring - 1 - place) + 1)


def fetches(plan, ring, w_proj, ready, sems):
    channels = ready.shape[1] // len(plan)
    moves = []
    for k, (stream, height, offset, _) in enumerate(plan):
        begin = pl.multiple_of((height * ring + on_ring(offset, ring)) * channels, LANES)
        columns = w_proj.at[stream, :, pl.ds(begin, channels)]
        moves.append(pltpu.make_async_copy(columns, ready.at[:, pl.ds(k * channels, channels)], sems.at[k]))
    return moves


def state_kernel(spans, plan, ring, feat, og, filt, bias, tables, *refs):
    later = len(spans)
    payloads = refs[:later]
    w_proj, rounded, sums, gp, ready, acc, prod, first_ext, second_ext, sems = refs[later:]
    exts = first_ext, second_ext
    moves = fetches(plan, ring, w_proj, ready, sems)
    for move in moves:
        move.start()
    tokens, channels = og.shape
    fold = channels // LANES
    modes = (tables.shape[0] // fold - tokens) // 3
    dec, res = tokens, tokens + 2 * modes
    briefs = [payloads[0].at[pl.ds(0, (modes + 2) * fold)], *payloads[1:]]
    for j in range(fold):
        lanes = slice(j * LANES, (j + 1) * LANES)
        p = feat[1, :, lanes] * feat[2, :, lanes]
        prod[pl.ds(j, tokens, stride=fold), :] = p
        s = og[:, lanes] * feat[0, :, lanes]
        sums[modes : modes + 1, lanes] = jnp.sum(s * p, axis=0, keepdims=True)

    def rows(ref, at):
        return ref[at * fold : (at + 1) * fold, :]

    direct = bias[...]
    group = 8
    for low in range(0, modes, group):
        chosen = range(low, min(low + group, modes))
        decay, weight = ([rows(tables, at + m) for m in chosen] for at in (dec, res))
        state = [all_carried(briefs, spans, m, tables, tokens, fold) for m in chosen]

        def corr(state, weight=weight):
            terms = [w * s for w, s in zip(weight, state)]
            while len(terms) > 1:
                terms = [a + b for a, b in zip(terms[::2], terms[1::2])] + terms[len(terms) // 2 * 2 :]
            return terms[0]

        def put(at, row, state, low=low, corr=corr):
            here = pl.ds(at * fold, fold)
            if low == 0:
                gp[here, :] = corr(state) + direct * row
            else:
                gp[here, :] = gp[here, :] + corr(state)

        for n in (1, 0):
            row = rows(payloads[0], modes + n)
            state = [row + d * s for d, s in zip(decay, state)]
            put(tokens + n, row, state)

        def step(i, carry, decay=decay, put=put):
            state, total = carry
            at = tokens - 1 - i
            row = tables[pl.ds(at * fold, fold), :]
            other = prod[pl.ds(at * fold, fold), :]
            state = [row + d * s for d, s in zip(decay, state)]
            total = [a + other * s for a, s in zip(total, state)]
            put(at, row, state)
            return state, total

        zero = [jnp.zeros((fold, LANES), F32) for _ in chosen]
        state, total = lax.fori_loop(0, tokens, step, (state, zero), unroll=4)
        for m, a in zip(chosen, total):
            acc[m * fold : (m + 1) * fold, :] = a

    product_gradients(feat, gp, payloads[0], exts)
    for p, ext in enumerate(exts):
        taps = [filt[p + 1, j : j + 1, :] for j in range(3)]
        for j in range(fold):
            lanes = slice(j * LANES, (j + 1) * LANES)
            rounded[p, lanes, :] = tapped(ext, taps, lanes, tokens).astype(BF16).T
    for j in range(fold):
        sums[0:modes, j * LANES : (j + 1) * LANES] = acc[pl.ds(j, modes, stride=fold), :]
    for move in moves:
        move.wait()


def state_streams(feat, og, filt, bias, tables, payloads, spans, plan, ring, w_proj):
    tokens, channels = og.shape
    fold = channels // LANES
    modes = (tables.shape[0] // fold - tokens) // 3
    return pl.pallas_call(
        functools.partial(state_kernel, spans, plan, ring),
        in_specs=[whole()] * (5 + len(payloads)) + [in_hbm()],
        out_specs=[whole()] * 4,
        out_shape=[
            pltpu.VMEM((2, channels, tokens), BF16),
            pltpu.VMEM((modes + 1, channels), F32),
            pltpu.VMEM(((tokens + 2) * fold, LANES), F32),
            pltpu.VMEM((w_proj.shape[1], len(plan) * channels), BF16),
        ],
        scratch_shapes=[pltpu.VMEM((modes * fold, LANES), F32), pltpu.VMEM((tokens * fold, LANES), F32)]
        + [pltpu.VMEM((tokens + 8, channels), F32)] * 2
        + [pltpu.SemaphoreType.DMA((len(plan),))],
        compiler_params=params(),
        cost_estimate=cost(4 << 30, 16 << 20),
        name="state_streams",
    )(feat, og, filt, bias, tables, *payloads, w_proj)


def product_kernel(plan, base, later, first, last, ring, w_proj, w, *refs):
    refs = list(refs)
    moves = []
    if later:
        sems = refs.pop()
        moves = fetches(later, ring, w_proj, refs.pop(), sems)
    elif last:
        sems = refs.pop()
        turned = refs.pop()
    out = refs.pop()
    before = None if first else refs.pop()
    for move in moves:
        move.start()
    x = jnp.concatenate([refs[n][h, p] for *_, parts in plan for n, h, p in parts], axis=0)
    columns = slice(base * (x.shape[0] // len(plan)), (base + len(plan)) * (x.shape[0] // len(plan)))
    features = w.shape[0]
    wide = min(256, features)
    for d in range(0, features, wide):
        rows = slice(d, d + wide)
        y = jnp.dot(w[rows, columns], x, preferred_element_type=F32)
        if not first:
            y = y + before[rows]
        if last:
            turned[:, rows] = y.T
            moves.append(pltpu.make_async_copy(
                turned.at[:, pl.ds(d, wide)], out.at[:, pl.ds(d, wide)], sems.at[d // wide]
            ))
            moves[-1].start()
        else:
            out[rows] = y
    for move in moves:
        move.wait()


def steps_of(pieces):
    arrays, plan = [], []
    for array, places, stream, offset in pieces:
        halves = array if isinstance(array, tuple) else (array,)
        for h in range(halves[0].shape[0]):
            for p in places:
                plan.append((stream + p, h, offset, [(len(arrays) + n, h, p) for n in range(len(halves))]))
        arrays += halves
    return arrays, plan


def add_product(total, ready, base, pieces, later, last, ring, w_proj, span):
    features = w_proj.shape[1]
    arrays, plan = steps_of(pieces)
    channels, tokens = w_proj.shape[2] // lax.axis_size("chan"), arrays[0].shape[3]
    first = total is None
    out_specs = [whole()]
    out_shape = [pltpu.VMEM((features, tokens), F32)]
    scratch = []
    if last:
        out_specs = [in_hbm()]
        out_shape = [jax.ShapeDtypeStruct((tokens, features), F32)]
        scratch = [pltpu.VMEM((tokens, features), F32), pltpu.SemaphoreType.DMA((max(1, features // 256),))]
    elif later:
        out_specs += [whole()]
        out_shape += [pltpu.VMEM((features, len(later) * channels), BF16)]
        scratch = [pltpu.SemaphoreType.DMA((len(later),))]
    return pl.pallas_call(
        functools.partial(product_kernel, plan, base, later, first, last, ring),
        in_specs=[in_hbm()]
        + [whole()] * (1 + len(arrays) + (not first)),
        out_specs=out_specs,
        out_shape=out_shape,
        scratch_shapes=scratch,
        compiler_params=params(),
        cost_estimate=cost(*span),
        name="add_product",
    )(w_proj, ready, *arrays, *([] if first else [total]))


def ring_order(size):
    return list(range(0, size, 2)) + list(range(size - 1 - size % 2, 0, -2))


def after(array, *others):
    return lax.optimization_barrier((array, *others))[0]


def body(features, saved_conv, out_grad, short_filter, residue, rate, bias, w_proj):
    tokens, channels = out_grad.shape
    modes = rate.shape[1]
    blocks = lax.axis_size("ctx")
    groups = lax.axis_size("chan")
    ring = min(groups, RING)
    heights = groups // ring

    order = ring_order(ring)
    pairs = {
        by: [
            (h * ring + order[i], h * ring + order[(i + by) % ring])
            for h in range(heights)
            for i in range(ring)
        ]
        for by in (1, -1)
    }

    def up(x):
        return lax.ppermute(x, "chan", pairs[1])

    def down(x):
        return lax.ppermute(x, "chan", pairs[-1])

    def stacked(block):
        if heights == 1:
            return block[None]
        groups = [[h * ring + i for h in range(heights)] for i in range(ring)]
        return lax.all_gather(block, "chan", axis_index_groups=groups)

    def from_later(array, by):
        return lax.ppermute(array, "ctx", [(i, i - by) for i in range(by, blocks)])

    def exchanged(sums, by):
        return sums + lax.ppermute(sums, "ctx", [(i, i ^ by) for i in range(blocks)])

    fold = channels // LANES
    feat, conv, og, filt, bias_row, tables, own, brief = front(
        features, saved_conv, out_grad, short_filter, residue.T, rate.T, bias[None]
    )
    payloads, spans = [from_later(own, 1)], [tokens]
    unit, window = 1, brief
    while unit < blocks:
        for by in range(len(payloads) % 3 + 1, 4):
            if by * unit < blocks:
                payloads.append(from_later(window, by * unit))
                spans.append(unit * tokens)
        unit *= 4
        if unit < blocks:
            near = [window, *payloads[-3:]]
            near[1] = near[1][: window.shape[0]]
            window = join(near, unit // 4 * tokens, tables, tokens, fold)
    gate = gate_stream(feat, conv, og, filt, bias_row, payloads[0])
    a0 = stacked(gate)
    a1, z1 = up(a0), down(a0)

    half = channels // 2
    back = ring // 2

    a, b = (0,), (0, 1)
    sets = [
        [("a0", a, 0, 0), ("b0", b, 1, 0)],
        [("a1", a, 0, ring - 1), ("z1", a, 0, 1)],
        [("b1", b, 1, ring - 1), ("y1", (0,), 1, 1)],
        [("y1", (1,), 1, 1), ("a2", a, 0, ring - 2), ("z2", a, 0, 2)],
        [("b2", b, 1, ring - 2), ("y2", (0,), 1, 2)],
        [("y2", (1,), 1, 2), ("a3", a, 0, ring - 3), ("z3", a, 0, 3)],
        [("b3", b, 1, ring - 3), ("y3", b, 1, 3)],
        [("a4", a, 0, back)],
        [("b4", a, 1, back)],
        [("y4", a, 2, back)],
    ]
    costs = [LONG, LONG, SHORT, LONG, SHORT, LONG, MIDDLE, TAIL, SHORT, SHORT]
    hollow = jax.ShapeDtypeStruct((heights, 2, channels, tokens), BF16)

    def plan_of(n):
        return steps_of([(hollow, *piece[1:]) for piece in sets[n]])[1]

    def times(n, total, ready, **arrays):
        pieces = [(arrays[name], *rest) for name, *rest in sets[n]]
        after_next = [plan_of(k) for k in range(7, len(sets))]
        later = plan_of(n + 1) if n < 6 else sum(after_next, []) if n == 6 else None
        base = sum(len(plan) for plan in after_next[: max(0, n - 7)])
        return add_product(total, ready, base, pieces, later, n == len(sets) - 1, ring, w_proj, costs[n])

    payloads[0], a0 = lax.optimization_barrier((payloads[0], a0))
    rounds, sums, gp, ready = state_streams(
        feat, og, filt, bias_row.reshape(fold, LANES), tables, payloads, spans, plan_of(0), ring, w_proj
    )
    b0 = stacked(rounds)

    b1, y1 = up(b0), down(b0)
    a1, z1, b0, sums = lax.optimization_barrier((a1, z1, b0, sums))
    a2, z2 = up(a1), down(z1)
    distances = [1 << n for n in range((blocks - 1).bit_length())]
    for by in distances[:1]:
        sums = exchanged(sums, by)
    total, ready = times(0, None, ready, a0=a0, b0=b0)
    total, ready = times(1, total, ready, a1=a1, z1=z1)
    b1, y1, total, sums = lax.optimization_barrier((b1, y1, total, sums))
    b2, y2 = up(b1), down(y1)
    total, ready = times(2, total, ready, b1=b1, y1=y1)

    a2, z2, total, sums = lax.optimization_barrier((a2, z2, total, sums))
    a3, z3 = up(a2), down(z2)
    for by in distances[1:]:
        sums = exchanged(sums, by)
    total, ready = times(3, total, ready, y1=y1, a2=a2, z2=z2)
    grads = gradients(features, saved_conv, out_grad, short_filter, bias[None], payloads[0], after(gp, total))

    b2, y2, total, sums, grads = lax.optimization_barrier((b2, y2, total, sums, grads))
    b3, y3 = up(b2), down(y2)
    total, ready = times(4, total, ready, b2=b2, y2=y2)

    a3, z3, total = lax.optimization_barrier((a3, z3, total))
    a4 = up(a3[:, :, :half]), down(z3[:, :, half:])
    total, ready = times(5, total, ready, y2=y2, a3=a3, z3=z3)

    b3, y3, total, sums = lax.optimization_barrier((b3, y3, total, sums))
    b4, y4 = up(b3[:, :1]), down(y3[:, 1:])
    total, ready = times(6, total, ready, b3=b3, y3=y3)

    a4, total, sums = lax.optimization_barrier((a4, total, sums))
    (total,) = times(7, total, ready, a4=a4)
    sums = sums * (tokens * blocks) ** (-0.5)
    grad_residue, grad_bias = sums[:modes].T, sums[modes]
    b4, total, grad_residue, grad_bias = lax.optimization_barrier((b4, total, grad_residue, grad_bias))
    (total,) = times(8, total, ready, b4=b4)
    (grad_x,) = times(9, total, ready, y4=y4)
    return (grads, grad_x, grad_residue, grad_bias)


def solution(mesh):
    return jax.shard_map(
        body,
        mesh=mesh,
        in_specs=(
            P(None, "ctx", "chan"),
            P("ctx", "chan"),
            P("ctx", "chan"),
            P(None, None, "chan"),
            P("chan", None),
            P("chan", None),
            P("chan"),
            P(None, "chan", None),
        ),
        out_specs=(P(None, "ctx", "chan"), P("ctx", "chan"), P("chan", None), P("chan")),
        check_vma=False,
    )
```

```python
import functools

import jax
import jax.numpy as jnp
from jax import lax
from jax.experimental import pallas as pl
from jax.experimental.pallas import tpu as pltpu
from jax.sharding import PartitionSpec as P

LANES = 128
RING = 8
LONG = 1 << 36, 1 << 28
SHORT = 1 << 16, 1 << 8
MIDDLE = 1 << 30, 9 << 20
TAIL = 7 << 28, 13 << 20
VMEM = 8 * 1024 * 1024
F32 = jnp.float32
BF16 = jnp.bfloat16


def whole():
    return pl.BlockSpec(memory_space=pltpu.VMEM)


def in_hbm():
    return pl.BlockSpec(memory_space=pltpu.HBM)


def params():
    return pltpu.CompilerParams(vmem_limit_bytes=VMEM)


def cost(flops, size):
    return pl.CostEstimate(flops=flops, bytes_accessed=size, transcendentals=0)


def by_row(values, out, fold, base=0):
    for j in range(fold):
        out[pl.ds(base * fold + j, values.shape[0], stride=fold), :] = values[:, j * LANES : (j + 1) * LANES]


def front_kernel(features, saved_conv, out_grad, short_filter, residue, rate, bias, *refs):
    feat, conv, og, filt, bias_in, tables, own, brief, res_in, rate_in, sems = refs
    tokens, channels = og.shape
    modes = rate_in.shape[0]
    fold = channels // LANES
    moves = [
        pltpu.make_async_copy(source, target, sems.at[n])
        for n, (source, target) in enumerate((
            (rate, rate_in),
            (out_grad, og),
            (features.at[0], feat.at[0]),
            (features.at[pl.ds(1, 2)], feat.at[pl.ds(1, 2)]),
            (saved_conv, conv),
            (short_filter, filt),
            (residue, res_in),
            (bias, bias_in),
        ))
    ]
    for move in moves:
        move.start()
    moves[0].wait()
    by_row(jnp.exp(-rate_in[...]), tables, fold, tokens)
    by_row(rate_in[...], tables, fold, tokens + modes)
    moves[1].wait()
    moves[2].wait()
    for j in range(fold):
        lanes = slice(j * LANES, (j + 1) * LANES)
        tables[pl.ds(j, tokens, stride=fold), :] = og[:, lanes] * feat[0, :, lanes]
    decay = [tables[(tokens + m) * fold : (tokens + m + 1) * fold, :] for m in range(modes)]

    def step(i, states):
        row = tables[pl.ds((tokens - 1 - i) * fold, fold), :]
        return tuple(row + d * s for d, s in zip(decay, states))

    zero = tuple(jnp.zeros((fold, LANES), F32) for _ in range(modes))
    states = lax.fori_loop(0, tokens - 2, step, zero, unroll=6)
    for target in (own, brief):
        for m in range(modes):
            target[m * fold : (m + 1) * fold, :] = states[m]
        target[modes * fold : (modes + 2) * fold, :] = tables[0 : 2 * fold, :]
    for n in range(3, 8):
        moves[n].wait()
    for n in range(3):
        by_row(feat[n, 0:2, :], own, fold, modes + 2 + 2 * n)
    by_row(conv[0:2, :], own, fold, modes + 8)
    by_row(og[0:2, :], own, fold, modes + 10)
    by_row(res_in[...], tables, fold, tokens + 2 * modes)


def front(features, saved_conv, out_grad, short_filter, residue, rate, bias):
    tokens, channels = out_grad.shape
    modes = rate.shape[0]
    fold = channels // LANES
    inputs = (features, saved_conv, out_grad, short_filter, residue, rate, bias)
    return pl.pallas_call(
        front_kernel,
        in_specs=[in_hbm()] * 7,
        out_specs=[whole()] * 8,
        out_shape=[pltpu.VMEM(a.shape, F32) for a in (*inputs[:4], bias)]
        + [pltpu.VMEM((n * fold, LANES), F32) for n in (tokens + 3 * modes, modes + 12, modes + 2)],
        scratch_shapes=[pltpu.VMEM(rate.shape, F32)] * 2 + [pltpu.SemaphoreType.DMA((8,))],
        compiler_params=params(),
        cost_estimate=cost(4 * tokens * channels * modes, 20 * tokens * channels),
        name="front",
    )(*(pltpu.with_memory_space_constraint(a, pltpu.HBM) for a in inputs))


def tapped(ext, taps, lanes, tokens):
    total = taps[0][:, lanes] * ext[0:tokens, lanes]
    total = total + taps[1][:, lanes] * ext[1 : tokens + 1, lanes]
    return total + taps[2][:, lanes] * ext[2 : tokens + 2, lanes]


def rim_rows(later, which, j, fold):
    modes = later.shape[0] // fold - 12
    return later[pl.ds((modes + 2 + 2 * which) * fold + j, 2, stride=fold), :]


def gate_gradient(feat, conv, og, bias, later, ext):
    tokens, channels = og.shape
    fold = channels // LANES
    for j in range(fold):
        lanes = slice(j * LANES, (j + 1) * LANES)
        product = feat[1, :, lanes] * feat[2, :, lanes]
        ext[0:tokens, lanes] = og[:, lanes] * (conv[:, lanes] + bias[:, lanes] * product)
        key, value, held, cotangent = (rim_rows(later, n, j, fold) for n in (1, 2, 3, 4))
        ext[tokens : tokens + 2, lanes] = cotangent * (held + bias[:, lanes] * (key * value))


def carried(own, m, later, state, decay, rate, span, fold):
    modes = own.shape[0] // fold - 2
    s0, s1 = (later[(modes + n) * fold : (modes + n + 1) * fold, :] for n in (0, 1))
    return own[m * fold : (m + 1) * fold, :] + jnp.exp(-(span - 2) * rate) * (s0 + decay * (s1 + decay * state))


def all_carried(summaries, spans, m, tables, tokens, fold):
    modes = summaries[0].shape[0] // fold - 2
    decay, rate = (tables[(tokens + n * modes + m) * fold : (tokens + n * modes + m + 1) * fold, :] for n in (0, 1))
    state = summaries[-1][m * fold : (m + 1) * fold, :]
    for own, later, span in reversed(list(zip(summaries, summaries[1:], spans))):
        state = carried(own, m, later, state, decay, rate, span, fold)
    return state


def join(summaries, span, tables, tokens, fold):
    def kernel(tables, *refs):
        *refs, out = refs
        modes = out.shape[0] // fold - 2
        for m in range(modes):
            out[m * fold : (m + 1) * fold, :] = all_carried(refs, [span] * (len(refs) - 1), m, tables, tokens, fold)
        out[modes * fold : (modes + 2) * fold, :] = refs[0][modes * fold : (modes + 2) * fold, :]

    return pl.pallas_call(
        kernel,
        in_specs=[whole()] * (1 + len(summaries)),
        out_specs=whole(),
        out_shape=pltpu.VMEM(summaries[0].shape, F32),
        compiler_params=params(),
        name="join",
    )(tables, *summaries)


def gate_kernel(feat, conv, og, filt, bias, later, rounded, ext):
    tokens, channels = og.shape
    taps = [filt[0, j : j + 1, :] for j in range(3)]
    gate_gradient(feat, conv, og, bias, later, ext)
    for j in range(channels // LANES):
        lanes = slice(j * LANES, (j + 1) * LANES)
        rounded[0, lanes, :] = tapped(ext, taps, lanes, tokens).astype(BF16).T


def gate_stream(feat, conv, og, filt, bias, later):
    tokens, channels = og.shape
    return pl.pallas_call(
        gate_kernel,
        in_specs=[whole()] * 6,
        out_specs=whole(),
        out_shape=pltpu.VMEM((1, channels, tokens), BF16),
        scratch_shapes=[pltpu.VMEM((tokens + 8, channels), F32)],
        compiler_params=params(),
        cost_estimate=cost(*LONG),
        name="gate_stream",
    )(feat, conv, og, filt, bias, later)


def product_gradients(feat, gp, later, exts):
    tokens, channels = feat.shape[1:]
    fold = channels // LANES
    for j in range(fold):
        lanes = slice(j * LANES, (j + 1) * LANES)
        g = gp[pl.ds(j, tokens, stride=fold), :]
        rim = gp[pl.ds(tokens * fold + j, 2, stride=fold), :]
        for ext, n in zip(exts, (2, 1)):
            ext[0:tokens, lanes] = g * feat[n, :, lanes]
            ext[tokens : tokens + 2, lanes] = rim * rim_rows(later, n, j, fold)


def gradients_kernel(feat, conv, og, filt, bias, later, gp, out, first, second, third, ready, sems):
    tokens, channels = og.shape
    gate_gradient(feat, conv, og, bias, later, first)
    product_gradients(feat, gp, later, (second, third))
    moves = []
    for p, ext in enumerate((first, second, third)):
        taps = [filt[p, j : j + 1, :] for j in range(3)]
        for j in range(channels // LANES):
            lanes = slice(j * LANES, (j + 1) * LANES)
            ready[p, :, lanes] = tapped(ext, taps, lanes, tokens)
        moves.append(pltpu.make_async_copy(ready.at[p], out.at[p], sems.at[p]))
        moves[-1].start()
    for move in moves:
        move.wait()


def gradients(feat, conv, og, filt, bias, later, gp):
    tokens, channels = og.shape
    return pl.pallas_call(
        gradients_kernel,
        in_specs=[whole()] * 7,
        out_specs=in_hbm(),
        out_shape=jax.ShapeDtypeStruct((3, tokens, channels), F32),
        scratch_shapes=[pltpu.VMEM((tokens + 8, channels), F32)] * 3
        + [pltpu.VMEM((3, tokens, channels), F32), pltpu.SemaphoreType.DMA((3,))],
        compiler_params=params(),
        cost_estimate=cost(30 * tokens * channels, 40 * tokens * channels),
        name="gradients",
    )(feat, conv, og, filt, bias, later, gp)


def on_ring(offset, ring):
    own = lax.rem(lax.axis_index("chan"), ring)
    place = jnp.where(lax.rem(own, 2) == 0, own // 2, ring - 1 - own // 2)
    place = lax.rem(place + offset, ring)
    return jnp.where(place < (ring + 1) // 2, 2 * place, 2 * (ring - 1 - place) + 1)


def fetches(plan, ring, w_proj, ready, sems):
    channels = ready.shape[1] // len(plan)
    moves = []
    for k, (stream, height, offset, _) in enumerate(plan):
        begin = pl.multiple_of((height * ring + on_ring(offset, ring)) * channels, LANES)
        columns = w_proj.at[stream, :, pl.ds(begin, channels)]
        moves.append(pltpu.make_async_copy(columns, ready.at[:, pl.ds(k * channels, channels)], sems.at[k]))
    return moves


def state_kernel(spans, plan, ring, feat, og, filt, bias, tables, *refs):
    later = len(spans)
    payloads = refs[:later]
    w_proj, rounded, sums, gp, ready, acc, prod, first_ext, second_ext, sems = refs[later:]
    exts = first_ext, second_ext
    moves = fetches(plan, ring, w_proj, ready, sems)
    for move in moves:
        move.start()
    tokens, channels = og.shape
    fold = channels // LANES
    modes = (tables.shape[0] // fold - tokens) // 3
    dec, res = tokens, tokens + 2 * modes
    briefs = [payloads[0].at[pl.ds(0, (modes + 2) * fold)], *payloads[1:]]
    for j in range(fold):
        lanes = slice(j * LANES, (j + 1) * LANES)
        p = feat[1, :, lanes] * feat[2, :, lanes]
        prod[pl.ds(j, tokens, stride=fold), :] = p
        s = og[:, lanes] * feat[0, :, lanes]
        sums[modes : modes + 1, lanes] = jnp.sum(s * p, axis=0, keepdims=True)

    def rows(ref, at):
        return ref[at * fold : (at + 1) * fold, :]

    direct = bias[...]
    group = 8
    for low in range(0, modes, group):
        chosen = range(low, min(low + group, modes))
        decay, weight = ([rows(tables, at + m) for m in chosen] for at in (dec, res))
        state = [all_carried(briefs, spans, m, tables, tokens, fold) for m in chosen]

        def corr(state, weight=weight):
            terms = [w * s for w, s in zip(weight, state)]
            while len(terms) > 1:
                terms = [a + b for a, b in zip(terms[::2], terms[1::2])] + terms[len(terms) // 2 * 2 :]
            return terms[0]

        def put(at, row, state, low=low, corr=corr):
            here = pl.ds(at * fold, fold)
            if low == 0:
                gp[here, :] = corr(state) + direct * row
            else:
                gp[here, :] = gp[here, :] + corr(state)

        for n in (1, 0):
            row = rows(payloads[0], modes + n)
            state = [row + d * s for d, s in zip(decay, state)]
            put(tokens + n, row, state)

        def step(i, carry, decay=decay, put=put):
            state, total = carry
            at = tokens - 1 - i
            row = tables[pl.ds(at * fold, fold), :]
            other = prod[pl.ds(at * fold, fold), :]
            state = [row + d * s for d, s in zip(decay, state)]
            total = [a + other * s for a, s in zip(total, state)]
            put(at, row, state)
            return state, total

        zero = [jnp.zeros((fold, LANES), F32) for _ in chosen]
        state, total = lax.fori_loop(0, tokens, step, (state, zero), unroll=4)
        for m, a in zip(chosen, total):
            acc[m * fold : (m + 1) * fold, :] = a

    product_gradients(feat, gp, payloads[0], exts)
    for p, ext in enumerate(exts):
        taps = [filt[p + 1, j : j + 1, :] for j in range(3)]
        for j in range(fold):
            lanes = slice(j * LANES, (j + 1) * LANES)
            rounded[p, lanes, :] = tapped(ext, taps, lanes, tokens).astype(BF16).T
    for j in range(fold):
        sums[0:modes, j * LANES : (j + 1) * LANES] = acc[pl.ds(j, modes, stride=fold), :]
    for move in moves:
        move.wait()


def state_streams(feat, og, filt, bias, tables, payloads, spans, plan, ring, w_proj):
    tokens, channels = og.shape
    fold = channels // LANES
    modes = (tables.shape[0] // fold - tokens) // 3
    return pl.pallas_call(
        functools.partial(state_kernel, spans, plan, ring),
        in_specs=[whole()] * (5 + len(payloads)) + [in_hbm()],
        out_specs=[whole()] * 4,
        out_shape=[
            pltpu.VMEM((2, channels, tokens), BF16),
            pltpu.VMEM((modes + 1, channels), F32),
            pltpu.VMEM(((tokens + 2) * fold, LANES), F32),
            pltpu.VMEM((w_proj.shape[1], len(plan) * channels), BF16),
        ],
        scratch_shapes=[pltpu.VMEM((modes * fold, LANES), F32), pltpu.VMEM((tokens * fold, LANES), F32)]
        + [pltpu.VMEM((tokens + 8, channels), F32)] * 2
        + [pltpu.SemaphoreType.DMA((len(plan),))],
        compiler_params=params(),
        cost_estimate=cost(4 << 30, 16 << 20),
        name="state_streams",
    )(feat, og, filt, bias, tables, *payloads, w_proj)


def product_kernel(plan, base, later, first, last, ring, w_proj, w, *refs):
    refs = list(refs)
    moves = []
    if later:
        sems = refs.pop()
        moves = fetches(later, ring, w_proj, refs.pop(), sems)
    elif last:
        sems = refs.pop()
        turned = refs.pop()
    out = refs.pop()
    before = None if first else refs.pop()
    for move in moves:
        move.start()
    x = jnp.concatenate([refs[n][h, p] for *_, parts in plan for n, h, p in parts], axis=0)
    columns = slice(base * (x.shape[0] // len(plan)), (base + len(plan)) * (x.shape[0] // len(plan)))
    features = w.shape[0]
    wide = min(512, features)
    for d in range(0, features, wide):
        rows = slice(d, d + wide)
        y = jnp.dot(w[rows, columns], x, preferred_element_type=F32)
        if not first:
            y = y + before[rows]
        if last:
            turned[:, rows] = y.T
            moves.append(pltpu.make_async_copy(
                turned.at[:, pl.ds(d, wide)], out.at[:, pl.ds(d, wide)], sems.at[d // wide]
            ))
            moves[-1].start()
        else:
            out[rows] = y
    for move in moves:
        move.wait()


def steps_of(pieces):
    arrays, plan = [], []
    for array, places, stream, offset in pieces:
        halves = array if isinstance(array, tuple) else (array,)
        for h in range(halves[0].shape[0]):
            for p in places:
                plan.append((stream + p, h, offset, [(len(arrays) + n, h, p) for n in range(len(halves))]))
        arrays += halves
    return arrays, plan


def add_product(total, ready, base, pieces, later, last, ring, w_proj, span):
    features = w_proj.shape[1]
    arrays, plan = steps_of(pieces)
    channels, tokens = w_proj.shape[2] // lax.axis_size("chan"), arrays[0].shape[3]
    first = total is None
    out_specs = [whole()]
    out_shape = [pltpu.VMEM((features, tokens), F32)]
    scratch = []
    if last:
        out_specs = [in_hbm()]
        out_shape = [jax.ShapeDtypeStruct((tokens, features), F32)]
        scratch = [pltpu.VMEM((tokens, features), F32), pltpu.SemaphoreType.DMA((max(1, features // 512),))]
    elif later:
        out_specs += [whole()]
        out_shape += [pltpu.VMEM((features, len(later) * channels), BF16)]
        scratch = [pltpu.SemaphoreType.DMA((len(later),))]
    return pl.pallas_call(
        functools.partial(product_kernel, plan, base, later, first, last, ring),
        in_specs=[in_hbm()]
        + [whole()] * (1 + len(arrays) + (not first)),
        out_specs=out_specs,
        out_shape=out_shape,
        scratch_shapes=scratch,
        compiler_params=params(),
        cost_estimate=cost(*span),
        name="add_product",
    )(w_proj, ready, *arrays, *([] if first else [total]))


def ring_order(size):
    return list(range(0, size, 2)) + list(range(size - 1 - size % 2, 0, -2))


def after(array, *others):
    return lax.optimization_barrier((array, *others))[0]


def body(features, saved_conv, out_grad, short_filter, residue, rate, bias, w_proj):
    tokens, channels = out_grad.shape
    modes = rate.shape[1]
    blocks = lax.axis_size("ctx")
    groups = lax.axis_size("chan")
    ring = min(groups, RING)
    heights = groups // ring

    order = ring_order(ring)
    pairs = {
        by: [
            (h * ring + order[i], h * ring + order[(i + by) % ring])
            for h in range(heights)
            for i in range(ring)
        ]
        for by in (1, -1)
    }

    def up(x):
        return lax.ppermute(x, "chan", pairs[1])

    def down(x):
        return lax.ppermute(x, "chan", pairs[-1])

    def stacked(block):
        if heights == 1:
            return block[None]
        groups = [[h * ring + i for h in range(heights)] for i in range(ring)]
        return lax.all_gather(block, "chan", axis_index_groups=groups)

    def from_later(array, by):
        return lax.ppermute(array, "ctx", [(i, i - by) for i in range(by, blocks)])

    def exchanged(sums, by):
        return sums + lax.ppermute(sums, "ctx", [(i, i ^ by) for i in range(blocks)])

    fold = channels // LANES
    feat, conv, og, filt, bias_row, tables, own, brief = front(
        features, saved_conv, out_grad, short_filter, residue.T, rate.T, bias[None]
    )
    payloads, spans = [from_later(own, 1)], [tokens]
    unit, window = 1, brief
    while unit < blocks:
        for by in range(len(payloads) % 3 + 1, 4):
            if by * unit < blocks:
                payloads.append(from_later(window, by * unit))
                spans.append(unit * tokens)
        unit *= 4
        if unit < blocks:
            near = [window, *payloads[-3:]]
            near[1] = near[1][: window.shape[0]]
            window = join(near, unit // 4 * tokens, tables, tokens, fold)
    gate = gate_stream(feat, conv, og, filt, bias_row, payloads[0])
    a0 = stacked(gate)
    a1, z1 = up(a0), down(a0)

    half = channels // 2
    back = ring // 2

    a, b = (0,), (0, 1)
    sets = [
        [("a0", a, 0, 0), ("a1", a, 0, ring - 1), ("z1", a, 0, 1)],
        [("b0", b, 1, 0)],
        [("b1", b, 1, ring - 1), ("y1", b, 1, 1)],
        [("a2", a, 0, ring - 2), ("z2", a, 0, 2)],
        [("b2", b, 1, ring - 2), ("y2", (0,), 1, 2)],
        [("y2", (1,), 1, 2), ("a3", a, 0, ring - 3), ("z3", a, 0, 3)],
        [("b3", b, 1, ring - 3), ("y3", b, 1, 3)],
        [("a4", a, 0, back)],
        [("b4", a, 1, back)],
        [("y4", a, 2, back)],
    ]
    costs = [LONG, LONG, SHORT, LONG, SHORT, LONG, MIDDLE, TAIL, SHORT, SHORT]
    hollow = jax.ShapeDtypeStruct((heights, 2, channels, tokens), BF16)

    def plan_of(n):
        return steps_of([(hollow, *piece[1:]) for piece in sets[n]])[1]

    def times(n, total, ready, **arrays):
        pieces = [(arrays[name], *rest) for name, *rest in sets[n]]
        after_next = [plan_of(k) for k in range(7, len(sets))]
        later = plan_of(n + 1) if n < 6 else sum(after_next, []) if n == 6 else None
        base = sum(len(plan) for plan in after_next[: max(0, n - 7)])
        return add_product(total, ready, base, pieces, later, n == len(sets) - 1, ring, w_proj, costs[n])

    payloads[0], a0 = lax.optimization_barrier((payloads[0], a0))
    rounds, sums, gp, ready = state_streams(
        feat, og, filt, bias_row.reshape(fold, LANES), tables, payloads, spans, plan_of(0), ring, w_proj
    )
    b0 = stacked(rounds)

    b1, y1 = up(b0), down(b0)
    a1, z1, b0, sums = lax.optimization_barrier((a1, z1, b0, sums))
    a2, z2 = up(a1), down(z1)
    distances = [1 << n for n in range((blocks - 1).bit_length())]
    for by in distances[:1]:
        sums = exchanged(sums, by)
    total, ready = times(0, None, ready, a0=a0, a1=a1, z1=z1)
    total, ready = times(1, total, ready, b0=b0)
    b1, y1, total, sums = lax.optimization_barrier((b1, y1, total, sums))
    b2, y2 = up(b1), down(y1)
    total, ready = times(2, total, ready, b1=b1, y1=y1)

    a2, z2, total, sums = lax.optimization_barrier((a2, z2, total, sums))
    a3, z3 = up(a2), down(z2)
    for by in distances[1:]:
        sums = exchanged(sums, by)
    total, ready = times(3, total, ready, a2=a2, z2=z2)
    grads = gradients(features, saved_conv, out_grad, short_filter, bias[None], payloads[0], after(gp, total))

    b2, y2, total, sums, grads = lax.optimization_barrier((b2, y2, total, sums, grads))
    b3, y3 = up(b2), down(y2)
    total, ready = times(4, total, ready, b2=b2, y2=y2)

    a3, z3, total = lax.optimization_barrier((a3, z3, total))
    a4 = up(a3[:, :, :half]), down(z3[:, :, half:])
    total, ready = times(5, total, ready, y2=y2, a3=a3, z3=z3)

    b3, y3, total, sums = lax.optimization_barrier((b3, y3, total, sums))
    b4, y4 = up(b3[:, :1]), down(y3[:, 1:])
    total, ready = times(6, total, ready, b3=b3, y3=y3)

    a4, total, sums = lax.optimization_barrier((a4, total, sums))
    (total,) = times(7, total, ready, a4=a4)
    sums = sums * (tokens * blocks) ** (-0.5)
    grad_residue, grad_bias = sums[:modes].T, sums[modes]
    b4, total, grad_residue, grad_bias = lax.optimization_barrier((b4, total, grad_residue, grad_bias))
    (total,) = times(8, total, ready, b4=b4)
    (grad_x,) = times(9, total, ready, y4=y4)
    return (grads, grad_x, grad_residue, grad_bias)


def solution(mesh):
    return jax.shard_map(
        body,
        mesh=mesh,
        in_specs=(
            P(None, "ctx", "chan"),
            P("ctx", "chan"),
            P("ctx", "chan"),
            P(None, None, "chan"),
            P("chan", None),
            P("chan", None),
            P("chan"),
            P(None, "chan", None),
        ),
        out_specs=(P(None, "ctx", "chan"), P("ctx", "chan"), P("chan", None), P("chan")),
        check_vma=False,
    )
```

```python
import functools

import jax
import jax.numpy as jnp
from jax import lax
from jax.experimental import pallas as pl
from jax.experimental.pallas import tpu as pltpu
from jax.sharding import PartitionSpec as P

LANES = 128
RING = 8
LONG = 1 << 36, 1 << 28
SHORT = 1 << 16, 1 << 8
MIDDLE = 1 << 30, 9 << 20
TAIL = 7 << 28, 13 << 20
VMEM = 8 * 1024 * 1024
F32 = jnp.float32
BF16 = jnp.bfloat16


def whole():
    return pl.BlockSpec(memory_space=pltpu.VMEM)


def in_hbm():
    return pl.BlockSpec(memory_space=pltpu.HBM)


def params():
    return pltpu.CompilerParams(vmem_limit_bytes=VMEM)


def cost(flops, size):
    return pl.CostEstimate(flops=flops, bytes_accessed=size, transcendentals=0)


def by_row(values, out, fold, base=0):
    for j in range(fold):
        out[pl.ds(base * fold + j, values.shape[0], stride=fold), :] = values[:, j * LANES : (j + 1) * LANES]


def front_kernel(features, saved_conv, out_grad, short_filter, residue, rate, bias, *refs):
    feat, conv, og, filt, bias_in, tables, own, brief, res_in, rate_in, sems = refs
    tokens, channels = og.shape
    modes = rate_in.shape[0]
    fold = channels // LANES
    moves = [
        pltpu.make_async_copy(source, target, sems.at[n])
        for n, (source, target) in enumerate((
            (rate, rate_in),
            (out_grad, og),
            (features.at[0], feat.at[0]),
            (features.at[pl.ds(1, 2)], feat.at[pl.ds(1, 2)]),
            (saved_conv, conv),
            (short_filter, filt),
            (residue, res_in),
            (bias, bias_in),
        ))
    ]
    for move in moves:
        move.start()
    moves[0].wait()
    by_row(jnp.exp(-rate_in[...]), tables, fold, tokens)
    by_row(rate_in[...], tables, fold, tokens + modes)
    moves[1].wait()
    moves[2].wait()
    for j in range(fold):
        lanes = slice(j * LANES, (j + 1) * LANES)
        tables[pl.ds(j, tokens, stride=fold), :] = og[:, lanes] * feat[0, :, lanes]
    decay = [tables[(tokens + m) * fold : (tokens + m + 1) * fold, :] for m in range(modes)]

    def step(i, states):
        row = tables[pl.ds((tokens - 1 - i) * fold, fold), :]
        return tuple(row + d * s for d, s in zip(decay, states))

    zero = tuple(jnp.zeros((fold, LANES), F32) for _ in range(modes))
    states = lax.fori_loop(0, tokens - 2, step, zero, unroll=6)
    for target in (own, brief):
        for m in range(modes):
            target[m * fold : (m + 1) * fold, :] = states[m]
        target[modes * fold : (modes + 2) * fold, :] = tables[0 : 2 * fold, :]
    for n in range(3, 8):
        moves[n].wait()
    for n in range(3):
        by_row(feat[n, 0:2, :], own, fold, modes + 2 + 2 * n)
    by_row(conv[0:2, :], own, fold, modes + 8)
    by_row(og[0:2, :], own, fold, modes + 10)
    by_row(res_in[...], tables, fold, tokens + 2 * modes)


def front(features, saved_conv, out_grad, short_filter, residue, rate, bias):
    tokens, channels = out_grad.shape
    modes = rate.shape[0]
    fold = channels // LANES
    inputs = (features, saved_conv, out_grad, short_filter, residue, rate, bias)
    return pl.pallas_call(
        front_kernel,
        in_specs=[in_hbm()] * 7,
        out_specs=[whole()] * 8,
        out_shape=[pltpu.VMEM(a.shape, F32) for a in (*inputs[:4], bias)]
        + [pltpu.VMEM((n * fold, LANES), F32) for n in (tokens + 3 * modes, modes + 12, modes + 2)],
        scratch_shapes=[pltpu.VMEM(rate.shape, F32)] * 2 + [pltpu.SemaphoreType.DMA((8,))],
        compiler_params=params(),
        cost_estimate=cost(4 * tokens * channels * modes, 20 * tokens * channels),
        name="front",
    )(*(pltpu.with_memory_space_constraint(a, pltpu.HBM) for a in inputs))


def tapped(ext, taps, lanes, tokens):
    total = taps[0][:, lanes] * ext[0:tokens, lanes]
    total = total + taps[1][:, lanes] * ext[1 : tokens + 1, lanes]
    return total + taps[2][:, lanes] * ext[2 : tokens + 2, lanes]


def rim_rows(later, which, j, fold):
    modes = later.shape[0] // fold - 12
    return later[pl.ds((modes + 2 + 2 * which) * fold + j, 2, stride=fold), :]


def gate_gradient(feat, conv, og, bias, later, ext):
    tokens, channels = og.shape
    fold = channels // LANES
    for j in range(fold):
        lanes = slice(j * LANES, (j + 1) * LANES)
        product = feat[1, :, lanes] * feat[2, :, lanes]
        ext[0:tokens, lanes] = og[:, lanes] * (conv[:, lanes] + bias[:, lanes] * product)
        key, value, held, cotangent = (rim_rows(later, n, j, fold) for n in (1, 2, 3, 4))
        ext[tokens : tokens + 2, lanes] = cotangent * (held + bias[:, lanes] * (key * value))


def carried(own, m, later, state, decay, rate, span, fold):
    modes = own.shape[0] // fold - 2
    s0, s1 = (later[(modes + n) * fold : (modes + n + 1) * fold, :] for n in (0, 1))
    return own[m * fold : (m + 1) * fold, :] + jnp.exp(-(span - 2) * rate) * (s0 + decay * (s1 + decay * state))


def all_carried(summaries, spans, m, tables, tokens, fold):
    modes = summaries[0].shape[0] // fold - 2
    decay, rate = (tables[(tokens + n * modes + m) * fold : (tokens + n * modes + m + 1) * fold, :] for n in (0, 1))
    state = summaries[-1][m * fold : (m + 1) * fold, :]
    for own, later, span in reversed(list(zip(summaries, summaries[1:], spans))):
        state = carried(own, m, later, state, decay, rate, span, fold)
    return state


def join(summaries, span, tables, tokens, fold):
    def kernel(tables, *refs):
        *refs, out = refs
        modes = out.shape[0] // fold - 2
        for m in range(modes):
            out[m * fold : (m + 1) * fold, :] = all_carried(refs, [span] * (len(refs) - 1), m, tables, tokens, fold)
        out[modes * fold : (modes + 2) * fold, :] = refs[0][modes * fold : (modes + 2) * fold, :]

    return pl.pallas_call(
        kernel,
        in_specs=[whole()] * (1 + len(summaries)),
        out_specs=whole(),
        out_shape=pltpu.VMEM(summaries[0].shape, F32),
        compiler_params=params(),
        name="join",
    )(tables, *summaries)


def gate_kernel(feat, conv, og, filt, bias, later, rounded, ext):
    tokens, channels = og.shape
    taps = [filt[0, j : j + 1, :] for j in range(3)]
    gate_gradient(feat, conv, og, bias, later, ext)
    for j in range(channels // LANES):
        lanes = slice(j * LANES, (j + 1) * LANES)
        rounded[0, lanes, :] = tapped(ext, taps, lanes, tokens).astype(BF16).T


def gate_stream(feat, conv, og, filt, bias, later):
    tokens, channels = og.shape
    return pl.pallas_call(
        gate_kernel,
        in_specs=[whole()] * 6,
        out_specs=whole(),
        out_shape=pltpu.VMEM((1, channels, tokens), BF16),
        scratch_shapes=[pltpu.VMEM((tokens + 8, channels), F32)],
        compiler_params=params(),
        cost_estimate=cost(*LONG),
        name="gate_stream",
    )(feat, conv, og, filt, bias, later)


def product_gradients(feat, gp, later, exts):
    tokens, channels = feat.shape[1:]
    fold = channels // LANES
    for j in range(fold):
        lanes = slice(j * LANES, (j + 1) * LANES)
        g = gp[pl.ds(j, tokens, stride=fold), :]
        rim = gp[pl.ds(tokens * fold + j, 2, stride=fold), :]
        for ext, n in zip(exts, (2, 1)):
            ext[0:tokens, lanes] = g * feat[n, :, lanes]
            ext[tokens : tokens + 2, lanes] = rim * rim_rows(later, n, j, fold)


def gradients_kernel(feat, conv, og, filt, bias, later, gp, out, first, second, third, ready, sems):
    tokens, channels = og.shape
    gate_gradient(feat, conv, og, bias, later, first)
    product_gradients(feat, gp, later, (second, third))
    moves = []
    for p, ext in enumerate((first, second, third)):
        taps = [filt[p, j : j + 1, :] for j in range(3)]
        for j in range(channels // LANES):
            lanes = slice(j * LANES, (j + 1) * LANES)
            ready[p, :, lanes] = tapped(ext, taps, lanes, tokens)
        moves.append(pltpu.make_async_copy(ready.at[p], out.at[p], sems.at[p]))
        moves[-1].start()
    for move in moves:
        move.wait()


def gradients(feat, conv, og, filt, bias, later, gp):
    tokens, channels = og.shape
    return pl.pallas_call(
        gradients_kernel,
        in_specs=[whole()] * 7,
        out_specs=in_hbm(),
        out_shape=jax.ShapeDtypeStruct((3, tokens, channels), F32),
        scratch_shapes=[pltpu.VMEM((tokens + 8, channels), F32)] * 3
        + [pltpu.VMEM((3, tokens, channels), F32), pltpu.SemaphoreType.DMA((3,))],
        compiler_params=params(),
        cost_estimate=cost(30 * tokens * channels, 40 * tokens * channels),
        name="gradients",
    )(feat, conv, og, filt, bias, later, gp)


def on_ring(offset, ring):
    own = lax.rem(lax.axis_index("chan"), ring)
    place = jnp.where(lax.rem(own, 2) == 0, own // 2, ring - 1 - own // 2)
    place = lax.rem(place + offset, ring)
    return jnp.where(place < (ring + 1) // 2, 2 * place, 2 * (ring - 1 - place) + 1)


def fetches(plan, ring, w_proj, ready, sems):
    channels = ready.shape[1] // len(plan)
    moves = []
    for k, (stream, height, offset, _) in enumerate(plan):
        begin = pl.multiple_of((height * ring + on_ring(offset, ring)) * channels, LANES)
        columns = w_proj.at[stream, :, pl.ds(begin, channels)]
        moves.append(pltpu.make_async_copy(columns, ready.at[:, pl.ds(k * channels, channels)], sems.at[k]))
    return moves


def state_kernel(spans, plan, ring, feat, og, filt, bias, tables, *refs):
    later = len(spans)
    payloads = refs[:later][::-1]
    w_proj, rounded, sums, gp, ready, acc, prod, first_ext, second_ext, sems = refs[later:]
    exts = first_ext, second_ext
    moves = fetches(plan, ring, w_proj, ready, sems)
    for move in moves:
        move.start()
    tokens, channels = og.shape
    fold = channels // LANES
    modes = (tables.shape[0] // fold - tokens) // 3
    dec, res = tokens, tokens + 2 * modes
    briefs = [payloads[0].at[pl.ds(0, (modes + 2) * fold)], *payloads[1:]]
    for j in range(fold):
        lanes = slice(j * LANES, (j + 1) * LANES)
        p = feat[1, :, lanes] * feat[2, :, lanes]
        prod[pl.ds(j, tokens, stride=fold), :] = p
        s = og[:, lanes] * feat[0, :, lanes]
        sums[modes : modes + 1, lanes] = jnp.sum(s * p, axis=0, keepdims=True)

    def rows(ref, at):
        return ref[at * fold : (at + 1) * fold, :]

    direct = bias[...]
    group = 8
    for low in range(0, modes, group):
        chosen = range(low, min(low + group, modes))
        decay, weight = ([rows(tables, at + m) for m in chosen] for at in (dec, res))
        state = [all_carried(briefs, spans, m, tables, tokens, fold) for m in chosen]

        def corr(state, weight=weight):
            terms = [w * s for w, s in zip(weight, state)]
            while len(terms) > 1:
                terms = [a + b for a, b in zip(terms[::2], terms[1::2])] + terms[len(terms) // 2 * 2 :]
            return terms[0]

        def put(at, row, state, low=low, corr=corr):
            here = pl.ds(at * fold, fold)
            if low == 0:
                gp[here, :] = corr(state) + direct * row
            else:
                gp[here, :] = gp[here, :] + corr(state)

        for n in (1, 0):
            row = rows(payloads[0], modes + n)
            state = [row + d * s for d, s in zip(decay, state)]
            put(tokens + n, row, state)

        def step(i, carry, decay=decay, put=put):
            state, total = carry
            at = tokens - 1 - i
            row = tables[pl.ds(at * fold, fold), :]
            other = prod[pl.ds(at * fold, fold), :]
            state = [row + d * s for d, s in zip(decay, state)]
            total = [a + other * s for a, s in zip(total, state)]
            put(at, row, state)
            return state, total

        zero = [jnp.zeros((fold, LANES), F32) for _ in chosen]
        state, total = lax.fori_loop(0, tokens, step, (state, zero), unroll=4)
        for m, a in zip(chosen, total):
            acc[m * fold : (m + 1) * fold, :] = a

    product_gradients(feat, gp, payloads[0], exts)
    for p, ext in enumerate(exts):
        taps = [filt[p + 1, j : j + 1, :] for j in range(3)]
        for j in range(fold):
            lanes = slice(j * LANES, (j + 1) * LANES)
            rounded[p, lanes, :] = tapped(ext, taps, lanes, tokens).astype(BF16).T
    for j in range(fold):
        sums[0:modes, j * LANES : (j + 1) * LANES] = acc[pl.ds(j, modes, stride=fold), :]
    for move in moves:
        move.wait()


def state_streams(feat, og, filt, bias, tables, payloads, spans, plan, ring, w_proj):
    tokens, channels = og.shape
    fold = channels // LANES
    modes = (tables.shape[0] // fold - tokens) // 3
    return pl.pallas_call(
        functools.partial(state_kernel, spans, plan, ring),
        in_specs=[whole()] * (5 + len(payloads)) + [in_hbm()],
        out_specs=[whole()] * 4,
        out_shape=[
            pltpu.VMEM((2, channels, tokens), BF16),
            pltpu.VMEM((modes + 1, channels), F32),
            pltpu.VMEM(((tokens + 2) * fold, LANES), F32),
            pltpu.VMEM((w_proj.shape[1], len(plan) * channels), BF16),
        ],
        scratch_shapes=[pltpu.VMEM((modes * fold, LANES), F32), pltpu.VMEM((tokens * fold, LANES), F32)]
        + [pltpu.VMEM((tokens + 8, channels), F32)] * 2
        + [pltpu.SemaphoreType.DMA((len(plan),))],
        compiler_params=params(),
        cost_estimate=cost(4 << 30, 16 << 20),
        name="state_streams",
    )(feat, og, filt, bias, tables, *reversed(payloads), w_proj)


def product_kernel(plan, base, later, first, last, ring, w_proj, w, *refs):
    refs = list(refs)
    moves = []
    if later:
        sems = refs.pop()
        moves = fetches(later, ring, w_proj, refs.pop(), sems)
    elif last:
        sems = refs.pop()
        turned = refs.pop()
    out = refs.pop()
    before = None if first else refs.pop()
    for move in moves:
        move.start()
    x = jnp.concatenate([refs[n][h, p] for *_, parts in plan for n, h, p in parts], axis=0)
    columns = slice(base * (x.shape[0] // len(plan)), (base + len(plan)) * (x.shape[0] // len(plan)))
    features = w.shape[0]
    wide = min(512, features)
    for d in range(0, features, wide):
        rows = slice(d, d + wide)
        y = jnp.dot(w[rows, columns], x, preferred_element_type=F32)
        if not first:
            y = y + before[rows]
        if last:
            turned[:, rows] = y.T
            moves.append(pltpu.make_async_copy(
                turned.at[:, pl.ds(d, wide)], out.at[:, pl.ds(d, wide)], sems.at[d // wide]
            ))
            moves[-1].start()
        else:
            out[rows] = y
    for move in moves:
        move.wait()


def steps_of(pieces):
    arrays, plan = [], []
    for array, places, stream, offset in pieces:
        halves = array if isinstance(array, tuple) else (array,)
        for h in range(halves[0].shape[0]):
            for p in places:
                plan.append((stream + p, h, offset, [(len(arrays) + n, h, p) for n in range(len(halves))]))
        arrays += halves
    return arrays, plan


def add_product(total, ready, base, pieces, later, last, ring, w_proj, span):
    features = w_proj.shape[1]
    arrays, plan = steps_of(pieces)
    channels, tokens = w_proj.shape[2] // lax.axis_size("chan"), arrays[0].shape[3]
    first = total is None
    out_specs = [whole()]
    out_shape = [pltpu.VMEM((features, tokens), F32)]
    scratch = []
    if last:
        out_specs = [in_hbm()]
        out_shape = [jax.ShapeDtypeStruct((tokens, features), F32)]
        scratch = [pltpu.VMEM((tokens, features), F32), pltpu.SemaphoreType.DMA((max(1, features // 512),))]
    elif later:
        out_specs += [whole()]
        out_shape += [pltpu.VMEM((features, len(later) * channels), BF16)]
        scratch = [pltpu.SemaphoreType.DMA((len(later),))]
    return pl.pallas_call(
        functools.partial(product_kernel, plan, base, later, first, last, ring),
        in_specs=[in_hbm()]
        + [whole()] * (1 + len(arrays) + (not first)),
        out_specs=out_specs,
        out_shape=out_shape,
        scratch_shapes=scratch,
        compiler_params=params(),
        cost_estimate=cost(*span),
        name="add_product",
    )(w_proj, ready, *arrays, *([] if first else [total]))


def ring_order(size):
    return list(range(0, size, 2)) + list(range(size - 1 - size % 2, 0, -2))


def after(array, *others):
    return lax.optimization_barrier((array, *others))[0]


def body(features, saved_conv, out_grad, short_filter, residue, rate, bias, w_proj):
    tokens, channels = out_grad.shape
    modes = rate.shape[1]
    blocks = lax.axis_size("ctx")
    groups = lax.axis_size("chan")
    ring = min(groups, RING)
    heights = groups // ring

    order = ring_order(ring)
    pairs = {
        by: [
            (h * ring + order[i], h * ring + order[(i + by) % ring])
            for h in range(heights)
            for i in range(ring)
        ]
        for by in (1, -1)
    }

    def up(x):
        return lax.ppermute(x, "chan", pairs[1])

    def down(x):
        return lax.ppermute(x, "chan", pairs[-1])

    def stacked(block):
        if heights == 1:
            return block[None]
        groups = [[h * ring + i for h in range(heights)] for i in range(ring)]
        return lax.all_gather(block, "chan", axis_index_groups=groups)

    def from_later(array, by):
        return lax.ppermute(array, "ctx", [(i, i - by) for i in range(by, blocks)])

    def exchanged(sums, by):
        return sums + lax.ppermute(sums, "ctx", [(i, i ^ by) for i in range(blocks)])

    fold = channels // LANES
    feat, conv, og, filt, bias_row, tables, own, brief = front(
        features, saved_conv, out_grad, short_filter, residue.T, rate.T, bias[None]
    )
    payloads, spans = [from_later(own, 1)], [tokens]
    unit, window = 1, brief
    while unit < blocks:
        for by in range(len(payloads) % 3 + 1, 4):
            if by * unit < blocks:
                payloads.append(from_later(window, by * unit))
                spans.append(unit * tokens)
        unit *= 4
        if unit < blocks:
            near = [window, *payloads[-3:]]
            near[1] = near[1][: window.shape[0]]
            window = join(near, unit // 4 * tokens, tables, tokens, fold)
    gate = gate_stream(feat, conv, og, filt, bias_row, payloads[0])
    a0 = stacked(gate)
    a1, z1 = up(a0), down(a0)

    half = channels // 2
    back = ring // 2

    a, b = (0,), (0, 1)
    sets = [
        [("a0", a, 0, 0), ("a1", a, 0, ring - 1), ("z1", a, 0, 1)],
        [("b0", b, 1, 0)],
        [("b1", b, 1, ring - 1), ("y1", b, 1, 1)],
        [("a2", a, 0, ring - 2), ("z2", a, 0, 2)],
        [("b2", b, 1, ring - 2), ("y2", (0,), 1, 2)],
        [("y2", (1,), 1, 2), ("a3", a, 0, ring - 3), ("z3", a, 0, 3)],
        [("b3", b, 1, ring - 3), ("y3", b, 1, 3)],
        [("a4", a, 0, back)],
        [("b4", a, 1, back)],
        [("y4", a, 2, back)],
    ]
    costs = [LONG, LONG, SHORT, LONG, SHORT, LONG, MIDDLE, TAIL, SHORT, SHORT]
    hollow = jax.ShapeDtypeStruct((heights, 2, channels, tokens), BF16)

    def plan_of(n):
        return steps_of([(hollow, *piece[1:]) for piece in sets[n]])[1]

    def times(n, total, ready, **arrays):
        pieces = [(arrays[name], *rest) for name, *rest in sets[n]]
        after_next = [plan_of(k) for k in range(7, len(sets))]
        later = plan_of(n + 1) if n < 6 else sum(after_next, []) if n == 6 else None
        base = sum(len(plan) for plan in after_next[: max(0, n - 7)])
        return add_product(total, ready, base, pieces, later, n == len(sets) - 1, ring, w_proj, costs[n])

    payloads[0], a0 = lax.optimization_barrier((payloads[0], a0))
    rounds, sums, gp, ready = state_streams(
        feat, og, filt, bias_row.reshape(fold, LANES), tables, payloads, spans, plan_of(0), ring, w_proj
    )
    b0 = stacked(rounds)

    b1, y1 = up(b0), down(b0)
    a1, z1, b0, sums = lax.optimization_barrier((a1, z1, b0, sums))
    a2, z2 = up(a1), down(z1)
    distances = [1 << n for n in range((blocks - 1).bit_length())]
    for by in distances[:1]:
        sums = exchanged(sums, by)
    total, ready = times(0, None, ready, a0=a0, a1=a1, z1=z1)
    total, ready = times(1, total, ready, b0=b0)
    b1, total, sums = lax.optimization_barrier((b1, total, sums))
    b2 = up(b1)
    y1, total = lax.optimization_barrier((y1, total))
    y2 = down(y1)
    total, ready = times(2, total, ready, b1=b1, y1=y1)

    a2, z2, total, sums = lax.optimization_barrier((a2, z2, total, sums))
    a3, z3 = up(a2), down(z2)
    for by in distances[1:]:
        sums = exchanged(sums, by)
    total, ready = times(3, total, ready, a2=a2, z2=z2)
    grads = gradients(features, saved_conv, out_grad, short_filter, bias[None], payloads[0], after(gp, total))

    b2, total, sums, grads = lax.optimization_barrier((b2, total, sums, grads))
    b3 = up(b2)
    y2, total = lax.optimization_barrier((y2, total))
    y3 = down(y2)
    total, ready = times(4, total, ready, b2=b2, y2=y2)

    a3, z3, total = lax.optimization_barrier((a3, z3, total))
    a4 = up(a3[:, :, :half]), down(z3[:, :, half:])
    total, ready = times(5, total, ready, y2=y2, a3=a3, z3=z3)

    sums = sums * (tokens * blocks) ** (-0.5)
    grad_residue, grad_bias = sums[:modes].T, sums[modes]
    b3, total, grad_residue, grad_bias = lax.optimization_barrier((b3, total, grad_residue, grad_bias))
    b4 = up(b3[:, :1])
    y3, total = lax.optimization_barrier((y3, total))
    y4 = down(y3[:, 1:])
    total, ready = times(6, total, ready, b3=b3, y3=y3)

    a4, total = lax.optimization_barrier((a4, total))
    (total,) = times(7, total, ready, a4=a4)
    b4, total = lax.optimization_barrier((b4, total))
    (total,) = times(8, total, ready, b4=b4)
    (grad_x,) = times(9, total, ready, y4=y4)
    return (grads, grad_x, grad_residue, grad_bias)


def solution(mesh):
    return jax.shard_map(
        body,
        mesh=mesh,
        in_specs=(
            P(None, "ctx", "chan"),
            P("ctx", "chan"),
            P("ctx", "chan"),
            P(None, None, "chan"),
            P("chan", None),
            P("chan", None),
            P("chan"),
            P(None, "chan", None),
        ),
        out_specs=(P(None, "ctx", "chan"), P("ctx", "chan"), P("chan", None), P("chan")),
        check_vma=False,
    )
```

```python
import functools

import jax
import jax.numpy as jnp
from jax import lax
from jax.experimental import pallas as pl
from jax.experimental.pallas import tpu as pltpu
from jax.sharding import PartitionSpec as P

LANES = 128
RING = 8
LONG = 1 << 36, 1 << 28
SHORT = 1 << 16, 1 << 8
VMEM = 8 * 1024 * 1024
F32 = jnp.float32
BF16 = jnp.bfloat16


def whole():
    return pl.BlockSpec(memory_space=pltpu.VMEM)


def in_hbm():
    return pl.BlockSpec(memory_space=pltpu.HBM)


def params():
    return pltpu.CompilerParams(vmem_limit_bytes=VMEM)


def cost(flops, size):
    return pl.CostEstimate(flops=flops, bytes_accessed=size, transcendentals=0)


def by_row(values, out, fold, base=0):
    for j in range(fold):
        out[pl.ds(base * fold + j, values.shape[0], stride=fold), :] = values[:, j * LANES : (j + 1) * LANES]


def front_kernel(features, saved_conv, out_grad, short_filter, residue, rate, bias, *refs):
    feat, conv, og, filt, bias_in, tables, own, brief, res_in, rate_in, sems = refs
    tokens, channels = og.shape
    modes = rate_in.shape[0]
    fold = channels // LANES
    moves = [
        pltpu.make_async_copy(source, target, sems.at[n])
        for n, (source, target) in enumerate((
            (rate, rate_in),
            (out_grad, og),
            (features.at[0], feat.at[0]),
            (features.at[pl.ds(1, 2)], feat.at[pl.ds(1, 2)]),
            (saved_conv, conv),
            (short_filter, filt),
            (residue, res_in),
            (bias, bias_in),
        ))
    ]
    for move in moves:
        move.start()
    moves[0].wait()
    by_row(jnp.exp(-rate_in[...]), tables, fold, tokens)
    by_row(rate_in[...], tables, fold, tokens + modes)
    moves[1].wait()
    moves[2].wait()
    for j in range(fold):
        lanes = slice(j * LANES, (j + 1) * LANES)
        tables[pl.ds(j, tokens, stride=fold), :] = og[:, lanes] * feat[0, :, lanes]
    decay = [tables[(tokens + m) * fold : (tokens + m + 1) * fold, :] for m in range(modes)]

    def step(i, states):
        row = tables[pl.ds((tokens - 1 - i) * fold, fold), :]
        return tuple(row + d * s for d, s in zip(decay, states))

    zero = tuple(jnp.zeros((fold, LANES), F32) for _ in range(modes))
    states = lax.fori_loop(0, tokens - 2, step, zero, unroll=6)
    for target in (own, brief):
        for m in range(modes):
            target[m * fold : (m + 1) * fold, :] = states[m]
        target[modes * fold : (modes + 2) * fold, :] = tables[0 : 2 * fold, :]
    for n in range(3, 8):
        moves[n].wait()
    for n in range(3):
        by_row(feat[n, 0:2, :], own, fold, modes + 2 + 2 * n)
    by_row(conv[0:2, :], own, fold, modes + 8)
    by_row(og[0:2, :], own, fold, modes + 10)
    by_row(res_in[...], tables, fold, tokens + 2 * modes)


def front(features, saved_conv, out_grad, short_filter, residue, rate, bias):
    tokens, channels = out_grad.shape
    modes = rate.shape[0]
    fold = channels // LANES
    inputs = (features, saved_conv, out_grad, short_filter, residue, rate, bias)
    return pl.pallas_call(
        front_kernel,
        in_specs=[in_hbm()] * 7,
        out_specs=[whole()] * 8,
        out_shape=[pltpu.VMEM(a.shape, F32) for a in (*inputs[:4], bias)]
        + [pltpu.VMEM((n * fold, LANES), F32) for n in (tokens + 3 * modes, modes + 12, modes + 2)],
        scratch_shapes=[pltpu.VMEM(rate.shape, F32)] * 2 + [pltpu.SemaphoreType.DMA((8,))],
        compiler_params=params(),
        cost_estimate=cost(4 * tokens * channels * modes, 20 * tokens * channels),
        name="front",
    )(*(pltpu.with_memory_space_constraint(a, pltpu.HBM) for a in inputs))


def tapped(ext, taps, lanes, tokens):
    total = taps[0][:, lanes] * ext[0:tokens, lanes]
    total = total + taps[1][:, lanes] * ext[1 : tokens + 1, lanes]
    return total + taps[2][:, lanes] * ext[2 : tokens + 2, lanes]


def rim_rows(later, which, j, fold):
    modes = later.shape[0] // fold - 12
    return later[pl.ds((modes + 2 + 2 * which) * fold + j, 2, stride=fold), :]


def gate_gradient(feat, conv, og, bias, later, ext):
    tokens, channels = og.shape
    fold = channels // LANES
    for j in range(fold):
        lanes = slice(j * LANES, (j + 1) * LANES)
        product = feat[1, :, lanes] * feat[2, :, lanes]
        ext[0:tokens, lanes] = og[:, lanes] * (conv[:, lanes] + bias[:, lanes] * product)
        key, value, held, cotangent = (rim_rows(later, n, j, fold) for n in (1, 2, 3, 4))
        ext[tokens : tokens + 2, lanes] = cotangent * (held + bias[:, lanes] * (key * value))


def carried(own, m, later, state, decay, rate, span, fold):
    modes = own.shape[0] // fold - 2
    s0, s1 = (later[(modes + n) * fold : (modes + n + 1) * fold, :] for n in (0, 1))
    return own[m * fold : (m + 1) * fold, :] + jnp.exp(-(span - 2) * rate) * (s0 + decay * (s1 + decay * state))


def all_carried(summaries, spans, m, tables, tokens, fold):
    modes = summaries[0].shape[0] // fold - 2
    decay, rate = (tables[(tokens + n * modes + m) * fold : (tokens + n * modes + m + 1) * fold, :] for n in (0, 1))
    state = summaries[-1][m * fold : (m + 1) * fold, :]
    for own, later, span in reversed(list(zip(summaries, summaries[1:], spans))):
        state = carried(own, m, later, state, decay, rate, span, fold)
    return state


def join(summaries, span, tables, tokens, fold):
    def kernel(tables, *refs):
        *refs, out = refs
        modes = out.shape[0] // fold - 2
        for m in range(modes):
            out[m * fold : (m + 1) * fold, :] = all_carried(refs, [span] * (len(refs) - 1), m, tables, tokens, fold)
        out[modes * fold : (modes + 2) * fold, :] = refs[0][modes * fold : (modes + 2) * fold, :]

    return pl.pallas_call(
        kernel,
        in_specs=[whole()] * (1 + len(summaries)),
        out_specs=whole(),
        out_shape=pltpu.VMEM(summaries[0].shape, F32),
        compiler_params=params(),
        name="join",
    )(tables, *summaries)


def gate_kernel(feat, conv, og, filt, bias, later, rounded, ext):
    tokens, channels = og.shape
    taps = [filt[0, j : j + 1, :] for j in range(3)]
    gate_gradient(feat, conv, og, bias, later, ext)
    for j in range(channels // LANES):
        lanes = slice(j * LANES, (j + 1) * LANES)
        rounded[0, lanes, :] = tapped(ext, taps, lanes, tokens).astype(BF16).T


def gate_stream(feat, conv, og, filt, bias, later):
    tokens, channels = og.shape
    return pl.pallas_call(
        gate_kernel,
        in_specs=[whole()] * 6,
        out_specs=whole(),
        out_shape=pltpu.VMEM((1, channels, tokens), BF16),
        scratch_shapes=[pltpu.VMEM((tokens + 8, channels), F32)],
        compiler_params=params(),
        cost_estimate=cost(*LONG),
        name="gate_stream",
    )(feat, conv, og, filt, bias, later)


def product_gradients(feat, gp, later, exts):
    tokens, channels = feat.shape[1:]
    fold = channels // LANES
    for j in range(fold):
        lanes = slice(j * LANES, (j + 1) * LANES)
        g = gp[pl.ds(j, tokens, stride=fold), :]
        rim = gp[pl.ds(tokens * fold + j, 2, stride=fold), :]
        for ext, n in zip(exts, (2, 1)):
            ext[0:tokens, lanes] = g * feat[n, :, lanes]
            ext[tokens : tokens + 2, lanes] = rim * rim_rows(later, n, j, fold)


def gradients_kernel(feat, conv, og, filt, bias, later, gp, out, first, second, third, ready, sems):
    tokens, channels = og.shape
    gate_gradient(feat, conv, og, bias, later, first)
    product_gradients(feat, gp, later, (second, third))
    moves = []
    for p, ext in enumerate((first, second, third)):
        taps = [filt[p, j : j + 1, :] for j in range(3)]
        for j in range(channels // LANES):
            lanes = slice(j * LANES, (j + 1) * LANES)
            ready[p, :, lanes] = tapped(ext, taps, lanes, tokens)
        moves.append(pltpu.make_async_copy(ready.at[p], out.at[p], sems.at[p]))
        moves[-1].start()
    for move in moves:
        move.wait()


def gradients(feat, conv, og, filt, bias, later, gp):
    tokens, channels = og.shape
    return pl.pallas_call(
        gradients_kernel,
        in_specs=[whole()] * 7,
        out_specs=in_hbm(),
        out_shape=jax.ShapeDtypeStruct((3, tokens, channels), F32),
        scratch_shapes=[pltpu.VMEM((tokens + 8, channels), F32)] * 3
        + [pltpu.VMEM((3, tokens, channels), F32), pltpu.SemaphoreType.DMA((3,))],
        compiler_params=params(),
        cost_estimate=cost(30 * tokens * channels, 40 * tokens * channels),
        name="gradients",
    )(feat, conv, og, filt, bias, later, gp)


def on_ring(offset, ring):
    own = lax.rem(lax.axis_index("chan"), ring)
    place = jnp.where(lax.rem(own, 2) == 0, own // 2, ring - 1 - own // 2)
    place = lax.rem(place + offset, ring)
    return jnp.where(place < (ring + 1) // 2, 2 * place, 2 * (ring - 1 - place) + 1)


def fetches(plan, ring, w_proj, ready, sems):
    channels = ready.shape[1] // len(plan)
    moves = []
    for k, (stream, height, offset, _) in enumerate(plan):
        begin = pl.multiple_of((height * ring + on_ring(offset, ring)) * channels, LANES)
        columns = w_proj.at[stream, :, pl.ds(begin, channels)]
        moves.append(pltpu.make_async_copy(columns, ready.at[:, pl.ds(k * channels, channels)], sems.at[k]))
    return moves


def state_kernel(spans, plan, ring, feat, og, filt, bias, tables, *refs):
    later = len(spans)
    payloads = refs[:later]
    w_proj, rounded, sums, gp, ready, acc, prod, first_ext, second_ext, sems = refs[later:]
    exts = first_ext, second_ext
    moves = fetches(plan, ring, w_proj, ready, sems)
    for move in moves:
        move.start()
    tokens, channels = og.shape
    fold = channels // LANES
    modes = (tables.shape[0] // fold - tokens) // 3
    dec, res = tokens, tokens + 2 * modes
    briefs = [payloads[0].at[pl.ds(0, (modes + 2) * fold)], *payloads[1:]]
    for j in range(fold):
        lanes = slice(j * LANES, (j + 1) * LANES)
        p = feat[1, :, lanes] * feat[2, :, lanes]
        prod[pl.ds(j, tokens, stride=fold), :] = p
        s = og[:, lanes] * feat[0, :, lanes]
        sums[modes : modes + 1, lanes] = jnp.sum(s * p, axis=0, keepdims=True)

    def rows(ref, at):
        return ref[at * fold : (at + 1) * fold, :]

    direct = bias[...]
    group = 8
    for low in range(0, modes, group):
        chosen = range(low, min(low + group, modes))
        decay, weight = ([rows(tables, at + m) for m in chosen] for at in (dec, res))
        state = [all_carried(briefs, spans, m, tables, tokens, fold) for m in chosen]

        def corr(state, weight=weight):
            terms = [w * s for w, s in zip(weight, state)]
            while len(terms) > 1:
                terms = [a + b for a, b in zip(terms[::2], terms[1::2])] + terms[len(terms) // 2 * 2 :]
            return terms[0]

        def put(at, row, state, low=low, corr=corr):
            here = pl.ds(at * fold, fold)
            if low == 0:
                gp[here, :] = corr(state) + direct * row
            else:
                gp[here, :] = gp[here, :] + corr(state)

        for n in (1, 0):
            row = rows(payloads[0], modes + n)
            state = [row + d * s for d, s in zip(decay, state)]
            put(tokens + n, row, state)

        def step(i, carry, decay=decay, put=put):
            state, total = carry
            at = tokens - 1 - i
            row = tables[pl.ds(at * fold, fold), :]
            other = prod[pl.ds(at * fold, fold), :]
            state = [row + d * s for d, s in zip(decay, state)]
            total = [a + other * s for a, s in zip(total, state)]
            put(at, row, state)
            return state, total

        zero = [jnp.zeros((fold, LANES), F32) for _ in chosen]
        state, total = lax.fori_loop(0, tokens, step, (state, zero), unroll=4)
        for m, a in zip(chosen, total):
            acc[m * fold : (m + 1) * fold, :] = a

    product_gradients(feat, gp, payloads[0], exts)
    for p, ext in enumerate(exts):
        taps = [filt[p + 1, j : j + 1, :] for j in range(3)]
        for j in range(fold):
            lanes = slice(j * LANES, (j + 1) * LANES)
            rounded[p, lanes, :] = tapped(ext, taps, lanes, tokens).astype(BF16).T
    for j in range(fold):
        sums[0:modes, j * LANES : (j + 1) * LANES] = acc[pl.ds(j, modes, stride=fold), :]
    for move in moves:
        move.wait()


def state_streams(feat, og, filt, bias, tables, payloads, spans, plan, ring, w_proj):
    tokens, channels = og.shape
    fold = channels // LANES
    modes = (tables.shape[0] // fold - tokens) // 3
    return pl.pallas_call(
        functools.partial(state_kernel, spans, plan, ring),
        in_specs=[whole()] * (5 + len(payloads)) + [in_hbm()],
        out_specs=[whole()] * 4,
        out_shape=[
            pltpu.VMEM((2, channels, tokens), BF16),
            pltpu.VMEM((modes + 1, channels), F32),
            pltpu.VMEM(((tokens + 2) * fold, LANES), F32),
            pltpu.VMEM((w_proj.shape[1], len(plan) * channels), BF16),
        ],
        scratch_shapes=[pltpu.VMEM((modes * fold, LANES), F32), pltpu.VMEM((tokens * fold, LANES), F32)]
        + [pltpu.VMEM((tokens + 8, channels), F32)] * 2
        + [pltpu.SemaphoreType.DMA((len(plan),))],
        compiler_params=params(),
        cost_estimate=cost(4 << 30, 16 << 20),
        name="state_streams",
    )(feat, og, filt, bias, tables, *payloads, w_proj)


def product_kernel(plan, parts, laters, first, last, ring, w_proj, *refs):
    refs = list(refs)
    moves = []
    if laters:
        sems = refs.pop()
        at = 0
        for later, target in zip(laters, refs[-len(laters) :]):
            moves += fetches(later, ring, w_proj, target, sems.at[pl.ds(at, len(later))])
            at += len(later)
        del refs[-len(laters) :]
    elif last:
        sems = refs.pop()
        turned = refs.pop()
    out = refs.pop()
    before = None if first else refs.pop()
    for move in moves:
        move.start()
    weights, xs = refs[: len(parts)], refs[len(parts) :]
    blocks = [[xs[n][h, p] for n, h, p in pieces] for *_, pieces in plan]
    channels = sum(x.shape[0] for x in blocks[0])
    features = weights[0].shape[0]
    wide = min(512, features)
    for d in range(0, features, wide):
        rows = slice(d, d + wide)
        y = None if first else before[rows]
        done = 0
        for w, (begin, count) in zip(weights, parts):
            x = jnp.concatenate(sum(blocks[done : done + count], []), axis=0)
            done += count
            z = jnp.dot(
                w[rows, begin * channels : (begin + count) * channels], x, preferred_element_type=F32
            )
            y = z if y is None else y + z
        if last:
            turned[:, rows] = y.T
            moves.append(pltpu.make_async_copy(
                turned.at[:, pl.ds(d, wide)], out.at[:, pl.ds(d, wide)], sems.at[d // wide]
            ))
            moves[-1].start()
        else:
            out[rows] = y
    for move in moves:
        move.wait()


def steps_of(pieces):
    arrays, plan = [], []
    for array, places, stream, offset in pieces:
        halves = array if isinstance(array, tuple) else (array,)
        for h in range(halves[0].shape[0]):
            for p in places:
                plan.append((stream + p, h, offset, [(len(arrays) + n, h, p) for n in range(len(halves))]))
        arrays += halves
    return arrays, plan


def add_product(total, weights, pieces, laters, last, ring, w_proj, span):
    features = w_proj.shape[1]
    arrays, plan = steps_of(pieces)
    channels, tokens = w_proj.shape[2] // lax.axis_size("chan"), arrays[0].shape[3]
    first = total is None
    out_specs = [whole()]
    out_shape = [pltpu.VMEM((features, tokens), F32)]
    scratch = []
    if last:
        out_specs = [in_hbm()]
        out_shape = [jax.ShapeDtypeStruct((tokens, features), F32)]
        scratch = [pltpu.VMEM((tokens, features), F32), pltpu.SemaphoreType.DMA((max(1, features // 512),))]
    elif laters:
        out_specs += [whole()] * len(laters)
        out_shape += [pltpu.VMEM((features, len(later) * channels), BF16) for later in laters]
        scratch = [pltpu.SemaphoreType.DMA((sum(map(len, laters)),))]
    parts = [(begin, count) for _, begin, count in weights]
    return pl.pallas_call(
        functools.partial(product_kernel, plan, parts, laters, first, last, ring),
        in_specs=[in_hbm()] + [whole()] * (len(weights) + len(arrays) + (not first)),
        out_specs=out_specs,
        out_shape=out_shape,
        scratch_shapes=scratch,
        compiler_params=params(),
        cost_estimate=cost(*span),
        name="add_product",
    )(w_proj, *(w for w, _, _ in weights), *arrays, *([] if first else [total]))


def ring_order(size):
    return list(range(0, size, 2)) + list(range(size - 1 - size % 2, 0, -2))


def after(array, *others):
    return lax.optimization_barrier((array, *others))[0]


def body(features, saved_conv, out_grad, short_filter, residue, rate, bias, w_proj):
    tokens, channels = out_grad.shape
    modes = rate.shape[1]
    blocks = lax.axis_size("ctx")
    groups = lax.axis_size("chan")
    ring = min(groups, RING)
    heights = groups // ring

    order = ring_order(ring)
    pairs = {
        by: [
            (h * ring + order[i], h * ring + order[(i + by) % ring])
            for h in range(heights)
            for i in range(ring)
        ]
        for by in (1, -1)
    }

    def up(x):
        return lax.ppermute(x, "chan", pairs[1])

    def down(x):
        return lax.ppermute(x, "chan", pairs[-1])

    def stacked(block):
        if heights == 1:
            return block[None]
        groups = [[h * ring + i for h in range(heights)] for i in range(ring)]
        return lax.all_gather(block, "chan", axis_index_groups=groups)

    def from_later(array, by):
        return lax.ppermute(array, "ctx", [(i, i - by) for i in range(by, blocks)])

    def exchanged(sums, by):
        return sums + lax.ppermute(sums, "ctx", [(i, i ^ by) for i in range(blocks)])

    fold = channels // LANES
    feat, conv, og, filt, bias_row, tables, own, brief = front(
        features, saved_conv, out_grad, short_filter, residue.T, rate.T, bias[None]
    )
    payloads, spans = [from_later(own, 1)], [tokens]
    unit, window = 1, brief
    while unit < blocks:
        for by in range(len(payloads) % 3 + 1, 4):
            if by * unit < blocks:
                payloads.append(from_later(window, by * unit))
                spans.append(unit * tokens)
        unit *= 4
        if unit < blocks:
            near = [window, *payloads[-3:]]
            near[1] = near[1][: window.shape[0]]
            window = join(near, unit // 4 * tokens, tables, tokens, fold)
    gate = gate_stream(feat, conv, og, filt, bias_row, payloads[0])
    a0 = stacked(gate)
    a1, z1 = up(a0), down(a0)

    half = channels // 2
    back = ring // 2

    a, b = (0,), (0, 1)
    sets = [
        [("a0", a, 0, 0), ("a1", a, 0, ring - 1), ("z1", a, 0, 1)],
        [("b0", b, 1, 0)],
        [("b1", b, 1, ring - 1), ("y1", b, 1, 1)],
        [("a2", a, 0, ring - 2), ("z2", a, 0, 2)],
        [("b2", b, 1, ring - 2), ("y2", (0,), 1, 2)],
        [("y2", (1,), 1, 2), ("a3", a, 0, ring - 3), ("z3", a, 0, 3)],
        [("b3", a, 1, ring - 3), ("y3", a, 2, 3), ("c3", a, 2, ring - 3), ("x3", a, 1, 3)],
        [("b4", a, 1, back), ("y4", a, 2, back)],
        [("a4", a, 0, back)],
    ]
    costs = [LONG, LONG, SHORT, LONG, SHORT, SHORT, SHORT, SHORT, SHORT]
    hollow = jax.ShapeDtypeStruct((heights, 2, channels, tokens), BF16)

    def plan_of(n):
        return steps_of([(hollow, *piece[1:]) for piece in sets[n]])[1]

    plans = [plan_of(n) for n in range(len(sets))]
    early, late = plans[6][: len(plans[6]) // 2], plans[6][len(plans[6]) // 2 :]
    laters = [[plan] for plan in plans[1:6]] + [[late], [plans[7] + plans[8]], [], []]
    laters[1].append(early)

    def times(n, total, weights, **arrays):
        pieces = [(arrays[name], *rest) for name, *rest in sets[n]]
        return add_product(total, weights, pieces, laters[n], n == len(sets) - 1, ring, w_proj, costs[n])

    def all_of(weights, n):
        return [(weights, 0, len(plans[n]))]

    payloads[0], a0 = lax.optimization_barrier((payloads[0], a0))
    rounds, sums, gp, ready = state_streams(
        feat, og, filt, bias_row.reshape(fold, LANES), tables, payloads, spans, plans[0], ring, w_proj
    )
    b0 = stacked(rounds)

    b1, y1 = up(b0), down(b0)
    a1, z1, b0, sums = lax.optimization_barrier((a1, z1, b0, sums))
    a2, z2 = up(a1), down(z1)
    distances = [1 << n for n in range((blocks - 1).bit_length())]
    for by in distances[:1]:
        sums = exchanged(sums, by)
    total, ready = times(0, None, all_of(ready, 0), a0=a0, a1=a1, z1=z1)
    total, ready, soon = times(1, total, all_of(ready, 1), b0=b0)

    b1, y1, total, sums = lax.optimization_barrier((b1, y1, total, sums))
    b2, y2 = up(b1), down(y1)
    total, ready = times(2, total, all_of(ready, 2), b1=b1, y1=y1)

    a2, z2, total, sums = lax.optimization_barrier((a2, z2, total, sums))
    a3, z3 = up(a2), down(z2)
    for by in distances[1:]:
        sums = exchanged(sums, by)
    total, ready = times(3, total, all_of(ready, 3), a2=a2, z2=z2)
    grads = gradients(features, saved_conv, out_grad, short_filter, bias[None], payloads[0], after(gp, total))

    sums = sums * (tokens * blocks) ** (-0.5)
    outputs = grads, sums[:modes].T, sums[modes]
    b2, y2, total, outputs = lax.optimization_barrier((b2, y2, total, outputs))
    b3, y3 = up(b2[:, :1]), down(y2[:, 1:])
    c3 = up(b2[:, 1:])
    total, ready = times(4, total, all_of(ready, 4), b2=b2, y2=y2)
    x3 = down(after(y2[:, :1], total))
    a3, z3, total = lax.optimization_barrier((a3, z3, total))
    total, ready = times(5, total, all_of(ready, 5), y2=y2, a3=a3, z3=z3)

    b3, y3, total = lax.optimization_barrier((b3, y3, total))
    b4, y4 = up(b3), down(y3)
    a4 = up(a3[:, :, :half]), down(z3[:, :, half:])
    weights = [(soon, 0, len(early)), (ready, 0, len(late))]
    total, ready = times(6, total, weights, b3=b3, y3=y3, c3=c3, x3=x3)

    b4, y4, total = lax.optimization_barrier((b4, y4, total))
    (total,) = times(7, total, [(ready, 0, len(plans[7]))], b4=b4, y4=y4)
    a4, total = lax.optimization_barrier((a4, total))
    (grad_x,) = times(8, total, [(ready, len(plans[7]), len(plans[8]))], a4=a4)
    grads, grad_residue, grad_bias = outputs
    return (grads, grad_x, grad_residue, grad_bias)


def solution(mesh):
    return jax.shard_map(
        body,
        mesh=mesh,
        in_specs=(
            P(None, "ctx", "chan"),
            P("ctx", "chan"),
            P("ctx", "chan"),
            P(None, None, "chan"),
            P("chan", None),
            P("chan", None),
            P("chan"),
            P(None, "chan", None),
        ),
        out_specs=(P(None, "ctx", "chan"), P("ctx", "chan"), P("chan", None), P("chan")),
        check_vma=False,
    )
```

```python
import functools

import jax
import jax.numpy as jnp
from jax import lax
from jax.experimental import pallas as pl
from jax.experimental.pallas import tpu as pltpu
from jax.sharding import PartitionSpec as P

LANES = 128
RING = 8
LONG = 1 << 36, 1 << 28
SHORT = 1 << 16, 1 << 8
VMEM = 8 * 1024 * 1024
F32 = jnp.float32
BF16 = jnp.bfloat16


def whole():
    return pl.BlockSpec(memory_space=pltpu.VMEM)


def in_hbm():
    return pl.BlockSpec(memory_space=pltpu.HBM)


def params():
    return pltpu.CompilerParams(vmem_limit_bytes=VMEM)


def cost(flops, size):
    return pl.CostEstimate(flops=flops, bytes_accessed=size, transcendentals=0)


def by_row(values, out, fold, base=0):
    for j in range(fold):
        out[pl.ds(base * fold + j, values.shape[0], stride=fold), :] = values[:, j * LANES : (j + 1) * LANES]


def front_kernel(features, saved_conv, out_grad, short_filter, residue, rate, bias, *refs):
    feat, conv, og, filt, bias_in, tables, own, brief, res_in, rate_in, sems = refs
    tokens, channels = og.shape
    modes = rate_in.shape[0]
    fold = channels // LANES
    moves = [
        pltpu.make_async_copy(source, target, sems.at[n])
        for n, (source, target) in enumerate((
            (rate, rate_in),
            (out_grad, og),
            (features.at[0], feat.at[0]),
            (features.at[pl.ds(1, 2)], feat.at[pl.ds(1, 2)]),
            (saved_conv, conv),
            (short_filter, filt),
            (residue, res_in),
            (bias, bias_in),
        ))
    ]
    for move in moves:
        move.start()
    moves[0].wait()
    by_row(jnp.exp(-rate_in[...]), tables, fold, tokens)
    by_row(rate_in[...], tables, fold, tokens + modes)
    moves[1].wait()
    moves[2].wait()
    for j in range(fold):
        lanes = slice(j * LANES, (j + 1) * LANES)
        tables[pl.ds(j, tokens, stride=fold), :] = og[:, lanes] * feat[0, :, lanes]
    decay = [tables[(tokens + m) * fold : (tokens + m + 1) * fold, :] for m in range(modes)]

    def step(i, states):
        row = tables[pl.ds((tokens - 1 - i) * fold, fold), :]
        return tuple(row + d * s for d, s in zip(decay, states))

    zero = tuple(jnp.zeros((fold, LANES), F32) for _ in range(modes))
    states = lax.fori_loop(0, tokens - 2, step, zero, unroll=6)
    for target in (own, brief):
        for m in range(modes):
            target[m * fold : (m + 1) * fold, :] = states[m]
        target[modes * fold : (modes + 2) * fold, :] = tables[0 : 2 * fold, :]
    for n in range(3, 8):
        moves[n].wait()
    for n in range(3):
        by_row(feat[n, 0:2, :], own, fold, modes + 2 + 2 * n)
    by_row(conv[0:2, :], own, fold, modes + 8)
    by_row(og[0:2, :], own, fold, modes + 10)
    by_row(res_in[...], tables, fold, tokens + 2 * modes)


def front(features, saved_conv, out_grad, short_filter, residue, rate, bias):
    tokens, channels = out_grad.shape
    modes = rate.shape[0]
    fold = channels // LANES
    inputs = (features, saved_conv, out_grad, short_filter, residue, rate, bias)
    return pl.pallas_call(
        front_kernel,
        in_specs=[in_hbm()] * 7,
        out_specs=[whole()] * 8,
        out_shape=[pltpu.VMEM(a.shape, F32) for a in (*inputs[:4], bias)]
        + [pltpu.VMEM((n * fold, LANES), F32) for n in (tokens + 3 * modes, modes + 12, modes + 2)],
        scratch_shapes=[pltpu.VMEM(rate.shape, F32)] * 2 + [pltpu.SemaphoreType.DMA((8,))],
        compiler_params=params(),
        cost_estimate=cost(4 * tokens * channels * modes, 20 * tokens * channels),
        name="front",
    )(*(pltpu.with_memory_space_constraint(a, pltpu.HBM) for a in inputs))


def tapped(ext, taps, lanes, tokens):
    total = taps[0][:, lanes] * ext[0:tokens, lanes]
    total = total + taps[1][:, lanes] * ext[1 : tokens + 1, lanes]
    return total + taps[2][:, lanes] * ext[2 : tokens + 2, lanes]


def rim_rows(later, which, j, fold):
    modes = later.shape[0] // fold - 12
    return later[pl.ds((modes + 2 + 2 * which) * fold + j, 2, stride=fold), :]


def gate_gradient(feat, conv, og, bias, later, ext):
    tokens, channels = og.shape
    fold = channels // LANES
    for j in range(fold):
        lanes = slice(j * LANES, (j + 1) * LANES)
        product = feat[1, :, lanes] * feat[2, :, lanes]
        ext[0:tokens, lanes] = og[:, lanes] * (conv[:, lanes] + bias[:, lanes] * product)
        key, value, held, cotangent = (rim_rows(later, n, j, fold) for n in (1, 2, 3, 4))
        ext[tokens : tokens + 2, lanes] = cotangent * (held + bias[:, lanes] * (key * value))


def carried(own, m, later, state, decay, rate, span, fold):
    modes = own.shape[0] // fold - 2
    s0, s1 = (later[(modes + n) * fold : (modes + n + 1) * fold, :] for n in (0, 1))
    return own[m * fold : (m + 1) * fold, :] + jnp.exp(-(span - 2) * rate) * (s0 + decay * (s1 + decay * state))


def all_carried(summaries, spans, m, tables, tokens, fold):
    modes = summaries[0].shape[0] // fold - 2
    decay, rate = (tables[(tokens + n * modes + m) * fold : (tokens + n * modes + m + 1) * fold, :] for n in (0, 1))
    state = summaries[-1][m * fold : (m + 1) * fold, :]
    for own, later, span in reversed(list(zip(summaries, summaries[1:], spans))):
        state = carried(own, m, later, state, decay, rate, span, fold)
    return state


def join(summaries, span, tables, tokens, fold):
    def kernel(tables, *refs):
        *refs, out = refs
        modes = out.shape[0] // fold - 2
        for m in range(modes):
            out[m * fold : (m + 1) * fold, :] = all_carried(refs, [span] * (len(refs) - 1), m, tables, tokens, fold)
        out[modes * fold : (modes + 2) * fold, :] = refs[0][modes * fold : (modes + 2) * fold, :]

    return pl.pallas_call(
        kernel,
        in_specs=[whole()] * (1 + len(summaries)),
        out_specs=whole(),
        out_shape=pltpu.VMEM(summaries[0].shape, F32),
        compiler_params=params(),
        name="join",
    )(tables, *summaries)


def gate_kernel(feat, conv, og, filt, bias, later, rounded, ext):
    tokens, channels = og.shape
    taps = [filt[0, j : j + 1, :] for j in range(3)]
    gate_gradient(feat, conv, og, bias, later, ext)
    for j in range(channels // LANES):
        lanes = slice(j * LANES, (j + 1) * LANES)
        rounded[0, lanes, :] = tapped(ext, taps, lanes, tokens).astype(BF16).T


def gate_stream(feat, conv, og, filt, bias, later):
    tokens, channels = og.shape
    return pl.pallas_call(
        gate_kernel,
        in_specs=[whole()] * 6,
        out_specs=whole(),
        out_shape=pltpu.VMEM((1, channels, tokens), BF16),
        scratch_shapes=[pltpu.VMEM((tokens + 8, channels), F32)],
        compiler_params=params(),
        cost_estimate=cost(*LONG),
        name="gate_stream",
    )(feat, conv, og, filt, bias, later)


def product_gradients(feat, gp, later, exts):
    tokens, channels = feat.shape[1:]
    fold = channels // LANES
    for j in range(fold):
        lanes = slice(j * LANES, (j + 1) * LANES)
        g = gp[pl.ds(j, tokens, stride=fold), :]
        rim = gp[pl.ds(tokens * fold + j, 2, stride=fold), :]
        for ext, n in zip(exts, (2, 1)):
            ext[0:tokens, lanes] = g * feat[n, :, lanes]
            ext[tokens : tokens + 2, lanes] = rim * rim_rows(later, n, j, fold)


def gradients_kernel(
    plan, ring, feat, conv, og, filt, bias, later, gp, w_proj, out, columns, first, second, third, ready, sems
):
    tokens, channels = og.shape
    moves = fetches(plan, ring, w_proj, columns, sems.at[pl.ds(3, len(plan))])
    for move in moves:
        move.start()
    gate_gradient(feat, conv, og, bias, later, first)
    product_gradients(feat, gp, later, (second, third))
    for p, ext in enumerate((first, second, third)):
        taps = [filt[p, j : j + 1, :] for j in range(3)]
        for j in range(channels // LANES):
            lanes = slice(j * LANES, (j + 1) * LANES)
            ready[p, :, lanes] = tapped(ext, taps, lanes, tokens)
        moves.append(pltpu.make_async_copy(ready.at[p], out.at[p], sems.at[p]))
        moves[-1].start()
    for move in moves:
        move.wait()


def gradients(feat, conv, og, filt, bias, later, gp, plan, ring, w_proj):
    tokens, channels = og.shape
    return pl.pallas_call(
        functools.partial(gradients_kernel, plan, ring),
        in_specs=[whole()] * 7 + [in_hbm()],
        out_specs=[in_hbm(), whole()],
        out_shape=[
            jax.ShapeDtypeStruct((3, tokens, channels), F32),
            pltpu.VMEM((w_proj.shape[1], len(plan) * channels), BF16),
        ],
        scratch_shapes=[pltpu.VMEM((tokens + 8, channels), F32)] * 3
        + [pltpu.VMEM((3, tokens, channels), F32), pltpu.SemaphoreType.DMA((3 + len(plan),))],
        compiler_params=params(),
        cost_estimate=cost(30 * tokens * channels, 40 * tokens * channels),
        name="gradients",
    )(feat, conv, og, filt, bias, later, gp, w_proj)


def on_ring(offset, ring):
    own = lax.rem(lax.axis_index("chan"), ring)
    place = jnp.where(lax.rem(own, 2) == 0, own // 2, ring - 1 - own // 2)
    place = lax.rem(place + offset, ring)
    return jnp.where(place < (ring + 1) // 2, 2 * place, 2 * (ring - 1 - place) + 1)


def fetches(plan, ring, w_proj, ready, sems):
    channels = ready.shape[1] // len(plan)
    moves = []
    for k, (stream, height, offset, _) in enumerate(plan):
        begin = pl.multiple_of((height * ring + on_ring(offset, ring)) * channels, LANES)
        columns = w_proj.at[stream, :, pl.ds(begin, channels)]
        moves.append(pltpu.make_async_copy(columns, ready.at[:, pl.ds(k * channels, channels)], sems.at[k]))
    return moves


def state_kernel(spans, plan, ring, feat, og, filt, bias, tables, *refs):
    later = len(spans)
    payloads = refs[:later]
    w_proj, rounded, sums, gp, ready, acc, prod, first_ext, second_ext, sems = refs[later:]
    exts = first_ext, second_ext
    moves = fetches(plan, ring, w_proj, ready, sems)
    for move in moves:
        move.start()
    tokens, channels = og.shape
    fold = channels // LANES
    modes = (tables.shape[0] // fold - tokens) // 3
    dec, res = tokens, tokens + 2 * modes
    briefs = [payloads[0].at[pl.ds(0, (modes + 2) * fold)], *payloads[1:]]
    for j in range(fold):
        lanes = slice(j * LANES, (j + 1) * LANES)
        p = feat[1, :, lanes] * feat[2, :, lanes]
        prod[pl.ds(j, tokens, stride=fold), :] = p
        s = og[:, lanes] * feat[0, :, lanes]
        sums[modes : modes + 1, lanes] = jnp.sum(s * p, axis=0, keepdims=True)

    def rows(ref, at):
        return ref[at * fold : (at + 1) * fold, :]

    direct = bias[...]
    group = 8
    for low in range(0, modes, group):
        chosen = range(low, min(low + group, modes))
        decay, weight = ([rows(tables, at + m) for m in chosen] for at in (dec, res))
        state = [all_carried(briefs, spans, m, tables, tokens, fold) for m in chosen]

        def corr(state, weight=weight):
            terms = [w * s for w, s in zip(weight, state)]
            while len(terms) > 1:
                terms = [a + b for a, b in zip(terms[::2], terms[1::2])] + terms[len(terms) // 2 * 2 :]
            return terms[0]

        def put(at, row, state, low=low, corr=corr):
            here = pl.ds(at * fold, fold)
            if low == 0:
                gp[here, :] = corr(state) + direct * row
            else:
                gp[here, :] = gp[here, :] + corr(state)

        for n in (1, 0):
            row = rows(payloads[0], modes + n)
            state = [row + d * s for d, s in zip(decay, state)]
            put(tokens + n, row, state)

        def step(i, carry, decay=decay, put=put):
            state, total = carry
            at = tokens - 1 - i
            row = tables[pl.ds(at * fold, fold), :]
            other = prod[pl.ds(at * fold, fold), :]
            state = [row + d * s for d, s in zip(decay, state)]
            total = [a + other * s for a, s in zip(total, state)]
            put(at, row, state)
            return state, total

        zero = [jnp.zeros((fold, LANES), F32) for _ in chosen]
        state, total = lax.fori_loop(0, tokens, step, (state, zero), unroll=4)
        for m, a in zip(chosen, total):
            acc[m * fold : (m + 1) * fold, :] = a

    product_gradients(feat, gp, payloads[0], exts)
    for p, ext in enumerate(exts):
        taps = [filt[p + 1, j : j + 1, :] for j in range(3)]
        for j in range(fold):
            lanes = slice(j * LANES, (j + 1) * LANES)
            rounded[p, lanes, :] = tapped(ext, taps, lanes, tokens).astype(BF16).T
    for j in range(fold):
        sums[0:modes, j * LANES : (j + 1) * LANES] = acc[pl.ds(j, modes, stride=fold), :]
    for move in moves:
        move.wait()


def state_streams(feat, og, filt, bias, tables, payloads, spans, plan, ring, w_proj):
    tokens, channels = og.shape
    fold = channels // LANES
    modes = (tables.shape[0] // fold - tokens) // 3
    return pl.pallas_call(
        functools.partial(state_kernel, spans, plan, ring),
        in_specs=[whole()] * (5 + len(payloads)) + [in_hbm()],
        out_specs=[whole()] * 4,
        out_shape=[
            pltpu.VMEM((2, channels, tokens), BF16),
            pltpu.VMEM((modes + 1, channels), F32),
            pltpu.VMEM(((tokens + 2) * fold, LANES), F32),
            pltpu.VMEM((w_proj.shape[1], len(plan) * channels), BF16),
        ],
        scratch_shapes=[pltpu.VMEM((modes * fold, LANES), F32), pltpu.VMEM((tokens * fold, LANES), F32)]
        + [pltpu.VMEM((tokens + 8, channels), F32)] * 2
        + [pltpu.SemaphoreType.DMA((len(plan),))],
        compiler_params=params(),
        cost_estimate=cost(4 << 30, 16 << 20),
        name="state_streams",
    )(feat, og, filt, bias, tables, *payloads, w_proj)


def product_kernel(plan, parts, laters, first, last, ring, w_proj, *refs):
    refs = list(refs)
    moves = []
    if laters:
        sems = refs.pop()
        at = 0
        for later, target in zip(laters, refs[-len(laters) :]):
            moves += fetches(later, ring, w_proj, target, sems.at[pl.ds(at, len(later))])
            at += len(later)
        del refs[-len(laters) :]
    elif last:
        sems = refs.pop()
        turned = refs.pop()
    out = refs.pop()
    before = None if first else refs.pop()
    for move in moves:
        move.start()
    weights, xs = refs[: len(parts)], refs[len(parts) :]
    blocks = [[xs[n][h, p] for n, h, p in pieces] for *_, pieces in plan]
    channels = sum(x.shape[0] for x in blocks[0])
    features = weights[0].shape[0]
    wide = min(512, features)
    for d in range(0, features, wide):
        rows = slice(d, d + wide)
        y = None if first else before[rows]
        done = 0
        for w, (begin, count) in zip(weights, parts):
            x = jnp.concatenate(sum(blocks[done : done + count], []), axis=0)
            done += count
            z = jnp.dot(
                w[rows, begin * channels : (begin + count) * channels], x, preferred_element_type=F32
            )
            y = z if y is None else y + z
        if last:
            turned[:, rows] = y.T
            moves.append(pltpu.make_async_copy(
                turned.at[:, pl.ds(d, wide)], out.at[:, pl.ds(d, wide)], sems.at[d // wide]
            ))
            moves[-1].start()
        else:
            out[rows] = y
    for move in moves:
        move.wait()


def steps_of(pieces):
    arrays, plan = [], []
    for array, places, stream, offset in pieces:
        halves = array if isinstance(array, tuple) else (array,)
        for h in range(halves[0].shape[0]):
            for p in places:
                plan.append((stream + p, h, offset, [(len(arrays) + n, h, p) for n in range(len(halves))]))
        arrays += halves
    return arrays, plan


def add_product(total, weights, pieces, laters, last, ring, w_proj, span):
    features = w_proj.shape[1]
    arrays, plan = steps_of(pieces)
    channels, tokens = w_proj.shape[2] // lax.axis_size("chan"), arrays[0].shape[3]
    first = total is None
    out_specs = [whole()]
    out_shape = [pltpu.VMEM((features, tokens), F32)]
    scratch = []
    if last:
        out_specs = [in_hbm()]
        out_shape = [jax.ShapeDtypeStruct((tokens, features), F32)]
        scratch = [pltpu.VMEM((tokens, features), F32), pltpu.SemaphoreType.DMA((max(1, features // 512),))]
    elif laters:
        out_specs += [whole()] * len(laters)
        out_shape += [pltpu.VMEM((features, len(later) * channels), BF16) for later in laters]
        scratch = [pltpu.SemaphoreType.DMA((sum(map(len, laters)),))]
    parts = [(begin, count) for _, begin, count in weights]
    return pl.pallas_call(
        functools.partial(product_kernel, plan, parts, laters, first, last, ring),
        in_specs=[in_hbm()] + [whole()] * (len(weights) + len(arrays) + (not first)),
        out_specs=out_specs,
        out_shape=out_shape,
        scratch_shapes=scratch,
        compiler_params=params(),
        cost_estimate=cost(*span),
        name="add_product",
    )(w_proj, *(w for w, _, _ in weights), *arrays, *([] if first else [total]))


def ring_order(size):
    return list(range(0, size, 2)) + list(range(size - 1 - size % 2, 0, -2))


def after(array, *others):
    return lax.optimization_barrier((array, *others))[0]


def body(features, saved_conv, out_grad, short_filter, residue, rate, bias, w_proj):
    tokens, channels = out_grad.shape
    modes = rate.shape[1]
    blocks = lax.axis_size("ctx")
    groups = lax.axis_size("chan")
    ring = min(groups, RING)
    heights = groups // ring

    order = ring_order(ring)
    pairs = {
        by: [
            (h * ring + order[i], h * ring + order[(i + by) % ring])
            for h in range(heights)
            for i in range(ring)
        ]
        for by in (1, -1)
    }

    def up(x):
        return lax.ppermute(x, "chan", pairs[1])

    def down(x):
        return lax.ppermute(x, "chan", pairs[-1])

    def stacked(block):
        if heights == 1:
            return block[None]
        groups = [[h * ring + i for h in range(heights)] for i in range(ring)]
        return lax.all_gather(block, "chan", axis_index_groups=groups)

    def from_later(array, by):
        return lax.ppermute(array, "ctx", [(i, i - by) for i in range(by, blocks)])

    def exchanged(sums, by):
        return sums + lax.ppermute(sums, "ctx", [(i, i ^ by) for i in range(blocks)])

    fold = channels // LANES
    feat, conv, og, filt, bias_row, tables, own, brief = front(
        features, saved_conv, out_grad, short_filter, residue.T, rate.T, bias[None]
    )
    payloads, spans = [from_later(own, 1)], [tokens]
    unit, window = 1, brief
    while unit < blocks:
        for by in range(len(payloads) % 3 + 1, 4):
            if by * unit < blocks:
                payloads.append(from_later(window, by * unit))
                spans.append(unit * tokens)
        unit *= 4
        if unit < blocks:
            near = [window, *payloads[-3:]]
            near[1] = near[1][: window.shape[0]]
            window = join(near, unit // 4 * tokens, tables, tokens, fold)
    gate = gate_stream(feat, conv, og, filt, bias_row, payloads[0])
    a0 = stacked(gate)
    a1, z1 = up(a0), down(a0)

    half = channels // 2
    back = ring // 2

    a, b = (0,), (0, 1)
    sets = [
        [("a0", a, 0, 0), ("a1", a, 0, ring - 1), ("z1", a, 0, 1)],
        [("b0", b, 1, 0)],
        [("b1", b, 1, ring - 1), ("y1", b, 1, 1)],
        [("a2", a, 0, ring - 2), ("z2", a, 0, 2)],
        [("b2", b, 1, ring - 2), ("y2", (0,), 1, 2)],
        [("y2", (1,), 1, 2), ("a3", a, 0, ring - 3), ("z3", a, 0, 3)],
        [("b3", a, 1, ring - 3), ("y3", a, 2, 3), ("c3", a, 2, ring - 3), ("x3", a, 1, 3)],
        [("b4", a, 1, back), ("y4", a, 2, back)],
        [("a4", a, 0, back)],
    ]
    costs = [LONG, LONG, SHORT, LONG, SHORT, SHORT, SHORT, SHORT, SHORT]
    hollow = jax.ShapeDtypeStruct((heights, 2, channels, tokens), BF16)

    def plan_of(n):
        return steps_of([(hollow, *piece[1:]) for piece in sets[n]])[1]

    plans = [plan_of(n) for n in range(len(sets))]
    early, late = plans[6][: len(plans[6]) // 2], plans[6][len(plans[6]) // 2 :]
    laters = [[plan] for plan in plans[1:6]] + [[late], [], [], []]
    laters[1].append(early)

    def times(n, total, weights, **arrays):
        pieces = [(arrays[name], *rest) for name, *rest in sets[n]]
        return add_product(total, weights, pieces, laters[n], n == len(sets) - 1, ring, w_proj, costs[n])

    def all_of(weights, n):
        return [(weights, 0, len(plans[n]))]

    payloads[0], a0 = lax.optimization_barrier((payloads[0], a0))
    rounds, sums, gp, ready = state_streams(
        feat, og, filt, bias_row.reshape(fold, LANES), tables, payloads, spans, plans[0], ring, w_proj
    )
    b0 = stacked(rounds)

    b1, y1 = up(b0), down(b0)
    a1, z1, b0, sums = lax.optimization_barrier((a1, z1, b0, sums))
    a2, z2 = up(a1), down(z1)
    distances = [1 << n for n in range((blocks - 1).bit_length())]
    for by in distances[:1]:
        sums = exchanged(sums, by)
    total, ready = times(0, None, all_of(ready, 0), a0=a0, a1=a1, z1=z1)
    total, ready, soon = times(1, total, all_of(ready, 1), b0=b0)

    b1, y1, total, sums = lax.optimization_barrier((b1, y1, total, sums))
    b2, y2 = up(b1), down(y1)
    total, ready = times(2, total, all_of(ready, 2), b1=b1, y1=y1)

    a2, z2, total, sums = lax.optimization_barrier((a2, z2, total, sums))
    a3, z3 = up(a2), down(z2)
    for by in distances[1:]:
        sums = exchanged(sums, by)
    total, ready = times(3, total, all_of(ready, 3), a2=a2, z2=z2)
    final_plan = plans[7] + plans[8]
    grads, final = gradients(
        features, saved_conv, out_grad, short_filter, bias[None], payloads[0], after(gp, total), final_plan, ring, w_proj
    )

    sums = sums * (tokens * blocks) ** (-0.5)
    outputs = grads, sums[:modes].T, sums[modes]
    b2, y2, total, outputs = lax.optimization_barrier((b2, y2, total, outputs))
    b3, y3 = up(b2[:, :1]), down(y2[:, 1:])
    c3 = up(b2[:, 1:])
    total, ready = times(4, total, all_of(ready, 4), b2=b2, y2=y2)
    x3 = down(after(y2[:, :1], total))
    a3, z3, total = lax.optimization_barrier((a3, z3, total))
    total, ready = times(5, total, all_of(ready, 5), y2=y2, a3=a3, z3=z3)

    b3, y3, total = lax.optimization_barrier((b3, y3, total))
    b4, y4 = up(b3), down(y3)
    a4 = up(a3[:, :, :half]), down(z3[:, :, half:])
    weights = [(soon, 0, len(early)), (ready, 0, len(late))]
    (total,) = times(6, total, weights, b3=b3, y3=y3, c3=c3, x3=x3)

    b4, y4, total = lax.optimization_barrier((b4, y4, total))
    (total,) = times(7, total, [(final, 0, len(plans[7]))], b4=b4, y4=y4)
    a4, total = lax.optimization_barrier((a4, total))
    (grad_x,) = times(8, total, [(final, len(plans[7]), len(plans[8]))], a4=a4)
    grads, grad_residue, grad_bias = outputs
    return (grads, grad_x, grad_residue, grad_bias)


def solution(mesh):
    return jax.shard_map(
        body,
        mesh=mesh,
        in_specs=(
            P(None, "ctx", "chan"),
            P("ctx", "chan"),
            P("ctx", "chan"),
            P(None, None, "chan"),
            P("chan", None),
            P("chan", None),
            P("chan"),
            P(None, "chan", None),
        ),
        out_specs=(P(None, "ctx", "chan"), P("ctx", "chan"), P("chan", None), P("chan")),
        check_vma=False,
    )
```
